32 devices in a mesh: grid: 4 (over z), gx: 4 (over y, x), gy: 2 (over core).
Axes of the slice: x: 2, y: 2, z: 4, core: 2. Of those that a mesh axis runs over, the one named last changes fastest.
Arguments:
- adjoint: float32 [4, 24, 128, 512], P('grid', None, 'gx', 'gy'), may hold values from -6 to 6
- sea_mask: int32 [4, 128, 512], P('grid', 'gx', 'gy'), may hold values 0 or 1
- diffusivity: float32 [4, 128, 512], P('grid', 'gx', 'gy'), may hold values from 0.03 to 0.24
- aggregation: float32 [4, 128, 512], P('grid', 'gx', 'gy'), may hold values from 0.02 to 0.3
- breakup: float32 [4, 128, 512], P('grid', 'gx', 'gy'), may hold values from 0.02 to 0.3
- sponge: float32 [4, 128, 512], P('grid', 'gx', 'gy'), may hold values from 0.05 to 0.6
- settling: float32 [4, 3], replicated, may hold values from 0.05 to 0.5
- partner_flip: int32 [3, 4, 2], replicated, may hold values from 0 to 1
- row_offset: int32 [3, 4, 2], replicated, may hold values from 0 to 16
- col_offset: int32 [3, 4, 2], replicated, may hold values from 0 to 128
Outputs:
- adjoint_out: float32 [4, 24, 128, 512], P('grid', None, 'gx', 'gy')
The draws below stay inside these ranges and needn't reach their ends.
Inputs may be any that keep to these rules, and one draw needn't show every extreme that they name: `partner_flip`: every child tile is paired with exactly one parent tile in its own tile column, in its own tile row or the row whose index differs in the lowest bit; a parent tile serves 0 to 6 child tiles. `row_offset`: the footprint lies inside the paired parent tile. `col_offset`: the footprint lies inside the paired parent tile.
All inputs are finite; a program needn't handle non-finite values. No bound on the sum of `sea_mask` on one device may be relied on, other than what follows from the above.
Results may differ from the reference program's by a relative error of at most 0.0001.
Values sent between devices are 32-bit elements; how exact they have to be, the bound alone decides.
No kernel may reach another device: no remote copies, remote signals or barrier semaphores. Data moves between devices by JAX's collectives and lax.ppermute only.
A program may use at most 64 MiB of HBM per device.

```python
import math
import jax
import jax.numpy as jnp
from jax import lax

NCLS = 3
LEV = 8
STEPS = 2
CR = 32
CC = 256
K = 24
NR = 128
NC = 512
N_GRID = 4
N_GX = 4
N_GY = 2


def place_ends(drawn, rng, least, largest):
    shape = drawn.shape
    index_at = [jax.random.randint(jax.random.fold_in(rng, axis), (), 0, shape[axis]) for axis in range(len(shape))]
    drawn = drawn.at[tuple(index_at)].set(least)
    longest = shape.index(max(shape))
    index_at[longest] = (index_at[longest] + 1) % shape[longest]
    return drawn.at[tuple(index_at)].set(largest)


def shard_levels(rng, shape, cuts, least, largest):
    def one(dim, blocks):
        heights = jax.random.uniform(jax.random.fold_in(jax.random.fold_in(rng, 6), dim), (blocks,), jnp.float32, least / len(cuts), largest / len(cuts))
        return jnp.repeat(jnp.exp(heights), shape[dim] // blocks).reshape((-1,) + (1,) * (len(shape) - dim - 1))

    loudness = one(*cuts[0])
    for cut in cuts[1:]:
        loudness = loudness * one(*cut)
    return loudness


def centred(own_key, shape, deviation, bound, shards=(), kind=jnp.bfloat16):
    entries = deviation * jax.random.normal(own_key, shape, jnp.float32)
    if shards:
        entries = entries * shard_levels(own_key, shape, shards, -0.22, 0.18)
    return jnp.clip(entries, -bound, bound).astype(kind)


def setup_inputs(seed: int = 0) -> dict:
    key_list = jax.random.split(jax.random.key(seed), 11)
    return {
        "adjoint": centred(key_list[0], (N_GRID, K, NR, NC), 1.0, 6.0, ((0, 4), (2, 4), (3, 2)), jnp.float32),
        "sea_mask": place_ends((jax.random.randint(key_list[1], (N_GRID, NR, NC), 0, 5) < 4).astype(jnp.int32), jax.random.fold_in(key_list[1], 1), 0, 1),
        "diffusivity": jnp.clip(0.03 + 0.21 * jax.random.uniform(key_list[2], (N_GRID, NR, NC), jnp.float32) ** shard_levels(key_list[2], (N_GRID, NR, NC), ((0, 4), (1, 4), (2, 2)), -0.2, 0.2), 0.03, 0.24),
        "aggregation": jnp.clip(jnp.exp(math.log(0.3) - 2.7080503 * jax.random.uniform(key_list[3], (N_GRID, NR, NC), jnp.float32) ** shard_levels(key_list[3], (N_GRID, NR, NC), ((0, 4), (1, 4), (2, 2)), -0.2, 0.2)), 0.02, 0.3),
        "breakup": jnp.clip(jnp.exp(math.log(0.3) - 2.7080503 * jax.random.uniform(key_list[4], (N_GRID, NR, NC), jnp.float32) ** shard_levels(key_list[4], (N_GRID, NR, NC), ((0, 4), (1, 4), (2, 2)), -0.2, 0.2)), 0.02, 0.3),
        "sponge": jnp.clip(0.05 + 0.55 * jax.random.uniform(key_list[5], (N_GRID, NR, NC), jnp.float32) ** shard_levels(key_list[5], (N_GRID, NR, NC), ((0, 4), (1, 4), (2, 2)), -0.2, 0.2), 0.05, 0.6),
        "settling": jnp.clip(jnp.exp(jax.random.uniform(key_list[6], (N_GRID, NCLS), jnp.float32, math.log(0.05), math.log(0.5))), 0.05, 0.5),
        "partner_flip": place_ends(jax.random.randint(key_list[7], (N_GRID - 1, N_GX, N_GY), 0, 2), jax.random.fold_in(key_list[7], 1), 0, 1).astype(jnp.int32),
        "row_offset": place_ends(jax.random.randint(key_list[8], (N_GRID - 1, N_GX, N_GY), 0, CR // 2 + 1), jax.random.fold_in(key_list[8], 1), 0, (CR // 2 + 1) - 1).astype(jnp.int32),
        "col_offset": place_ends(jax.random.randint(key_list[9], (N_GRID - 1, N_GX, N_GY), 0, CC // 2 + 1), jax.random.fold_in(key_list[9], 1), 0, (CC // 2 + 1) - 1).astype(jnp.int32),
    }


relaxation = 0.125


def block_sums(values):
    shape = values.shape
    return values.reshape(shape[:-2] + (shape[-2] // 2, 2, shape[-1] // 2, 2)).sum(axis=(-3, -1))


def expand_cells(values):
    return jnp.repeat(jnp.repeat(values, 2, axis=-2), 2, axis=-1)


def swap_pairs(values, axis):
    shape = values.shape
    split = values.reshape(shape[:axis] + (shape[axis] // 2, 2) + shape[axis + 1:])
    return jnp.flip(split, axis + 1).reshape(shape)


def nest_adjoint(state, sponge, partner_flip, row_offset, col_offset):
    half_r = CR // 2
    half_c = CC // 2
    parent = state[0].reshape(K, N_GX, CR, N_GY, CC).transpose(1, 3, 0, 2, 4)
    children = state[1:].reshape(N_GRID - 1, K, N_GX, CR, N_GY, CC).transpose(0, 2, 4, 1, 3, 5)
    weights = sponge[1:].reshape(N_GRID - 1, N_GX, CR, N_GY, CC).transpose(0, 1, 3, 2, 4)
    flips = partner_flip[..., None, None, None]
    source = jnp.where(flips == 0, parent[None], swap_pairs(parent, 0)[None])
    number = (N_GRID - 1) * N_GX * N_GY
    tops = row_offset.reshape(number).astype(jnp.int32)
    lefts = col_offset.reshape(number).astype(jnp.int32)
    anchor = jnp.zeros((), jnp.int32)

    def cut_block(block, top_row, left_col):
        return lax.dynamic_slice(block, (anchor, top_row, left_col), (K, half_r, half_c))

    prints = jax.vmap(cut_block)(source.reshape(number, K, CR, CC), tops, lefts)
    prints = prints.reshape(N_GRID - 1, N_GX, N_GY, K, half_r, half_c)
    new_children = (1.0 - weights[:, :, :, None]) * children + (relaxation / 4.0) * expand_cells(prints)
    sent = block_sums(weights[:, :, :, None] * children).reshape(number, K, half_r, half_c)

    def place_block(piece, top_row, left_col):
        return lax.dynamic_update_slice(jnp.zeros((K, CR, CC), jnp.float32), piece, (anchor, top_row, left_col))

    def cover_block(top_row, left_col):
        return lax.dynamic_update_slice(jnp.zeros((CR, CC), jnp.float32), jnp.ones((half_r, half_c), jnp.float32), (top_row, left_col))

    placed = jax.vmap(place_block)(sent, tops, lefts).reshape(N_GRID - 1, N_GX, N_GY, K, CR, CC)
    boxes = jax.vmap(cover_block)(tops, lefts).reshape(N_GRID - 1, N_GX, N_GY, CR, CC)
    same = (partner_flip == 0).astype(jnp.float32)
    cross = (partner_flip == 1).astype(jnp.float32)
    gathered = jnp.sum(placed * same[..., None, None, None] + swap_pairs(placed * cross[..., None, None, None], 1), axis=0)
    covered = jnp.sum(boxes * same[..., None, None] + swap_pairs(boxes * cross[..., None, None], 1), axis=0)
    new_parent = (1.0 - relaxation * covered[:, :, None]) * parent + gathered
    parent_back = new_parent.transpose(2, 0, 3, 1, 4).reshape(K, N_GX * CR, N_GY * CC)
    children_back = new_children.transpose(0, 3, 1, 4, 2, 5).reshape(N_GRID - 1, K, N_GX * CR, N_GY * CC)
    return jnp.concatenate([parent_back[None], children_back], axis=0)


def floc_adjoint(values, aggregation, breakup):
    shape = values.shape
    split = values.reshape((shape[0], NCLS, LEV) + shape[2:])
    agg = aggregation[:, None]
    brk = breakup[:, None]
    first = split[:, 0]
    second = split[:, 1]
    third = split[:, 2]
    new_first = (1.0 - agg) * first + agg * second
    new_second = brk * first + (1.0 - agg - brk) * second + agg * third
    new_third = brk * second + (1.0 - brk) * third
    return jnp.stack([new_first, new_second, new_third], axis=1).reshape(shape)


def settle_adjoint(values, rates):
    shape = values.shape
    split = values.reshape((shape[0], NCLS, LEV) + shape[2:])
    below = jnp.concatenate([split[:, :, 1:], jnp.zeros_like(split[:, :, :1])], axis=2)
    speed = rates[:, :, None, None, None]
    return ((1.0 - speed) * split + speed * below).reshape(shape)


def reference(adjoint, sea_mask, diffusivity, aggregation, breakup, sponge, settling, partner_flip, row_offset, col_offset):
    state = adjoint
    for step_number in range(STEPS):
        state = nest_adjoint(state, sponge, partner_flip, row_offset, col_offset)
        state = floc_adjoint(state, aggregation, breakup)
        state = settle_adjoint(state, settling)
        wet = sea_mask.astype(jnp.float32)[:, None] * state
        flux = diffusivity[:, None] * wet
        padded = jnp.pad(flux, ((0, 0), (0, 0), (1, 1), (1, 1)))
        state = wet + padded[:, :, :-2, 1:-1] + padded[:, :, 2:, 1:-1] + padded[:, :, 1:-1, :-2] + padded[:, :, 1:-1, 2:] - 4.0 * flux
    return state
```

```python
import functools

import jax
import jax.numpy as jnp
from jax import lax
from jax.experimental import pallas as pl
from jax.experimental.pallas import tpu as pltpu
from jax.sharding import PartitionSpec as P

NCLS = 3
LEV = 8
STEPS = 2
SLOTS = 3
LANES = 128

relaxation = 0.125

VM = pl.BlockSpec(memory_space=pltpu.VMEM)
SM = pl.BlockSpec(memory_space=pltpu.SMEM)
PARAMS = pltpu.CompilerParams(vmem_limit_bytes=16 * 2**20)


def place():
    return lax.axis_index("grid"), lax.axis_index("gx"), lax.axis_index("gy")


def pieces(flip, top, left):
    _, i, j = place()
    for slot in range(SLOTS):
        for kind, row in ((0, i), (1, jnp.bitwise_xor(i, 1))):
            yield slot, kind, flip[slot, row, j] == kind, top[slot, row, j], left[slot, row, j]


def widen(half, cells):
    row = lax.broadcasted_iota(jnp.int32, (half, cells), 0)
    col = lax.broadcasted_iota(jnp.int32, (half, cells), 1)
    return (lax.shift_right_logical(col, 1) == row).astype(jnp.float32)


def narrow(cells, half):
    row = lax.broadcasted_iota(jnp.int32, (cells, half), 0)
    col = lax.broadcasted_iota(jnp.int32, (cells, half), 1)
    return (lax.shift_right_logical(row, 1) == col).astype(jnp.float32)


def payload(flip, top, left, state, sponge, straight, crossed, rows, fine):
    comps, cells_r, cells_c = state.shape
    half_r, half_c = cells_r // 2, cells_c // 2
    grid, _, _ = place()

    @pl.when(grid == 0)
    def _():
        for slot, kind, serves, first, begin in pieces(flip, top, left):
            out = (straight, crossed)[kind][slot]

            @pl.when(serves)
            def _():
                def cut(c, carry):
                    block = pltpu.roll(state[c], lax.rem(cells_r - first, cells_r), 0)[:half_r]
                    out[c] = pltpu.roll(block, lax.rem(cells_c - begin, cells_c), 1)[:, :half_c]
                    return carry

                lax.fori_loop(0, comps, cut, 0)

    @pl.when(grid > 0)
    def _():
        weight = sponge[0]

        def fold(c, carry):
            block = weight * state[c]
            for k in range(cells_c // LANES):
                part = slice(k * LANES, (k + 1) * LANES)
                fine[k] = block[:, part]
                rows[c, :, part] = fine[k, pl.ds(0, half_r, 2), :] + fine[k, pl.ds(1, half_r, 2), :]
            return carry

        lax.fori_loop(0, comps, fold, 0)
        block = jnp.dot(
            rows[...].reshape(comps * half_r, cells_c),
            narrow(cells_c, half_c),
            precision=lax.Precision.HIGHEST,
            preferred_element_type=jnp.float32,
        ).reshape(comps, half_r, half_c)
        for slot in range(SLOTS):

            @pl.when(grid == slot + 1)
            def _():
                straight[slot][...] = block
                crossed[slot][...] = block


def first_kernel(flip, top, left, state, sponge, *rest):
    outs, (rows, fine) = rest[:-2], rest[-2:]
    payload(flip, top, left, state.at[0], sponge, outs[:SLOTS], outs[SLOTS:], rows, fine)


def edge_sides(index):
    even = lax.rem(index, 2) == 0
    return even, jnp.logical_not(even)


def update_kernel(n_cols, flip, top, left, rates, state, sponge, agg, brk, mask, diff, *rest):
    got = rest[: 2 * SLOTS]
    n_side = 2 + n_cols
    bulk, sides = rest[2 * SLOTS], rest[2 * SLOTS + 1 : 2 * SLOTS + 1 + n_side]
    nested, wide, coarse, fine = rest[2 * SLOTS + 1 + n_side :]
    comps, cells_r, cells_c = bulk.shape
    half_r, half_c = cells_r // 2, cells_c // 2
    grid, i, j = place()
    row_id = lax.broadcasted_iota(jnp.int32, (cells_r, cells_c), 0)
    col_id = lax.broadcasted_iota(jnp.int32, (cells_r, cells_c), 1)

    @pl.when(grid == 0)
    def _():
        covered = jnp.zeros((cells_r, cells_c), jnp.float32)
        for _, _, serves, first, begin in pieces(flip, top, left):
            inside = (row_id >= first) & (row_id < first + half_r) & (col_id >= begin) & (col_id < begin + half_c)
            covered = covered + jnp.where(inside & serves, 1.0, 0.0)
        keep = 1.0 - relaxation * covered

        def own(c, carry):
            nested[c] = keep * state[c]
            return carry

        lax.fori_loop(0, comps, own, 0)
        for slot, kind, serves, first, begin in pieces(flip, top, left):
            piece = got[kind * SLOTS + slot]

            @pl.when(serves)
            def _():
                def put(c, carry):
                    block = piece[c]
                    block = jnp.concatenate([block, jnp.zeros_like(block)], axis=1)
                    block = pltpu.roll(block, begin, 1)
                    block = jnp.concatenate([block, jnp.zeros_like(block)], axis=0)
                    nested[c] += pltpu.roll(block, first, 0)
                    return carry

                lax.fori_loop(0, comps, put, 0)

    @pl.when(grid > 0)
    def _():
        for slot in range(SLOTS):
            for kind in range(2):

                @pl.when((grid == slot + 1) & (flip[slot, i, j] == kind))
                def _():
                    coarse[...] = got[kind * SLOTS + slot][...]

        wide[...] = jnp.dot(
            coarse[...].reshape(comps * half_r, half_c),
            widen(half_c, cells_c) * (relaxation / 4.0),
            precision=lax.Precision.HIGHEST,
            preferred_element_type=jnp.float32,
        ).reshape(comps, half_r, cells_c)
        keep = 1.0 - sponge[0]

        def own(c, carry):
            for k in range(cells_c // LANES):
                part = slice(k * LANES, (k + 1) * LANES)
                block = wide[c, :, part]
                fine[k, pl.ds(0, half_r, 2), :] = block
                fine[k, pl.ds(1, half_r, 2), :] = block
                nested[c, :, part] = keep[:, part] * state[c, :, part] + fine[k]
            return carry

        lax.fori_loop(0, comps, own, 0)

    a, b = agg[0], brk[0]
    wet = mask[0].astype(jnp.float32)
    spread = diff[0]
    row_far = edge_sides(i)
    col_far = edge_sides(j)
    lane = lax.broadcasted_iota(jnp.int32, (cells_r, LANES), 1)

    def level(step, carry):
        below, columns = carry
        l = LEV - 1 - step
        u0, u1, u2 = nested[l], nested[LEV + l], nested[2 * LEV + l]
        flocced = ((1.0 - a) * u0 + a * u1, b * u0 + (1.0 - a - b) * u1 + a * u2, b * u1 + (1.0 - b) * u2)
        columns = list(columns)
        for cls in range(NCLS):
            c = cls * LEV + l
            rate = rates[grid, cls]
            w = wet * ((1.0 - rate) * flocced[cls] + rate * below[cls])
            f = spread * w
            total = w - 4.0 * f
            total = total + jnp.where(row_id == 0, 0.0, pltpu.roll(f, 1, 0))
            total = total + jnp.where(row_id == cells_r - 1, 0.0, pltpu.roll(f, cells_r - 1, 0))
            total = total + jnp.where(col_id == 0, 0.0, pltpu.roll(f, 1, 1))
            total = total + jnp.where(col_id == cells_c - 1, 0.0, pltpu.roll(f, cells_c - 1, 1))
            bulk[c] = total
            for phase in range(2):
                sides[phase][pl.ds(c, 1), :] = jnp.where(row_far[phase], f[cells_r - 1 :], f[:1])
            for phase in range(n_cols):
                far = col_far[phase]
                slab = jnp.where(far, f[:, cells_c - LANES :], f[:, :LANES])
                turn = lax.rem(c - jnp.where(far, LANES - 1, 0) + LANES, LANES)
                columns[phase] = jnp.where(lane == c, pltpu.roll(slab, turn, 1), columns[phase])
        return flocced, tuple(columns)

    nothing = jnp.zeros((cells_r, cells_c), jnp.float32)
    empty = jnp.zeros((cells_r, LANES), jnp.float32)
    _, columns = lax.fori_loop(0, LEV, level, ((nothing,) * NCLS, (empty,) * n_cols))
    for phase in range(n_cols):
        sides[2 + phase][...] = columns[phase]


def halo_kernel(n_cols, sizes, last, flip, top, left, bulk, sponge, *rest):
    sides = rest[: 2 + n_cols]
    state = rest[2 + n_cols]
    new = state.at[0] if last else state
    comps, cells_r, cells_c = bulk.shape
    _, i, j = place()
    row_id = lax.broadcasted_iota(jnp.int32, (cells_r, cells_c), 0)
    lane = lax.broadcasted_iota(jnp.int32, (cells_r, LANES), 1)
    row_far = edge_sides(i)
    col_far = edge_sides(j)
    row_at = [jnp.where(far, cells_r - 1, 0) for far in row_far]
    row_at[1] = jnp.where((row_far[1] & (i == sizes[0] - 1)) | (row_far[0] & (i == 0)), -1, row_at[1])
    col_at = [jnp.where(far, LANES - 1, 0) for far in col_far]
    col_on = [jnp.bool_(True), jnp.logical_not((col_far[1] & (j == sizes[1] - 1)) | (col_far[0] & (j == 0)))]

    def add(c, carry):
        total = bulk[c]
        for phase in range(2):
            total = total + jnp.where(row_id == row_at[phase], sides[phase][pl.ds(c, 1), :], 0.0)
        first, final = total[:, :LANES], total[:, cells_c - LANES :]
        for phase in range(n_cols):
            far, at = col_far[phase], col_at[phase]
            slab = pltpu.roll(sides[2 + phase][...], lax.rem(at - c + LANES, LANES), 1)
            slab = jnp.where((lane == at) & col_on[phase], slab, 0.0)
            first = first + jnp.where(far, 0.0, slab)
            final = final + jnp.where(far, slab, 0.0)
        new[c] = jnp.concatenate([first, total[:, LANES : cells_c - LANES], final], axis=1) if cells_c > 2 * LANES else jnp.concatenate([first, final], axis=1)
        return carry

    lax.fori_loop(0, comps, add, 0)
    if not last:
        outs, (rows, fine) = rest[3 + n_cols : -2], rest[-2:]
        payload(flip, top, left, new, sponge, outs[:SLOTS], outs[SLOTS:], rows, fine)


def exchange(blocks):
    n_x = lax.axis_size("gx")
    got = [None] * (2 * SLOTS)
    for slot in reversed(range(SLOTS)):
        for kind in range(2):
            pairs = []
            for i in range(n_x):
                parent, child = i, (slot + 1) * n_x + (i ^ kind)
                pairs += [(parent, child), (child, parent)]
            got[kind * SLOTS + slot] = lax.ppermute(blocks[kind * SLOTS + slot], ("grid", "gx"), pairs)
    return got


def swap_pairs(size, phase):
    pairs = []
    for k in range(phase, size + phase, 2):
        first, second = k % size, (k + 1) % size
        pairs += [(first, second), (second, first)]
    return pairs


def local(adjoint, sea_mask, diffusivity, aggregation, breakup, sponge, settling, partner_flip, row_offset, col_offset):
    comps, cells_r, cells_c = adjoint.shape[1:]
    half_r, half_c = cells_r // 2, cells_c // 2
    n_x, n_y = lax.axis_size("gx"), lax.axis_size("gy")
    n_cols = 1 if n_y == 2 else 2
    f32 = jnp.float32
    tile = jax.ShapeDtypeStruct((comps, cells_r, cells_c), f32)
    block = jax.ShapeDtypeStruct((comps, half_r, half_c), f32)
    side = [jax.ShapeDtypeStruct((comps, cells_c), f32)] * 2 + [jax.ShapeDtypeStruct((cells_r, LANES), f32)] * n_cols
    fold_scratch = [pltpu.VMEM((comps, half_r, cells_c), f32), pltpu.VMEM((cells_c // LANES, cells_r, LANES), f32)]
    tables = (partner_flip, row_offset, col_offset)

    blocks = pl.pallas_call(
        first_kernel,
        out_shape=[block] * (2 * SLOTS),
        in_specs=[SM] * 3 + [VM] * 2,
        out_specs=[VM] * (2 * SLOTS),
        scratch_shapes=fold_scratch,
        compiler_params=PARAMS,
        name="first_payload",
    )(*tables, adjoint, sponge)
    state = adjoint.reshape(tile.shape)
    for step in range(STEPS):
        last = step == STEPS - 1
        got = exchange(blocks)
        bulk, *sides = pl.pallas_call(
            functools.partial(update_kernel, n_cols),
            out_shape=[tile] + side,
            in_specs=[SM] * 4 + [VM] * (6 + 2 * SLOTS),
            out_specs=[VM] * (1 + len(side)),
            scratch_shapes=[
                pltpu.VMEM(tile.shape, f32),
                pltpu.VMEM((comps, half_r, cells_c), f32),
                pltpu.VMEM(block.shape, f32),
                pltpu.VMEM((cells_c // LANES, cells_r, LANES), f32),
            ],
            compiler_params=PARAMS,
            name="update",
        )(*tables, settling, state, sponge, aggregation, breakup, sea_mask, diffusivity, *got)
        sides = [lax.ppermute(sides[k], "gx", swap_pairs(n_x, k)) for k in range(2)] + [
            lax.ppermute(sides[2 + k], "gy", swap_pairs(n_y, k)) for k in range(n_cols)
        ]
        new = jax.ShapeDtypeStruct(adjoint.shape, f32) if last else tile
        out = pl.pallas_call(
            functools.partial(halo_kernel, n_cols, (n_x, n_y), last),
            out_shape=[new] + ([] if last else [block] * (2 * SLOTS)),
            in_specs=[SM] * 3 + [VM] * (2 + len(side)),
            out_specs=[VM] * (1 if last else 1 + 2 * SLOTS),
            scratch_shapes=[] if last else fold_scratch,
            compiler_params=PARAMS,
            name="halo_last" if last else "halo",
        )(*tables, bulk, sponge, *sides)
        state, blocks = out[0], out[1:]
    return state


def solution(mesh):
    in_specs = (
        P("grid", None, "gx", "gy"),
        P("grid", "gx", "gy"),
        P("grid", "gx", "gy"),
        P("grid", "gx", "gy"),
        P("grid", "gx", "gy"),
        P("grid", "gx", "gy"),
        P(),
        P(),
        P(),
        P(),
    )
    out_specs = P("grid", None, "gx", "gy")
    return jax.shard_map(local, mesh=mesh, in_specs=in_specs, out_specs=out_specs, check_vma=False)
```

```python
import functools

import jax
import jax.numpy as jnp
from jax import lax
from jax.experimental import pallas as pl
from jax.experimental.pallas import tpu as pltpu
from jax.sharding import PartitionSpec as P

NCLS = 3
LEV = 8
STEPS = 2
SLOTS = 3
LANES = 128
CHUNK = 8

relaxation = 0.125

VM = pl.BlockSpec(memory_space=pltpu.VMEM)
SM = pl.BlockSpec(memory_space=pltpu.SMEM)
PARAMS = pltpu.CompilerParams(vmem_limit_bytes=16 * 2**20)


def place():
    return lax.axis_index("grid"), lax.axis_index("gx"), lax.axis_index("gy")


def pieces(flip, top, left):
    _, i, j = place()
    for slot in range(SLOTS):
        for kind, row in ((0, i), (1, jnp.bitwise_xor(i, 1))):
            yield slot, kind, flip[slot, j, row] == kind, top[slot, j, row], left[slot, j, row]


def widen(half, cells):
    row = lax.broadcasted_iota(jnp.int32, (half, cells), 0)
    col = lax.broadcasted_iota(jnp.int32, (half, cells), 1)
    return (lax.shift_right_logical(col, 1) == row).astype(jnp.float32)


def narrow(cells, half):
    row = lax.broadcasted_iota(jnp.int32, (cells, half), 0)
    col = lax.broadcasted_iota(jnp.int32, (cells, half), 1)
    return (lax.shift_right_logical(row, 1) == col).astype(jnp.float32)


def near(first, half_r):
    base = jnp.minimum(lax.shift_right_logical(first, 3) * 8, half_r - 8)
    return pl.multiple_of(base, 8), first - base


def crop(source, out, first, begin):
    comps, cells_r, cells_c = source.shape
    half_r, half_c = out.shape[1:]
    groups = half_r // 8
    base, rest = near(first, half_r)
    row = lax.broadcasted_iota(jnp.int32, (8, half_c), 0)
    lane = lax.broadcasted_iota(jnp.int32, (8, half_c), 1)
    turn_c = lax.rem(2 * half_c - begin, half_c)
    turn_r = lax.rem(8 - rest, 8)
    left_part = lane < half_c - begin
    upper_part = row < 8 - rest
    for c in range(0, comps, CHUNK):
        block = source[c : c + CHUNK, pl.ds(base, half_r + 8), :].reshape(CHUNK * (groups + 1), 8, cells_c)
        low = pltpu.roll(block[..., :half_c], turn_c, 2)
        high = pltpu.roll(block[..., half_c:], turn_c, 2)
        block = pltpu.roll(jnp.where(left_part, low, high), turn_r, 1).reshape(CHUNK, groups + 1, 8, half_c)
        for k in range(groups):
            out[c : c + CHUNK, k * 8 : k * 8 + 8, :] = jnp.where(upper_part, block[:, k], block[:, k + 1])


def add_at(total, piece, first, begin):
    comps, half_r, half_c = piece.shape
    groups = half_r // 8
    base, rest = near(first, half_r)
    row = lax.broadcasted_iota(jnp.int32, (8, half_c), 0)
    lane = lax.broadcasted_iota(jnp.int32, (8, half_c), 1)
    turn_c = lax.rem(begin, half_c)
    turn_r = lax.rem(rest, 8)
    lower_part = row >= rest
    right_part = lane >= begin
    for c in range(0, comps, CHUNK):
        block = piece[c : c + CHUNK].reshape(CHUNK * groups, 8, half_c)
        block = pltpu.roll(block, turn_r, 1).reshape(CHUNK, groups, 8, half_c)
        none = jnp.zeros((CHUNK, 8, half_c), jnp.float32)
        for k in range(groups + 1):
            here = block[:, k] if k < groups else none
            above = block[:, k - 1] if k else none
            turned = pltpu.roll(jnp.where(lower_part, here, above), turn_c, 2)
            rows = pl.ds(base + k * 8, 8)
            total[c : c + CHUNK, rows, :half_c] += jnp.where(right_part, turned, 0.0)
            total[c : c + CHUNK, rows, half_c:] += jnp.where(right_part, 0.0, turned)


def payload(flip, top, left, state, sponge, straight, crossed, rows, fine):
    comps, cells_r, cells_c = state.shape
    half_r, half_c = cells_r // 2, cells_c // 2
    grid, _, _ = place()

    @pl.when(grid == 0)
    def _():
        for slot, kind, serves, first, begin in pieces(flip, top, left):

            @pl.when(serves)
            def _():
                crop(state, (straight, crossed)[kind][slot], first, begin)

    @pl.when(grid > 0)
    def _():
        weight = sponge[0]

        def fold(c, carry):
            block = weight * state[c]
            for k in range(cells_c // LANES):
                part = slice(k * LANES, (k + 1) * LANES)
                fine[k] = block[:, part]
                rows[c, :, part] = fine[k, pl.ds(0, half_r, 2), :] + fine[k, pl.ds(1, half_r, 2), :]
            return carry

        lax.fori_loop(0, comps, fold, 0)
        block = jnp.dot(
            rows[...].reshape(comps * half_r, cells_c),
            narrow(cells_c, half_c),
            precision=lax.Precision.HIGHEST,
            preferred_element_type=jnp.float32,
        ).reshape(comps, half_r, half_c)
        for slot in range(SLOTS):

            @pl.when(grid == slot + 1)
            def _():
                straight[slot][...] = block
                crossed[slot][...] = block


def first_kernel(flip, top, left, state, sponge, *rest):
    outs, (rows, fine) = rest[:-2], rest[-2:]
    payload(flip, top, left, state.at[0], sponge, outs[:SLOTS], outs[SLOTS:], rows, fine)


def edge_sides(index):
    even = lax.rem(index, 2) == 0
    return even, jnp.logical_not(even)


def update_kernel(n_cols, flip, top, left, rates, state, sponge, agg, brk, mask, diff, *rest):
    got = rest[: 2 * SLOTS]
    n_side = 2 + n_cols
    bulk, sides = rest[2 * SLOTS], rest[2 * SLOTS + 1 : 2 * SLOTS + 1 + n_side]
    bulk = bulk.at[0] if len(bulk.shape) == 4 else bulk
    nested, wide, coarse, fine = rest[2 * SLOTS + 1 + n_side :]
    comps, cells_r, cells_c = bulk.shape
    half_r, half_c = cells_r // 2, cells_c // 2
    grid, i, j = place()
    row_id = lax.broadcasted_iota(jnp.int32, (cells_r, cells_c), 0)
    col_id = lax.broadcasted_iota(jnp.int32, (cells_r, cells_c), 1)

    @pl.when(grid == 0)
    def _():
        covered = jnp.zeros((cells_r, cells_c), jnp.float32)
        for _, _, serves, first, begin in pieces(flip, top, left):
            inside = (row_id >= first) & (row_id < first + half_r) & (col_id >= begin) & (col_id < begin + half_c)
            covered = covered + jnp.where(inside & serves, 1.0, 0.0)
        keep = 1.0 - relaxation * covered

        def own(step, carry):
            rows = pl.ds(step * CHUNK, CHUNK)
            nested[rows] = keep * state[rows]
            return carry

        lax.fori_loop(0, comps // CHUNK, own, 0)
        for slot, kind, serves, first, begin in pieces(flip, top, left):

            @pl.when(serves)
            def _():
                add_at(nested, got[kind * SLOTS + slot], first, begin)

    @pl.when(grid > 0)
    def _():
        for slot in range(SLOTS):
            for kind in range(2):

                @pl.when((grid == slot + 1) & (flip[slot, j, i] == kind))
                def _():
                    coarse[...] = got[kind * SLOTS + slot][...]

        wide[...] = jnp.dot(
            coarse[...].reshape(comps * half_r, half_c),
            widen(half_c, cells_c) * (relaxation / 4.0),
            precision=lax.Precision.HIGHEST,
            preferred_element_type=jnp.float32,
        ).reshape(comps, half_r, cells_c)
        keep = 1.0 - sponge[0]

        def own(c, carry):
            for k in range(cells_c // LANES):
                part = slice(k * LANES, (k + 1) * LANES)
                block = wide[c, :, part]
                fine[k, pl.ds(0, half_r, 2), :] = block
                fine[k, pl.ds(1, half_r, 2), :] = block
                nested[c, :, part] = keep[:, part] * state[c, :, part] + fine[k]
            return carry

        lax.fori_loop(0, comps, own, 0)

    a, b = agg[0], brk[0]
    wet = mask[0].astype(jnp.float32)
    spread = diff[0]
    row_far = edge_sides(i)
    col_far = edge_sides(j)
    lane = lax.broadcasted_iota(jnp.int32, (cells_r, LANES), 1)

    def level(step, carry):
        below, columns = carry
        l = LEV - 1 - step
        u0, u1, u2 = nested[l], nested[LEV + l], nested[2 * LEV + l]
        flocced = ((1.0 - a) * u0 + a * u1, b * u0 + (1.0 - a - b) * u1 + a * u2, b * u1 + (1.0 - b) * u2)
        columns = list(columns)
        for cls in range(NCLS):
            c = cls * LEV + l
            rate = rates[grid, cls]
            w = wet * ((1.0 - rate) * flocced[cls] + rate * below[cls])
            f = spread * w
            total = w - 4.0 * f
            total = total + jnp.where(row_id == 0, 0.0, pltpu.roll(f, 1, 0))
            total = total + jnp.where(row_id == cells_r - 1, 0.0, pltpu.roll(f, cells_r - 1, 0))
            total = total + jnp.where(col_id == 0, 0.0, pltpu.roll(f, 1, 1))
            total = total + jnp.where(col_id == cells_c - 1, 0.0, pltpu.roll(f, cells_c - 1, 1))
            bulk[c] = total
            for phase in range(2):
                sides[phase][pl.ds(c, 1), :] = jnp.where(row_far[phase], f[cells_r - 1 :], f[:1])
            for phase in range(n_cols):
                far = col_far[phase]
                slab = jnp.where(far, f[:, cells_c - LANES :], f[:, :LANES])
                turn = lax.rem(c - jnp.where(far, LANES - 1, 0) + LANES, LANES)
                columns[phase] = jnp.where(lane == c, pltpu.roll(slab, turn, 1), columns[phase])
        return flocced, tuple(columns)

    nothing = jnp.zeros((cells_r, cells_c), jnp.float32)
    empty = jnp.zeros((cells_r, LANES), jnp.float32)
    _, columns = lax.fori_loop(0, LEV, level, ((nothing,) * NCLS, (empty,) * n_cols))
    for phase in range(n_cols):
        sides[2 + phase][...] = columns[phase]


def halo_kernel(n_cols, sizes, last, flip, top, left, bulk, sponge, *rest):
    sides = rest[: 2 + n_cols]
    state = rest[2 + n_cols]
    old, new = (bulk.at[0], state.at[0]) if last else (bulk, state)
    comps, cells_r, cells_c = new.shape
    _, i, j = place()
    row = lax.broadcasted_iota(jnp.int32, (8, cells_c), 0)
    even, _ = edge_sides(i)
    first, second = sides[0][...], sides[1][...]
    above = jnp.where(i == 0, 0.0, jnp.where(even, second, first))
    below = jnp.where(i == sizes[0] - 1, 0.0, jnp.where(even, first, second))
    for c in range(comps):
        new[c, :8, :] = old[c, :8, :] + jnp.where(row == 0, above[c : c + 1], 0.0)
        new[c, 8 : cells_r - 8, :] = old[c, 8 : cells_r - 8, :]
        new[c, cells_r - 8 :, :] = old[c, cells_r - 8 :, :] + jnp.where(row == 7, below[c : c + 1], 0.0)
    lane = lax.broadcasted_iota(jnp.int32, (cells_r, LANES), 1)
    for phase, far in zip(range(n_cols), edge_sides(j)):
        column = sides[2 + phase][...]

        @pl.when(far & (j < sizes[1] - 1))
        def _():
            for c in range(comps):
                new[c, :, cells_c - LANES :] += jnp.where(lane == LANES - 1, pltpu.roll(column, LANES - 1 - c, 1), 0.0)

        @pl.when(jnp.logical_not(far) & (j > 0))
        def _():
            for c in range(comps):
                new[c, :, :LANES] += jnp.where(lane == 0, pltpu.roll(column, (LANES - c) % LANES, 1), 0.0)

    if not last:
        outs, (rows, fine) = rest[3 + n_cols : -2], rest[-2:]
        payload(flip, top, left, new, sponge, outs[:SLOTS], outs[SLOTS:], rows, fine)


def exchange(blocks):
    n_x = lax.axis_size("gx")
    got = [None] * (2 * SLOTS)
    for slot in reversed(range(SLOTS)):
        for kind in range(2):
            pairs = []
            for i in range(n_x):
                parent, child = i, (slot + 1) * n_x + (i ^ kind)
                pairs += [(parent, child), (child, parent)]
            got[kind * SLOTS + slot] = lax.ppermute(blocks[kind * SLOTS + slot], ("grid", "gx"), pairs)
    return got


def swap_pairs(size, phase):
    pairs = []
    for k in range(phase, size + phase, 2):
        first, second = k % size, (k + 1) % size
        pairs += [(first, second), (second, first)]
    return pairs


def local(adjoint, sea_mask, diffusivity, aggregation, breakup, sponge, settling, partner_flip, row_offset, col_offset):
    comps, cells_r, cells_c = adjoint.shape[1:]
    half_r, half_c = cells_r // 2, cells_c // 2
    n_x, n_y = lax.axis_size("gx"), lax.axis_size("gy")
    n_cols = 1 if n_y == 2 else 2
    f32 = jnp.float32
    tile = jax.ShapeDtypeStruct((comps, cells_r, cells_c), f32)
    block = jax.ShapeDtypeStruct((comps, half_r, half_c), f32)
    side = [jax.ShapeDtypeStruct((comps, cells_c), f32)] * 2 + [jax.ShapeDtypeStruct((cells_r, LANES), f32)] * n_cols
    fold_scratch = [pltpu.VMEM((comps, half_r, cells_c), f32), pltpu.VMEM((cells_c // LANES, cells_r, LANES), f32)]
    tables = [table.transpose(0, 2, 1) for table in (partner_flip, row_offset, col_offset)]

    blocks = pl.pallas_call(
        first_kernel,
        out_shape=[block] * (2 * SLOTS),
        in_specs=[SM] * 3 + [VM] * 2,
        out_specs=[VM] * (2 * SLOTS),
        scratch_shapes=fold_scratch,
        compiler_params=PARAMS,
        name="first_payload",
    )(*tables, adjoint, sponge)
    state = adjoint.reshape(tile.shape)
    for step in range(STEPS):
        got = exchange(blocks)
        last = step == STEPS - 1
        new = jax.ShapeDtypeStruct(adjoint.shape, f32) if last else tile
        bulk, *sides = pl.pallas_call(
            functools.partial(update_kernel, n_cols),
            out_shape=[new] + side,
            in_specs=[SM] * 4 + [VM] * (6 + 2 * SLOTS),
            out_specs=[VM] * (1 + len(side)),
            scratch_shapes=[
                pltpu.VMEM(tile.shape, f32),
                pltpu.VMEM((comps, half_r, cells_c), f32),
                pltpu.VMEM(block.shape, f32),
                pltpu.VMEM((cells_c // LANES, cells_r, LANES), f32),
            ],
            compiler_params=PARAMS,
            name="update",
        )(*tables, settling, state, sponge, aggregation, breakup, sea_mask, diffusivity, *got)
        sides = [lax.ppermute(sides[k], "gx", swap_pairs(n_x, k)) for k in range(2)] + [
            lax.ppermute(sides[2 + k], "gy", swap_pairs(n_y, k)) for k in range(n_cols)
        ]
        out = pl.pallas_call(
            functools.partial(halo_kernel, n_cols, (n_x, n_y), last),
            out_shape=[new] + ([] if last else [block] * (2 * SLOTS)),
            in_specs=[SM] * 3 + [VM] * (2 + len(side)),
            out_specs=[VM] * (1 if last else 1 + 2 * SLOTS),
            scratch_shapes=[] if last else fold_scratch,
            compiler_params=PARAMS,
            name="halo_last" if last else "halo",
        )(*tables, bulk, sponge, *sides)
        state, blocks = out[0], out[1:]
    return state


def solution(mesh):
    in_specs = (
        P("grid", None, "gx", "gy"),
        P("grid", "gx", "gy"),
        P("grid", "gx", "gy"),
        P("grid", "gx", "gy"),
        P("grid", "gx", "gy"),
        P("grid", "gx", "gy"),
        P(),
        P(),
        P(),
        P(),
    )
    out_specs = P("grid", None, "gx", "gy")
    return jax.shard_map(local, mesh=mesh, in_specs=in_specs, out_specs=out_specs, check_vma=False)
```

```python
import functools

import jax
import jax.numpy as jnp
from jax import lax
from jax.experimental import pallas as pl
from jax.experimental.pallas import tpu as pltpu
from jax.sharding import PartitionSpec as P

NCLS = 3
LEV = 8
STEPS = 2
SLOTS = 3
LANES = 128
CHUNK = 8

relaxation = 0.125

VM = pl.BlockSpec(memory_space=pltpu.VMEM)
SM = pl.BlockSpec(memory_space=pltpu.SMEM)
PARAMS = pltpu.CompilerParams(vmem_limit_bytes=16 * 2**20)


def place():
    return lax.axis_index("grid"), lax.axis_index("gx"), lax.axis_index("gy")


ORDER = ((0, 0), (0, 1), (1, 0), (1, 1), (2, 0), (2, 1))


def sorted_out(blocks):
    return [blocks[ORDER.index((slot, kind))] for kind in range(2) for slot in range(SLOTS)]


def pieces(flip, top, left):
    _, i, j = place()
    for slot in range(SLOTS):
        for kind, row in ((0, i), (1, jnp.bitwise_xor(i, 1))):
            yield slot, kind, flip[slot, j, row] == kind, top[slot, j, row], left[slot, j, row]


def widen(half, cells):
    row = lax.broadcasted_iota(jnp.int32, (half, cells), 0)
    col = lax.broadcasted_iota(jnp.int32, (half, cells), 1)
    return (lax.shift_right_logical(col, 1) == row).astype(jnp.float32)


def narrow(cells, half):
    row = lax.broadcasted_iota(jnp.int32, (cells, half), 0)
    col = lax.broadcasted_iota(jnp.int32, (cells, half), 1)
    return (lax.shift_right_logical(row, 1) == col).astype(jnp.float32)


def near(first, half_r):
    base = jnp.minimum(lax.shift_right_logical(first, 3) * 8, half_r - 8)
    return pl.multiple_of(base, 8), first - base


def crop(source, out, first, begin):
    comps, cells_r, cells_c = source.shape
    half_r, half_c = out.shape[1:]
    groups = half_r // 8
    base, rest = near(first, half_r)
    row = lax.broadcasted_iota(jnp.int32, (8, half_c), 0)
    lane = lax.broadcasted_iota(jnp.int32, (8, half_c), 1)
    turn_c = lax.rem(2 * half_c - begin, half_c)
    turn_r = lax.rem(8 - rest, 8)
    left_part = lane < half_c - begin
    upper_part = row < 8 - rest
    for c in range(0, comps, CHUNK):
        block = source[c : c + CHUNK, pl.ds(base, half_r + 8), :].reshape(CHUNK * (groups + 1), 8, cells_c)
        low = pltpu.roll(block[..., :half_c], turn_c, 2)
        high = pltpu.roll(block[..., half_c:], turn_c, 2)
        block = pltpu.roll(jnp.where(left_part, low, high), turn_r, 1).reshape(CHUNK, groups + 1, 8, half_c)
        for k in range(groups):
            out[c : c + CHUNK, k * 8 : k * 8 + 8, :] = jnp.where(upper_part, block[:, k], block[:, k + 1])


def add_at(total, piece, first, begin):
    comps, half_r, half_c = piece.shape
    groups = half_r // 8
    base, rest = near(first, half_r)
    row = lax.broadcasted_iota(jnp.int32, (8, half_c), 0)
    lane = lax.broadcasted_iota(jnp.int32, (8, half_c), 1)
    turn_c = lax.rem(begin, half_c)
    turn_r = lax.rem(rest, 8)
    lower_part = row >= rest
    right_part = lane >= begin
    for c in range(0, comps, CHUNK):
        block = piece[c : c + CHUNK].reshape(CHUNK * groups, 8, half_c)
        block = pltpu.roll(block, turn_r, 1).reshape(CHUNK, groups, 8, half_c)
        none = jnp.zeros((CHUNK, 8, half_c), jnp.float32)
        for k in range(groups + 1):
            here = block[:, k] if k < groups else none
            above = block[:, k - 1] if k else none
            turned = pltpu.roll(jnp.where(lower_part, here, above), turn_c, 2)
            rows = pl.ds(base + k * 8, 8)
            total[c : c + CHUNK, rows, :half_c] += jnp.where(right_part, turned, 0.0)
            total[c : c + CHUNK, rows, half_c:] += jnp.where(right_part, 0.0, turned)


def payload(flip, top, left, state, sponge, straight, crossed, rows, fine):
    comps, cells_r, cells_c = state.shape
    half_r, half_c = cells_r // 2, cells_c // 2
    grid, _, _ = place()

    @pl.when(grid == 0)
    def _():
        for slot, kind, serves, first, begin in pieces(flip, top, left):

            @pl.when(serves)
            def _():
                crop(state, (straight, crossed)[kind][slot], first, begin)

    @pl.when(grid > 0)
    def _():
        weight = sponge[0]

        def fold(c, carry):
            block = weight * state[c]
            for k in range(cells_c // LANES):
                part = slice(k * LANES, (k + 1) * LANES)
                fine[k] = block[:, part]
                rows[c, :, part] = fine[k, pl.ds(0, half_r, 2), :] + fine[k, pl.ds(1, half_r, 2), :]
            return carry

        lax.fori_loop(0, comps, fold, 0)
        block = jnp.dot(
            rows[...].reshape(comps * half_r, cells_c),
            narrow(cells_c, half_c),
            precision=lax.Precision.HIGHEST,
            preferred_element_type=jnp.float32,
        ).reshape(comps, half_r, half_c)
        for slot in range(SLOTS):

            @pl.when(grid == slot + 1)
            def _():
                straight[slot][...] = block
                crossed[slot][...] = block


def first_kernel(flip, top, left, state, sponge, *rest):
    outs, (rows, fine) = rest[:-2], rest[-2:]
    outs = sorted_out(outs)
    payload(flip, top, left, state.at[0], sponge, outs[:SLOTS], outs[SLOTS:], rows, fine)


def edge_sides(index):
    even = lax.rem(index, 2) == 0
    return even, jnp.logical_not(even)


def update_kernel(n_cols, flip, top, left, rates, state, sponge, agg, brk, mask, diff, *rest):
    got = sorted_out(rest[: 2 * SLOTS])
    n_side = 2 + n_cols
    bulk, sides = rest[2 * SLOTS], rest[2 * SLOTS + 1 : 2 * SLOTS + 1 + n_side]
    bulk = bulk.at[0] if len(bulk.shape) == 4 else bulk
    nested, wide, coarse, fine = rest[2 * SLOTS + 1 + n_side :]
    comps, cells_r, cells_c = bulk.shape
    half_r, half_c = cells_r // 2, cells_c // 2
    grid, i, j = place()
    row_id = lax.broadcasted_iota(jnp.int32, (cells_r, cells_c), 0)
    col_id = lax.broadcasted_iota(jnp.int32, (cells_r, cells_c), 1)

    @pl.when(grid == 0)
    def _():
        covered = jnp.zeros((cells_r, cells_c), jnp.float32)
        for _, _, serves, first, begin in pieces(flip, top, left):
            inside = (row_id >= first) & (row_id < first + half_r) & (col_id >= begin) & (col_id < begin + half_c)
            covered = covered + jnp.where(inside & serves, 1.0, 0.0)
        keep = 1.0 - relaxation * covered

        def own(step, carry):
            rows = pl.ds(step * CHUNK, CHUNK)
            nested[rows] = keep * state[rows]
            return carry

        lax.fori_loop(0, comps // CHUNK, own, 0)
        for slot, kind, serves, first, begin in pieces(flip, top, left):

            @pl.when(serves)
            def _():
                add_at(nested, got[kind * SLOTS + slot], first, begin)

    @pl.when(grid > 0)
    def _():
        for slot in range(SLOTS):
            for kind in range(2):

                @pl.when((grid == slot + 1) & (flip[slot, j, i] == kind))
                def _():
                    coarse[...] = got[kind * SLOTS + slot][...]

        wide[...] = jnp.dot(
            coarse[...].reshape(comps * half_r, half_c),
            widen(half_c, cells_c) * (relaxation / 4.0),
            precision=lax.Precision.HIGHEST,
            preferred_element_type=jnp.float32,
        ).reshape(comps, half_r, cells_c)
        keep = 1.0 - sponge[0]

        def own(c, carry):
            for k in range(cells_c // LANES):
                part = slice(k * LANES, (k + 1) * LANES)
                block = wide[c, :, part]
                fine[k, pl.ds(0, half_r, 2), :] = block
                fine[k, pl.ds(1, half_r, 2), :] = block
                nested[c, :, part] = keep[:, part] * state[c, :, part] + fine[k]
            return carry

        lax.fori_loop(0, comps, own, 0)

    a, b = agg[0], brk[0]
    wet = mask[0].astype(jnp.float32)
    spread = diff[0]
    row_far = edge_sides(i)
    col_far = edge_sides(j)
    lane = lax.broadcasted_iota(jnp.int32, (cells_r, LANES), 1)

    def level(step, carry):
        below, columns = carry
        l = LEV - 1 - step
        u0, u1, u2 = nested[l], nested[LEV + l], nested[2 * LEV + l]
        flocced = ((1.0 - a) * u0 + a * u1, b * u0 + (1.0 - a - b) * u1 + a * u2, b * u1 + (1.0 - b) * u2)
        columns = list(columns)
        for cls in range(NCLS):
            c = cls * LEV + l
            rate = rates[grid, cls]
            w = wet * ((1.0 - rate) * flocced[cls] + rate * below[cls])
            f = spread * w
            total = w - 4.0 * f
            total = total + jnp.where(row_id == 0, 0.0, pltpu.roll(f, 1, 0))
            total = total + jnp.where(row_id == cells_r - 1, 0.0, pltpu.roll(f, cells_r - 1, 0))
            total = total + jnp.where(col_id == 0, 0.0, pltpu.roll(f, 1, 1))
            total = total + jnp.where(col_id == cells_c - 1, 0.0, pltpu.roll(f, cells_c - 1, 1))
            bulk[c] = total
            for phase in range(2):
                sides[phase][pl.ds(c, 1), :] = jnp.where(row_far[phase], f[cells_r - 1 :], f[:1])
            for phase in range(n_cols):
                far = col_far[phase]
                slab = jnp.where(far, f[:, cells_c - LANES :], f[:, :LANES])
                turn = lax.rem(c - jnp.where(far, LANES - 1, 0) + LANES, LANES)
                columns[phase] = jnp.where(lane == c, pltpu.roll(slab, turn, 1), columns[phase])
        return flocced, tuple(columns)

    nothing = jnp.zeros((cells_r, cells_c), jnp.float32)
    empty = jnp.zeros((cells_r, LANES), jnp.float32)
    _, columns = lax.fori_loop(0, LEV, level, ((nothing,) * NCLS, (empty,) * n_cols))
    for phase in range(n_cols):
        sides[2 + phase][...] = columns[phase]


def halo_kernel(n_cols, sizes, last, flip, top, left, bulk, sponge, *rest):
    sides = rest[: 2 + n_cols]
    state = rest[2 + n_cols]
    old, new = (bulk.at[0], state.at[0]) if last else (bulk, state)
    comps, cells_r, cells_c = new.shape
    _, i, j = place()
    row = lax.broadcasted_iota(jnp.int32, (8, cells_c), 0)
    even, _ = edge_sides(i)
    first, second = sides[0][...], sides[1][...]
    above = jnp.where(i == 0, 0.0, jnp.where(even, second, first))
    below = jnp.where(i == sizes[0] - 1, 0.0, jnp.where(even, first, second))
    for c in range(comps):
        new[c, :8, :] = old[c, :8, :] + jnp.where(row == 0, above[c : c + 1], 0.0)
        new[c, 8 : cells_r - 8, :] = old[c, 8 : cells_r - 8, :]
        new[c, cells_r - 8 :, :] = old[c, cells_r - 8 :, :] + jnp.where(row == 7, below[c : c + 1], 0.0)
    lane = lax.broadcasted_iota(jnp.int32, (cells_r, LANES), 1)
    for phase, far in zip(range(n_cols), edge_sides(j)):
        column = sides[2 + phase][...]

        @pl.when(far & (j < sizes[1] - 1))
        def _():
            for c in range(comps):
                new[c, :, cells_c - LANES :] += jnp.where(lane == LANES - 1, pltpu.roll(column, LANES - 1 - c, 1), 0.0)

        @pl.when(jnp.logical_not(far) & (j > 0))
        def _():
            for c in range(comps):
                new[c, :, :LANES] += jnp.where(lane == 0, pltpu.roll(column, (LANES - c) % LANES, 1), 0.0)

    if not last:
        outs, (rows, fine) = rest[3 + n_cols : -2], rest[-2:]
        outs = sorted_out(outs)
        payload(flip, top, left, new, sponge, outs[:SLOTS], outs[SLOTS:], rows, fine)


def exchange(blocks):
    n_x = lax.axis_size("gx")
    got = []
    for (slot, kind), block in zip(ORDER, blocks):
        pairs = []
        for i in range(n_x):
            parent, child = i, (slot + 1) * n_x + (i ^ kind)
            pairs += [(parent, child), (child, parent)]
        got.append(lax.ppermute(block, ("grid", "gx"), pairs))
    return got


def swap_pairs(size, phase):
    pairs = []
    for k in range(phase, size + phase, 2):
        first, second = k % size, (k + 1) % size
        pairs += [(first, second), (second, first)]
    return pairs


def local(adjoint, sea_mask, diffusivity, aggregation, breakup, sponge, settling, partner_flip, row_offset, col_offset):
    comps, cells_r, cells_c = adjoint.shape[1:]
    half_r, half_c = cells_r // 2, cells_c // 2
    n_x, n_y = lax.axis_size("gx"), lax.axis_size("gy")
    n_cols = 1 if n_y == 2 else 2
    f32 = jnp.float32
    tile = jax.ShapeDtypeStruct((comps, cells_r, cells_c), f32)
    block = jax.ShapeDtypeStruct((comps, half_r, half_c), f32)
    side = [jax.ShapeDtypeStruct((comps, cells_c), f32)] * 2 + [jax.ShapeDtypeStruct((cells_r, LANES), f32)] * n_cols
    fold_scratch = [pltpu.VMEM((comps, half_r, cells_c), f32), pltpu.VMEM((cells_c // LANES, cells_r, LANES), f32)]
    tables = [table.transpose(0, 2, 1) for table in (partner_flip, row_offset, col_offset)]

    blocks = pl.pallas_call(
        first_kernel,
        out_shape=[block] * (2 * SLOTS),
        in_specs=[SM] * 3 + [VM] * 2,
        out_specs=[VM] * (2 * SLOTS),
        scratch_shapes=fold_scratch,
        compiler_params=PARAMS,
        name="first_payload",
    )(*tables, adjoint, sponge)
    state = adjoint.reshape(tile.shape)
    for step in range(STEPS):
        got = exchange(blocks)
        last = step == STEPS - 1
        new = jax.ShapeDtypeStruct(adjoint.shape, f32) if last else tile
        bulk, *sides = pl.pallas_call(
            functools.partial(update_kernel, n_cols),
            out_shape=[new] + side,
            in_specs=[SM] * 4 + [VM] * (6 + 2 * SLOTS),
            out_specs=[VM] * (1 + len(side)),
            scratch_shapes=[
                pltpu.VMEM(tile.shape, f32),
                pltpu.VMEM((comps, half_r, cells_c), f32),
                pltpu.VMEM(block.shape, f32),
                pltpu.VMEM((cells_c // LANES, cells_r, LANES), f32),
            ],
            compiler_params=PARAMS,
            name="update",
        )(*tables, settling, state, sponge, aggregation, breakup, sea_mask, diffusivity, *got)
        sides = [lax.ppermute(sides[k], "gx", swap_pairs(n_x, k)) for k in range(2)] + [
            lax.ppermute(sides[2 + k], "gy", swap_pairs(n_y, k)) for k in range(n_cols)
        ]
        out = pl.pallas_call(
            functools.partial(halo_kernel, n_cols, (n_x, n_y), last),
            out_shape=[new] + ([] if last else [block] * (2 * SLOTS)),
            in_specs=[SM] * 3 + [VM] * (2 + len(side)),
            out_specs=[VM] * (1 if last else 1 + 2 * SLOTS),
            scratch_shapes=[] if last else fold_scratch,
            compiler_params=PARAMS,
            name="halo_last" if last else "halo",
        )(*tables, bulk, sponge, *sides)
        state, blocks = out[0], out[1:]
    return state


def solution(mesh):
    in_specs = (
        P("grid", None, "gx", "gy"),
        P("grid", "gx", "gy"),
        P("grid", "gx", "gy"),
        P("grid", "gx", "gy"),
        P("grid", "gx", "gy"),
        P("grid", "gx", "gy"),
        P(),
        P(),
        P(),
        P(),
    )
    out_specs = P("grid", None, "gx", "gy")
    return jax.shard_map(local, mesh=mesh, in_specs=in_specs, out_specs=out_specs, check_vma=False)
```

```python
import functools

import jax
import jax.numpy as jnp
from jax import lax
from jax.experimental import pallas as pl
from jax.experimental.pallas import tpu as pltpu
from jax.sharding import PartitionSpec as P

NCLS = 3
LEV = 8
STEPS = 2
SLOTS = 3
LANES = 128
CHUNK = 8

relaxation = 0.125

VM = pl.BlockSpec(memory_space=pltpu.VMEM)
SM = pl.BlockSpec(memory_space=pltpu.SMEM)
PARAMS = pltpu.CompilerParams(vmem_limit_bytes=16 * 2**20)


def place():
    return lax.axis_index("grid"), lax.axis_index("gx"), lax.axis_index("gy")


ORDER = ((0, 0), (0, 1), (1, 0), (1, 1), (2, 0), (2, 1))


def sorted_out(blocks):
    return [blocks[ORDER.index((slot, kind))] for kind in range(2) for slot in range(SLOTS)]


def pieces(flip, top, left):
    _, i, j = place()
    for slot in range(SLOTS):
        for kind, row in ((0, i), (1, jnp.bitwise_xor(i, 1))):
            yield slot, kind, flip[slot, j, row] == kind, top[slot, j, row], left[slot, j, row]


def widen(half, cells):
    row = lax.broadcasted_iota(jnp.int32, (half, cells), 0)
    col = lax.broadcasted_iota(jnp.int32, (half, cells), 1)
    return (lax.shift_right_logical(col, 1) == row).astype(jnp.float32)


def narrow(cells, half):
    row = lax.broadcasted_iota(jnp.int32, (cells, half), 0)
    col = lax.broadcasted_iota(jnp.int32, (cells, half), 1)
    return (lax.shift_right_logical(row, 1) == col).astype(jnp.float32)


def near(first, half_r):
    base = jnp.minimum(lax.shift_right_logical(first, 3) * 8, half_r - 8)
    return pl.multiple_of(base, 8), first - base


def crop(source, out, first, begin):
    comps, cells_r, cells_c = source.shape
    half_r, half_c = out.shape[1:]
    groups = half_r // 8
    base, rest = near(first, half_r)
    row = lax.broadcasted_iota(jnp.int32, (8, half_c), 0)
    lane = lax.broadcasted_iota(jnp.int32, (8, half_c), 1)
    turn_c = lax.rem(2 * half_c - begin, half_c)
    turn_r = lax.rem(8 - rest, 8)
    left_part = lane < half_c - begin
    upper_part = row < 8 - rest
    for c in range(0, comps, CHUNK):
        block = source[c : c + CHUNK, pl.ds(base, half_r + 8), :].reshape(CHUNK * (groups + 1), 8, cells_c)
        low = pltpu.roll(block[..., :half_c], turn_c, 2)
        high = pltpu.roll(block[..., half_c:], turn_c, 2)
        block = pltpu.roll(jnp.where(left_part, low, high), turn_r, 1).reshape(CHUNK, groups + 1, 8, half_c)
        for k in range(groups):
            out[c : c + CHUNK, k * 8 : k * 8 + 8, :] = jnp.where(upper_part, block[:, k], block[:, k + 1])


def add_at(total, piece, first, begin):
    comps, half_r, half_c = piece.shape
    groups = half_r // 8
    base, rest = near(first, half_r)
    row = lax.broadcasted_iota(jnp.int32, (8, half_c), 0)
    lane = lax.broadcasted_iota(jnp.int32, (8, half_c), 1)
    turn_c = lax.rem(begin, half_c)
    turn_r = lax.rem(rest, 8)
    lower_part = row >= rest
    right_part = lane >= begin
    for c in range(0, comps, CHUNK):
        block = piece[c : c + CHUNK].reshape(CHUNK * groups, 8, half_c)
        block = pltpu.roll(block, turn_r, 1).reshape(CHUNK, groups, 8, half_c)
        none = jnp.zeros((CHUNK, 8, half_c), jnp.float32)
        for k in range(groups + 1):
            here = block[:, k] if k < groups else none
            above = block[:, k - 1] if k else none
            turned = pltpu.roll(jnp.where(lower_part, here, above), turn_c, 2)
            rows = pl.ds(base + k * 8, 8)
            total[c : c + CHUNK, rows, :half_c] += jnp.where(right_part, turned, 0.0)
            total[c : c + CHUNK, rows, half_c:] += jnp.where(right_part, 0.0, turned)


def payload(flip, top, left, state, sponge, straight, crossed, rows, fine):
    comps, cells_r, cells_c = state.shape
    half_r, half_c = cells_r // 2, cells_c // 2
    grid, _, _ = place()

    @pl.when(grid == 0)
    def _():
        for slot, kind, serves, first, begin in pieces(flip, top, left):

            @pl.when(serves)
            def _():
                crop(state, (straight, crossed)[kind][slot], first, begin)

    @pl.when(grid > 0)
    def _():
        weight = sponge[0]

        def fold(c, carry):
            block = weight * state[c]
            for k in range(cells_c // LANES):
                part = slice(k * LANES, (k + 1) * LANES)
                fine[k] = block[:, part]
                rows[c, :, part] = fine[k, pl.ds(0, half_r, 2), :] + fine[k, pl.ds(1, half_r, 2), :]
            return carry

        lax.fori_loop(0, comps, fold, 0)
        block = jnp.dot(
            rows[...].reshape(comps * half_r, cells_c),
            narrow(cells_c, half_c),
            precision=lax.Precision.HIGHEST,
            preferred_element_type=jnp.float32,
        ).reshape(comps, half_r, half_c)
        for slot in range(SLOTS):

            @pl.when(grid == slot + 1)
            def _():
                straight[slot][...] = block
                crossed[slot][...] = block


def first_kernel(*refs):
    given, outs, token = refs[:5], sorted_out(refs[5 : 5 + 2 * SLOTS]), refs[5 + 2 * SLOTS]
    rows, fine, *held, done = refs[6 + 2 * SLOTS :]
    token[...] = jnp.zeros_like(token)
    copies = [pltpu.make_async_copy(source, to, done.at[k]) for k, (source, to) in enumerate(zip(given, held))]
    for copy in copies:
        copy.start()
    for copy in copies:
        copy.wait()
    flip, top, left, state, sponge = held
    payload(flip, top, left, state.at[0], sponge, outs[:SLOTS], outs[SLOTS:], rows, fine)


def stage_kernel(token, *refs):
    given, held, done = refs[:10], refs[10:20], refs[20]
    copies = [pltpu.make_async_copy(source, to, done.at[k]) for k, (source, to) in enumerate(zip(given, held))]
    for copy in copies:
        copy.start()
    for copy in copies:
        copy.wait()


def edge_sides(index):
    even = lax.rem(index, 2) == 0
    return even, jnp.logical_not(even)


def update_kernel(n_cols, flip, top, left, rates, state, sponge, agg, brk, mask, diff, *rest):
    got = sorted_out(rest[: 2 * SLOTS])
    n_side = 2 + n_cols
    bulk, sides = rest[2 * SLOTS], rest[2 * SLOTS + 1 : 2 * SLOTS + 1 + n_side]
    bulk = bulk.at[0] if len(bulk.shape) == 4 else bulk
    nested, wide, coarse, fine = rest[2 * SLOTS + 1 + n_side :]
    comps, cells_r, cells_c = bulk.shape
    half_r, half_c = cells_r // 2, cells_c // 2
    grid, i, j = place()
    row_id = lax.broadcasted_iota(jnp.int32, (cells_r, cells_c), 0)
    col_id = lax.broadcasted_iota(jnp.int32, (cells_r, cells_c), 1)

    @pl.when(grid == 0)
    def _():
        covered = jnp.zeros((cells_r, cells_c), jnp.float32)
        for _, _, serves, first, begin in pieces(flip, top, left):
            inside = (row_id >= first) & (row_id < first + half_r) & (col_id >= begin) & (col_id < begin + half_c)
            covered = covered + jnp.where(inside & serves, 1.0, 0.0)
        keep = 1.0 - relaxation * covered

        def own(step, carry):
            rows = pl.ds(step * CHUNK, CHUNK)
            nested[rows] = keep * state[rows]
            return carry

        lax.fori_loop(0, comps // CHUNK, own, 0)
        for slot, kind, serves, first, begin in pieces(flip, top, left):

            @pl.when(serves)
            def _():
                add_at(nested, got[kind * SLOTS + slot], first, begin)

    @pl.when(grid > 0)
    def _():
        for slot in range(SLOTS):
            for kind in range(2):

                @pl.when((grid == slot + 1) & (flip[slot, j, i] == kind))
                def _():
                    coarse[...] = got[kind * SLOTS + slot][...]

        wide[...] = jnp.dot(
            coarse[...].reshape(comps * half_r, half_c),
            widen(half_c, cells_c) * (relaxation / 4.0),
            precision=lax.Precision.HIGHEST,
            preferred_element_type=jnp.float32,
        ).reshape(comps, half_r, cells_c)
        keep = 1.0 - sponge[0]

        def own(c, carry):
            for k in range(cells_c // LANES):
                part = slice(k * LANES, (k + 1) * LANES)
                block = wide[c, :, part]
                fine[k, pl.ds(0, half_r, 2), :] = block
                fine[k, pl.ds(1, half_r, 2), :] = block
                nested[c, :, part] = keep[:, part] * state[c, :, part] + fine[k]
            return carry

        lax.fori_loop(0, comps, own, 0)

    a, b = agg[0], brk[0]
    wet = mask[0].astype(jnp.float32)
    spread = diff[0]
    row_far = edge_sides(i)
    col_far = edge_sides(j)
    lane = lax.broadcasted_iota(jnp.int32, (cells_r, LANES), 1)

    def level(step, carry):
        below, columns = carry
        l = LEV - 1 - step
        u0, u1, u2 = nested[l], nested[LEV + l], nested[2 * LEV + l]
        flocced = ((1.0 - a) * u0 + a * u1, b * u0 + (1.0 - a - b) * u1 + a * u2, b * u1 + (1.0 - b) * u2)
        columns = list(columns)
        for cls in range(NCLS):
            c = cls * LEV + l
            rate = rates[grid, cls]
            w = wet * ((1.0 - rate) * flocced[cls] + rate * below[cls])
            f = spread * w
            total = w - 4.0 * f
            total = total + jnp.where(row_id == 0, 0.0, pltpu.roll(f, 1, 0))
            total = total + jnp.where(row_id == cells_r - 1, 0.0, pltpu.roll(f, cells_r - 1, 0))
            total = total + jnp.where(col_id == 0, 0.0, pltpu.roll(f, 1, 1))
            total = total + jnp.where(col_id == cells_c - 1, 0.0, pltpu.roll(f, cells_c - 1, 1))
            bulk[c] = total
            for phase in range(2):
                sides[phase][pl.ds(c, 1), :] = jnp.where(row_far[phase], f[cells_r - 1 :], f[:1])
            for phase in range(n_cols):
                far = col_far[phase]
                slab = jnp.where(far, f[:, cells_c - LANES :], f[:, :LANES])
                turn = lax.rem(c - jnp.where(far, LANES - 1, 0) + LANES, LANES)
                columns[phase] = jnp.where(lane == c, pltpu.roll(slab, turn, 1), columns[phase])
        return flocced, tuple(columns)

    nothing = jnp.zeros((cells_r, cells_c), jnp.float32)
    empty = jnp.zeros((cells_r, LANES), jnp.float32)
    _, columns = lax.fori_loop(0, LEV, level, ((nothing,) * NCLS, (empty,) * n_cols))
    for phase in range(n_cols):
        sides[2 + phase][...] = columns[phase]


def halo_kernel(n_cols, sizes, last, flip, top, left, bulk, sponge, *rest):
    sides = rest[: 2 + n_cols]
    state = rest[2 + n_cols]
    old, new = (bulk.at[0], state.at[0]) if last else (bulk, state)
    comps, cells_r, cells_c = new.shape
    _, i, j = place()
    row = lax.broadcasted_iota(jnp.int32, (8, cells_c), 0)
    even, _ = edge_sides(i)
    first, second = sides[0][...], sides[1][...]
    above = jnp.where(i == 0, 0.0, jnp.where(even, second, first))
    below = jnp.where(i == sizes[0] - 1, 0.0, jnp.where(even, first, second))
    for c in range(comps):
        new[c, :8, :] = old[c, :8, :] + jnp.where(row == 0, above[c : c + 1], 0.0)
        new[c, 8 : cells_r - 8, :] = old[c, 8 : cells_r - 8, :]
        new[c, cells_r - 8 :, :] = old[c, cells_r - 8 :, :] + jnp.where(row == 7, below[c : c + 1], 0.0)
    lane = lax.broadcasted_iota(jnp.int32, (cells_r, LANES), 1)
    for phase, far in zip(range(n_cols), edge_sides(j)):
        column = sides[2 + phase][...]

        @pl.when(far & (j < sizes[1] - 1))
        def _():
            for c in range(comps):
                new[c, :, cells_c - LANES :] += jnp.where(lane == LANES - 1, pltpu.roll(column, LANES - 1 - c, 1), 0.0)

        @pl.when(jnp.logical_not(far) & (j > 0))
        def _():
            for c in range(comps):
                new[c, :, :LANES] += jnp.where(lane == 0, pltpu.roll(column, (LANES - c) % LANES, 1), 0.0)

    if not last:
        outs, (rows, fine) = rest[3 + n_cols : -2], rest[-2:]
        outs = sorted_out(outs)
        payload(flip, top, left, new, sponge, outs[:SLOTS], outs[SLOTS:], rows, fine)


def exchange(blocks):
    n_x = lax.axis_size("gx")
    got = []
    for (slot, kind), block in zip(ORDER, blocks):
        pairs = []
        for i in range(n_x):
            parent, child = i, (slot + 1) * n_x + (i ^ kind)
            pairs += [(parent, child), (child, parent)]
        got.append(lax.ppermute(block, ("grid", "gx"), pairs))
    return got


def swap_pairs(size, phase):
    pairs = []
    for k in range(phase, size + phase, 2):
        first, second = k % size, (k + 1) % size
        pairs += [(first, second), (second, first)]
    return pairs


def local(adjoint, sea_mask, diffusivity, aggregation, breakup, sponge, settling, partner_flip, row_offset, col_offset):
    comps, cells_r, cells_c = adjoint.shape[1:]
    half_r, half_c = cells_r // 2, cells_c // 2
    n_x, n_y = lax.axis_size("gx"), lax.axis_size("gy")
    n_cols = 1 if n_y == 2 else 2
    f32 = jnp.float32
    tile = jax.ShapeDtypeStruct((comps, cells_r, cells_c), f32)
    block = jax.ShapeDtypeStruct((comps, half_r, half_c), f32)
    side = [jax.ShapeDtypeStruct((comps, cells_c), f32)] * 2 + [jax.ShapeDtypeStruct((cells_r, LANES), f32)] * n_cols
    fold_scratch = [pltpu.VMEM((comps, half_r, cells_c), f32), pltpu.VMEM((cells_c // LANES, cells_r, LANES), f32)]
    tables = [table.transpose(0, 2, 1) for table in (partner_flip, row_offset, col_offset)]

    *blocks, token = pl.pallas_call(
        first_kernel,
        out_shape=[block] * (2 * SLOTS) + [jax.ShapeDtypeStruct((8, LANES), f32)],
        in_specs=[pl.BlockSpec(memory_space=pltpu.HBM)] * 5,
        out_specs=[VM] * (2 * SLOTS + 1),
        scratch_shapes=fold_scratch
        + [pltpu.SMEM(table.shape, table.dtype) for table in tables]
        + [pltpu.VMEM(adjoint.shape, f32), pltpu.VMEM(sponge.shape, f32), pltpu.SemaphoreType.DMA((5,))],
        compiler_params=pltpu.CompilerParams(vmem_limit_bytes=60 * 2**20),
        name="first_payload",
    )(*tables, adjoint, sponge)
    fields = (adjoint, sponge, settling, aggregation, breakup, sea_mask, diffusivity, *tables)
    state, sponge, rates, *fields = pl.pallas_call(
        stage_kernel,
        out_shape=[jax.ShapeDtypeStruct(field.shape, field.dtype) for field in fields],
        in_specs=[VM] + [pl.BlockSpec(memory_space=pltpu.HBM)] * 10,
        out_specs=[VM] * 10,
        scratch_shapes=[pltpu.SemaphoreType.DMA((10,))],
        compiler_params=PARAMS,
        name="stage_fields",
    )(token, *fields)
    state = state.reshape(tile.shape)
    fields, tables = fields[:4], fields[4:]
    for step in range(STEPS):
        got = exchange(blocks)
        last = step == STEPS - 1
        new = jax.ShapeDtypeStruct(adjoint.shape, f32) if last else tile
        bulk, *sides = pl.pallas_call(
            functools.partial(update_kernel, n_cols),
            out_shape=[new] + side,
            in_specs=[SM] * 4 + [VM] * (6 + 2 * SLOTS),
            out_specs=[VM] * (1 + len(side)),
            scratch_shapes=[
                pltpu.VMEM(tile.shape, f32),
                pltpu.VMEM((comps, half_r, cells_c), f32),
                pltpu.VMEM(block.shape, f32),
                pltpu.VMEM((cells_c // LANES, cells_r, LANES), f32),
            ],
            compiler_params=PARAMS,
            name="update",
        )(*tables, rates, state, sponge, *fields, *got)
        sides = [lax.ppermute(sides[k], "gx", swap_pairs(n_x, k)) for k in range(2)] + [
            lax.ppermute(sides[2 + k], "gy", swap_pairs(n_y, k)) for k in range(n_cols)
        ]
        out = pl.pallas_call(
            functools.partial(halo_kernel, n_cols, (n_x, n_y), last),
            out_shape=[new] + ([] if last else [block] * (2 * SLOTS)),
            in_specs=[SM] * 3 + [VM] * (2 + len(side)),
            out_specs=[VM] * (1 if last else 1 + 2 * SLOTS),
            scratch_shapes=[] if last else fold_scratch,
            compiler_params=PARAMS,
            name="halo_last" if last else "halo",
        )(*tables, bulk, sponge, *sides)
        state, blocks = out[0], out[1:]
    return state


def solution(mesh):
    in_specs = (
        P("grid", None, "gx", "gy"),
        P("grid", "gx", "gy"),
        P("grid", "gx", "gy"),
        P("grid", "gx", "gy"),
        P("grid", "gx", "gy"),
        P("grid", "gx", "gy"),
        P(),
        P(),
        P(),
        P(),
    )
    out_specs = P("grid", None, "gx", "gy")
    return jax.shard_map(local, mesh=mesh, in_specs=in_specs, out_specs=out_specs, check_vma=False)
```

```python
import functools

import jax
import jax.numpy as jnp
from jax import lax
from jax.experimental import pallas as pl
from jax.experimental.pallas import tpu as pltpu
from jax.sharding import PartitionSpec as P

NCLS = 3
LEV = 8
STEPS = 2
SLOTS = 3
LANES = 128
CHUNK = 8

relaxation = 0.125

VM = pl.BlockSpec(memory_space=pltpu.VMEM)
SM = pl.BlockSpec(memory_space=pltpu.SMEM)
PARAMS = pltpu.CompilerParams(vmem_limit_bytes=16 * 2**20)


def place():
    return lax.axis_index("grid"), lax.axis_index("gx"), lax.axis_index("gy")


ORDER = ((0, 0), (0, 1), (1, 0), (1, 1), (2, 0), (2, 1))


def sorted_out(blocks):
    return [blocks[ORDER.index((slot, kind))] for kind in range(2) for slot in range(SLOTS)]


def pieces_of(flip, top, left):
    _, i, j = place()
    for slot in range(SLOTS):
        for kind, row in ((0, i), (1, jnp.bitwise_xor(i, 1))):
            yield slot, kind, flip[slot, j, row] == kind, top[slot, j, row], left[slot, j, row]


def pieces(plan):
    for k in range(2 * SLOTS):
        yield k // 2, k % 2, plan[3 * k] == 1, plan[3 * k + 1], plan[3 * k + 2]


def widen(half, cells):
    row = lax.broadcasted_iota(jnp.int32, (half, cells), 0)
    col = lax.broadcasted_iota(jnp.int32, (half, cells), 1)
    return (lax.shift_right_logical(col, 1) == row).astype(jnp.float32)


def narrow(cells, half):
    row = lax.broadcasted_iota(jnp.int32, (cells, half), 0)
    col = lax.broadcasted_iota(jnp.int32, (cells, half), 1)
    return (lax.shift_right_logical(row, 1) == col).astype(jnp.float32)


def near(first, half_r):
    base = jnp.minimum(lax.shift_right_logical(first, 3) * 8, half_r - 8)
    return pl.multiple_of(base, 8), first - base


def crop(source, out, first, begin):
    comps, cells_r, cells_c = source.shape
    half_r, half_c = out.shape[1:]
    groups = half_r // 8
    base, rest = near(first, half_r)
    row = lax.broadcasted_iota(jnp.int32, (8, half_c), 0)
    lane = lax.broadcasted_iota(jnp.int32, (8, half_c), 1)
    turn_c = lax.rem(2 * half_c - begin, half_c)
    turn_r = lax.rem(8 - rest, 8)
    left_part = lane < half_c - begin
    upper_part = row < 8 - rest
    for c in range(0, comps, CHUNK):
        block = source[c : c + CHUNK, pl.ds(base, half_r + 8), :].reshape(CHUNK * (groups + 1), 8, cells_c)
        low = pltpu.roll(block[..., :half_c], turn_c, 2)
        high = pltpu.roll(block[..., half_c:], turn_c, 2)
        block = pltpu.roll(jnp.where(left_part, low, high), turn_r, 1).reshape(CHUNK, groups + 1, 8, half_c)
        for k in range(groups):
            out[c : c + CHUNK, k * 8 : k * 8 + 8, :] = jnp.where(upper_part, block[:, k], block[:, k + 1])


def add_at(total, piece, first, begin):
    comps, half_r, half_c = piece.shape
    groups = half_r // 8
    base, rest = near(first, half_r)
    row = lax.broadcasted_iota(jnp.int32, (8, half_c), 0)
    lane = lax.broadcasted_iota(jnp.int32, (8, half_c), 1)
    turn_c = lax.rem(begin, half_c)
    turn_r = lax.rem(rest, 8)
    lower_part = row >= rest
    right_part = lane >= begin
    for c in range(0, comps, CHUNK):
        block = piece[c : c + CHUNK].reshape(CHUNK * groups, 8, half_c)
        block = pltpu.roll(block, turn_r, 1).reshape(CHUNK, groups, 8, half_c)
        none = jnp.zeros((CHUNK, 8, half_c), jnp.float32)
        for k in range(groups + 1):
            here = block[:, k] if k < groups else none
            above = block[:, k - 1] if k else none
            turned = pltpu.roll(jnp.where(lower_part, here, above), turn_c, 2)
            rows = pl.ds(base + k * 8, 8)
            total[c : c + CHUNK, rows, :half_c] += jnp.where(right_part, turned, 0.0)
            total[c : c + CHUNK, rows, half_c:] += jnp.where(right_part, 0.0, turned)


def fold(state, sponge, rows, fine):
    comps, cells_r, cells_c = state.shape
    half_r, half_c = cells_r // 2, cells_c // 2
    weight = sponge[0]

    def one(c, carry):
        block = weight * state[c]
        for k in range(cells_c // LANES):
            part = slice(k * LANES, (k + 1) * LANES)
            fine[k] = block[:, part]
            rows[c, :, part] = fine[k, pl.ds(0, half_r, 2), :] + fine[k, pl.ds(1, half_r, 2), :]
        return carry

    lax.fori_loop(0, comps, one, 0, unroll=4)
    return jnp.dot(
        rows[...].reshape(comps * half_r, cells_c),
        narrow(cells_c, half_c),
        precision=lax.Precision.HIGHEST,
        preferred_element_type=jnp.float32,
    ).reshape(comps, half_r, half_c)


def pack_fold(out, comps, above, below, low, high, sponge, fine):
    weight = sponge[0]
    cells_r, cells_c = weight.shape
    half_r, half_c = cells_r // 2, cells_c // 2
    lines = jnp.concatenate([weight[:1] * above, weight[cells_r - 1 :] * below], axis=0)
    out[: 2 * comps, :] = jnp.dot(
        lines, narrow(cells_c, half_c), precision=lax.Precision.HIGHEST, preferred_element_type=jnp.float32
    )
    for k, line in enumerate((weight[:, :1] * low, weight[:, cells_c - 1 :] * high)):
        fine[k] = line
        out[2 * comps + k * half_r : 2 * comps + (k + 1) * half_r, :] = (
            fine[k, pl.ds(0, half_r, 2), :] + fine[k, pl.ds(1, half_r, 2), :]
        )


def patch(block, extra, outs):
    comps, half_r, half_c = block.shape
    row = lax.broadcasted_iota(jnp.int32, (half_r, half_c), 0)
    lane = lax.broadcasted_iota(jnp.int32, (half_r, half_c), 1)
    low = extra[2 * comps : 2 * comps + half_r, :]
    high = extra[2 * comps + half_r : 2 * comps + 2 * half_r, :]
    for c in range(comps):
        total = block[c]
        total = total + jnp.where(row == 0, extra[c : c + 1, :], 0.0)
        total = total + jnp.where(row == half_r - 1, extra[comps + c : comps + c + 1, :], 0.0)
        total = total + jnp.where(lane == 0, pltpu.roll(low, (half_c - c) % half_c, 1), 0.0)
        total = total + jnp.where(lane == half_c - 1, pltpu.roll(high, half_c - 1 - c, 1), 0.0)
        for out in outs:
            out[c] = total


def first_kernel(*refs):
    given, outs, token = refs[:5], sorted_out(refs[5 : 5 + 2 * SLOTS]), refs[5 + 2 * SLOTS]
    rows, fine, *held, done = refs[6 + 2 * SLOTS :]
    token[...] = jnp.zeros_like(token)
    copies = [pltpu.make_async_copy(source, to, done.at[k]) for k, (source, to) in enumerate(zip(given, held))]
    for copy in copies:
        copy.start()
    for copy in copies:
        copy.wait()
    flip, top, left, state, sponge = held
    state = state.at[0]
    grid, _, _ = place()

    @pl.when(grid == 0)
    def _():
        for slot, kind, serves, first, begin in pieces_of(flip, top, left):

            @pl.when(serves)
            def _():
                crop(state, outs[kind * SLOTS + slot], first, begin)

    @pl.when(grid > 0)
    def _():
        block = fold(state, sponge, rows, fine)
        for slot in range(SLOTS):

            @pl.when(grid == slot + 1)
            def _():
                outs[slot][...] = block
                outs[SLOTS + slot][...] = block


def stage_kernel(token, *refs):
    given, held, (rates, plan), scratch = refs[:10], list(refs[10:16]), refs[16:18], refs[18:]
    speeds, *tables, done = scratch
    copies = [
        pltpu.make_async_copy(source, to, done.at[k])
        for k, (source, to) in enumerate(zip(given, held + [speeds] + tables))
    ]
    for copy in copies:
        copy.start()
    for copy in copies:
        copy.wait()
    grid, i, j = place()
    for cls in range(NCLS):
        rates[cls] = jnp.full(rates.shape[1:], speeds[grid, cls], jnp.float32)
    for k, (_, _, serves, first, begin) in enumerate(pieces_of(*tables)):
        plan[3 * k] = serves.astype(jnp.int32)
        plan[3 * k + 1] = first
        plan[3 * k + 2] = begin
    plan[6 * SLOTS] = tables[0][jnp.maximum(grid - 1, 0), j, i]


def edge_sides(index):
    even = lax.rem(index, 2) == 0
    return even, jnp.logical_not(even)


def update_kernel(n_cols, plan, rates, state, sponge, agg, brk, mask, diff, *rest):
    got, rest = sorted_out(rest[: 2 * SLOTS]), rest[2 * SLOTS :]
    wets, flux, sides = rest[0], rest[1], rest[2 : 4 + n_cols]
    nested, wide, coarse, fine = rest[4 + n_cols :]
    comps, cells_r, cells_c = wets.shape
    half_r, half_c = cells_r // 2, cells_c // 2
    grid, i, j = place()
    row_id = lax.broadcasted_iota(jnp.int32, (cells_r, cells_c), 0)
    col_id = lax.broadcasted_iota(jnp.int32, (cells_r, cells_c), 1)

    @pl.when(grid == 0)
    def _():
        covered = jnp.zeros((cells_r, cells_c), jnp.float32)
        for _, _, serves, first, begin in pieces(plan):
            inside = (row_id >= first) & (row_id < first + half_r) & (col_id >= begin) & (col_id < begin + half_c)
            covered = covered + jnp.where(inside & serves, 1.0, 0.0)
        keep = 1.0 - relaxation * covered

        def own(step, carry):
            rows = pl.ds(step * CHUNK, CHUNK)
            nested[rows] = keep * state[rows]
            return carry

        lax.fori_loop(0, comps // CHUNK, own, 0)
        for slot, kind, serves, first, begin in pieces(plan):

            @pl.when(serves)
            def _():
                add_at(nested, got[kind * SLOTS + slot], first, begin)

    @pl.when(grid > 0)
    def _():
        for slot in range(SLOTS):
            for kind in range(2):

                @pl.when((grid == slot + 1) & (plan[6 * SLOTS] == kind))
                def _():
                    coarse[...] = got[kind * SLOTS + slot][...]

        wide[...] = jnp.dot(
            coarse[...].reshape(comps * half_r, half_c),
            widen(half_c, cells_c) * (relaxation / 4.0),
            precision=lax.Precision.HIGHEST,
            preferred_element_type=jnp.float32,
        ).reshape(comps, half_r, cells_c)
        keep = 1.0 - sponge[0]

        def own(c, carry):
            for k in range(cells_c // LANES):
                part = slice(k * LANES, (k + 1) * LANES)
                block = wide[c, :, part]
                fine[k, pl.ds(0, half_r, 2), :] = block
                fine[k, pl.ds(1, half_r, 2), :] = block
                nested[c, :, part] = keep[:, part] * state[c, :, part] + fine[k]
            return carry

        lax.fori_loop(0, comps, own, 0, unroll=4)

    a, b = agg[0], brk[0]
    wet = mask[0].astype(jnp.float32)
    spread = diff[0]
    row_far = edge_sides(i)[::-1]
    col_far = edge_sides(j)
    lane = lax.broadcasted_iota(jnp.int32, (cells_r, LANES), 1)

    def level(step, carry):
        below, columns = carry
        l = LEV - 1 - step
        u0, u1, u2 = nested[l], nested[LEV + l], nested[2 * LEV + l]
        flocced = ((1.0 - a) * u0 + a * u1, b * u0 + (1.0 - a - b) * u1 + a * u2, b * u1 + (1.0 - b) * u2)
        columns = list(columns)
        for cls in range(NCLS):
            c = cls * LEV + l
            rate = rates[cls]
            w = wet * ((1.0 - rate) * flocced[cls] + rate * below[cls])
            f = spread * w
            wets[c] = w
            flux[c] = f
            for phase in range(2):
                sides[phase][pl.ds(c, 1), :] = jnp.where(row_far[phase], f[cells_r - 1 :], f[:1])
            for phase in range(n_cols):
                far = col_far[phase]
                slab = jnp.where(far, f[:, cells_c - LANES :], f[:, :LANES])
                turn = lax.rem(c - jnp.where(far, LANES - 1, 0) + LANES, LANES)
                columns[phase] = jnp.where(lane == c, pltpu.roll(slab, turn, 1), columns[phase])
        return flocced, tuple(columns)

    nothing = jnp.zeros((cells_r, cells_c), jnp.float32)
    empty = jnp.zeros((cells_r, LANES), jnp.float32)
    _, columns = lax.fori_loop(0, LEV, level, ((nothing,) * NCLS, (empty,) * n_cols), unroll=True)
    for phase in range(n_cols):
        sides[2 + phase][...] = columns[phase]


def spread_kernel(last, wets, flux, *rest):
    bulk = rest[0].at[0] if last else rest[1]
    comps, cells_r, cells_c = bulk.shape
    grid, _, _ = place()
    row_id = lax.broadcasted_iota(jnp.int32, (cells_r, cells_c), 0)
    col_id = lax.broadcasted_iota(jnp.int32, (cells_r, cells_c), 1)

    def one(c, carry):
        f = flux[c]
        total = wets[c] - 4.0 * f
        total = total + jnp.where(row_id == 0, 0.0, pltpu.roll(f, 1, 0))
        total = total + jnp.where(row_id == cells_r - 1, 0.0, pltpu.roll(f, cells_r - 1, 0))
        total = total + jnp.where(col_id == 0, 0.0, pltpu.roll(f, 1, 1))
        total = total + jnp.where(col_id == cells_c - 1, 0.0, pltpu.roll(f, cells_c - 1, 1))
        bulk[c] = total
        return carry

    lax.fori_loop(0, comps, one, 0, unroll=2)
    if not last:
        sponge, _, folded, rows, fine = rest

        @pl.when(grid > 0)
        def _():
            folded[...] = fold(bulk, sponge, rows, fine)


def halo_kernel(n_cols, sizes, last, *rest):
    plan, rest = (None, rest) if last else (rest[0], rest[1:])
    bulk, rest = rest[0], rest[1:]
    given, rest = ((), rest) if last else (rest[:2], rest[2:])
    sides, state, rest = rest[: 2 + n_cols], rest[2 + n_cols], rest[3 + n_cols :]
    old, new = (bulk.at[0], state.at[0]) if last else (bulk, state)
    comps, cells_r, cells_c = new.shape
    grid, i, j = place()
    row = lax.broadcasted_iota(jnp.int32, (8, cells_c), 0)
    even, _ = edge_sides(i)
    second, first = sides[0][...], sides[1][...]
    above = jnp.where(i == 0, 0.0, jnp.where(even, second, first))
    below = jnp.where(i == sizes[0] - 1, 0.0, jnp.where(even, first, second))
    low = high = jnp.zeros((cells_r, LANES), jnp.float32)
    for phase, far in zip(range(n_cols), edge_sides(j)):
        column = sides[2 + phase][...]
        low = low + jnp.where(jnp.logical_not(far) & (j > 0), column, 0.0)
        high = high + jnp.where(far & (j < sizes[1] - 1), column, 0.0)
    for c in range(comps):
        new[c, :8, :] = old[c, :8, :] + jnp.where(row == 0, above[c : c + 1], 0.0)
        new[c, 8 : cells_r - 8, :] = old[c, 8 : cells_r - 8, :]
        new[c, cells_r - 8 :, :] = old[c, cells_r - 8 :, :] + jnp.where(row == 7, below[c : c + 1], 0.0)
    lane = lax.broadcasted_iota(jnp.int32, (cells_r, LANES), 1)

    @pl.when(j < sizes[1] - 1)
    def _():
        for c in range(comps):
            new[c, :, cells_c - LANES :] += jnp.where(lane == LANES - 1, pltpu.roll(high, LANES - 1 - c, 1), 0.0)

    @pl.when(j > 0)
    def _():
        for c in range(comps):
            new[c, :, :LANES] += jnp.where(lane == 0, pltpu.roll(low, (LANES - c) % LANES, 1), 0.0)

    if last:
        return
    sponge, folded = given
    outs, (packed, fine) = rest[: 2 * SLOTS], rest[2 * SLOTS :]

    @pl.when(grid == 0)
    def _():
        for slot, kind, serves, start, begin in pieces(plan):

            @pl.when(serves)
            def _():
                crop(new, outs[ORDER.index((slot, kind))], start, begin)

    @pl.when(grid > 0)
    def _():
        pack_fold(packed, comps, above, below, low, high, sponge, fine)

    for slot in range(SLOTS):

        @pl.when(grid == slot + 1)
        def _():
            patch(folded, packed, [outs[ORDER.index((slot, kind))] for kind in range(2)])


def exchange(blocks):
    n_x = lax.axis_size("gx")
    got = []
    for (slot, kind), block in zip(ORDER, blocks):
        pairs = []
        for i in range(n_x):
            parent, child = i, (slot + 1) * n_x + (i ^ kind)
            pairs += [(parent, child), (child, parent)]
        got.append(lax.ppermute(block, ("grid", "gx"), pairs))
    return got


def swap_pairs(size, phase):
    pairs = []
    for k in range(phase, size + phase, 2):
        first, second = k % size, (k + 1) % size
        pairs += [(first, second), (second, first)]
    return pairs


def local(adjoint, sea_mask, diffusivity, aggregation, breakup, sponge, settling, partner_flip, row_offset, col_offset):
    comps, cells_r, cells_c = adjoint.shape[1:]
    half_r, half_c = cells_r // 2, cells_c // 2
    n_x, n_y = lax.axis_size("gx"), lax.axis_size("gy")
    n_cols = 1 if n_y == 2 else 2
    f32 = jnp.float32
    tile = jax.ShapeDtypeStruct((comps, cells_r, cells_c), f32)
    block = jax.ShapeDtypeStruct((comps, half_r, half_c), f32)
    side = [jax.ShapeDtypeStruct((comps, cells_c), f32)] * 2 + [jax.ShapeDtypeStruct((cells_r, LANES), f32)] * n_cols
    fold_scratch = [pltpu.VMEM((comps, half_r, cells_c), f32), pltpu.VMEM((cells_c // LANES, cells_r, LANES), f32)]
    tables = [table.transpose(0, 2, 1) for table in (partner_flip, row_offset, col_offset)]

    *blocks, token = pl.pallas_call(
        first_kernel,
        out_shape=[block] * (2 * SLOTS) + [jax.ShapeDtypeStruct((8, LANES), f32)],
        in_specs=[pl.BlockSpec(memory_space=pltpu.HBM)] * 5,
        out_specs=[VM] * (2 * SLOTS + 1),
        scratch_shapes=fold_scratch
        + [pltpu.SMEM(table.shape, table.dtype) for table in tables]
        + [pltpu.VMEM(adjoint.shape, f32), pltpu.VMEM(sponge.shape, f32), pltpu.SemaphoreType.DMA((5,))],
        compiler_params=pltpu.CompilerParams(vmem_limit_bytes=60 * 2**20),
        name="first_payload",
    )(*tables, adjoint, sponge)
    fields = (adjoint, sponge, aggregation, breakup, sea_mask, diffusivity)
    state, sponge, *fields, rates, plan = pl.pallas_call(
        stage_kernel,
        out_shape=[jax.ShapeDtypeStruct(field.shape, field.dtype) for field in fields]
        + [jax.ShapeDtypeStruct((NCLS, 1, cells_c), f32), jax.ShapeDtypeStruct((6 * SLOTS + 1,), jnp.int32)],
        in_specs=[VM] + [pl.BlockSpec(memory_space=pltpu.HBM)] * 10,
        out_specs=[VM] * 7 + [SM],
        scratch_shapes=[pltpu.SMEM(settling.shape, f32)]
        + [pltpu.SMEM(table.shape, table.dtype) for table in tables]
        + [pltpu.SemaphoreType.DMA((10,))],
        compiler_params=PARAMS,
        name="stage_fields",
    )(token, *fields, settling, *tables)
    state = state.reshape(tile.shape)
    fold_scratch = [pltpu.VMEM((comps, half_r, cells_c), f32), pltpu.VMEM((cells_c // LANES, cells_r, LANES), f32)]
    for step in range(STEPS):
        last = step == STEPS - 1
        new = jax.ShapeDtypeStruct(adjoint.shape, f32) if last else tile
        got = exchange(blocks)
        wets, flux, *sides = pl.pallas_call(
            functools.partial(update_kernel, n_cols),
            out_shape=[tile] * 2 + side,
            in_specs=[SM] + [VM] * (7 + 2 * SLOTS),
            out_specs=[VM] * (2 + len(side)),
            scratch_shapes=[
                pltpu.VMEM(tile.shape, f32),
                pltpu.VMEM((comps, half_r, cells_c), f32),
                pltpu.VMEM(block.shape, f32),
                pltpu.VMEM((cells_c // LANES, cells_r, LANES), f32),
            ],
            compiler_params=PARAMS,
            name="update",
        )(plan, rates, state, sponge, *fields, *got)
        sides = [lax.ppermute(sides[k], "gx", swap_pairs(n_x, 1 - k)) for k in range(2)] + [
            lax.ppermute(sides[2 + k], "gy", swap_pairs(n_y, k)) for k in range(n_cols)
        ]
        bulk, *folded = pl.pallas_call(
            functools.partial(spread_kernel, last),
            out_shape=[new] + ([] if last else [block]),
            in_specs=[VM] * (2 if last else 3),
            out_specs=[VM] * (1 if last else 2),
            scratch_shapes=[] if last else fold_scratch,
            compiler_params=PARAMS,
            name="spread_last" if last else "spread",
        )(wets, flux, *([] if last else [sponge]))
        state, *blocks = pl.pallas_call(
            functools.partial(halo_kernel, n_cols, (n_x, n_y), last),
            out_shape=[new] + ([] if last else [block] * (2 * SLOTS)),
            in_specs=[SM] * (0 if last else 1) + [VM] * (1 + len(side) + (0 if last else 2)),
            out_specs=[VM] * (1 if last else 1 + 2 * SLOTS),
            scratch_shapes=[] if last else [pltpu.VMEM((2 * comps + 2 * half_r, half_c), f32), fold_scratch[1]],
            compiler_params=PARAMS,
            name="halo_last" if last else "halo",
        )(*([] if last else [plan]), bulk, *([] if last else [sponge, *folded]), *sides)
    return state


def solution(mesh):
    in_specs = (
        P("grid", None, "gx", "gy"),
        P("grid", "gx", "gy"),
        P("grid", "gx", "gy"),
        P("grid", "gx", "gy"),
        P("grid", "gx", "gy"),
        P("grid", "gx", "gy"),
        P(),
        P(),
        P(),
        P(),
    )
    out_specs = P("grid", None, "gx", "gy")
    return jax.shard_map(local, mesh=mesh, in_specs=in_specs, out_specs=out_specs, check_vma=False)
```

```python
import functools

import jax
import jax.numpy as jnp
from jax import lax
from jax.experimental import pallas as pl
from jax.experimental.pallas import tpu as pltpu
from jax.sharding import PartitionSpec as P

NCLS = 3
LEV = 8
STEPS = 2
SLOTS = 3
LANES = 128
CHUNK = 8

relaxation = 0.125

VM = pl.BlockSpec(memory_space=pltpu.VMEM)
SM = pl.BlockSpec(memory_space=pltpu.SMEM)
PARAMS = pltpu.CompilerParams(vmem_limit_bytes=16 * 2**20)


def place():
    return lax.axis_index("grid"), lax.axis_index("gx"), lax.axis_index("gy")


TURNED = 2
FORWARDED = 0
EARLY = ((FORWARDED, 0), (TURNED, 1))
LATE = ((0, 1), (2, 1), (1, 0), (1, 1), (2, 0))
GOT = (EARLY[0],) + LATE


def pieces_of(flip, top, left):
    _, i, j = place()
    for slot in range(SLOTS):
        for kind, row in ((0, i), (1, jnp.bitwise_xor(i, 1))):
            yield slot, kind, flip[slot, j, row] == kind, top[slot, j, row], left[slot, j, row]


def pieces(plan):
    for k in range(2 * SLOTS):
        yield k // 2, k % 2, plan[3 * k] == 1, plan[3 * k + 1], plan[3 * k + 2]


def widen(half, cells):
    row = lax.broadcasted_iota(jnp.int32, (half, cells), 0)
    col = lax.broadcasted_iota(jnp.int32, (half, cells), 1)
    return (lax.shift_right_logical(col, 1) == row).astype(jnp.float32)


def narrow(cells, half):
    row = lax.broadcasted_iota(jnp.int32, (cells, half), 0)
    col = lax.broadcasted_iota(jnp.int32, (cells, half), 1)
    return (lax.shift_right_logical(row, 1) == col).astype(jnp.float32)


def near(first, half_r):
    base = jnp.minimum(lax.shift_right_logical(first, 3) * 8, half_r - 8)
    return pl.multiple_of(base, 8), first - base


def crop(source, out, first, begin):
    comps, cells_r, cells_c = source.shape
    half_r, half_c = out.shape[1:]
    groups = half_r // 8
    base, rest = near(first, half_r)
    row = lax.broadcasted_iota(jnp.int32, (8, half_c), 0)
    lane = lax.broadcasted_iota(jnp.int32, (8, half_c), 1)
    turn_c = lax.rem(2 * half_c - begin, half_c)
    turn_r = lax.rem(8 - rest, 8)
    left_part = lane < half_c - begin
    upper_part = row < 8 - rest
    for c in range(0, comps, CHUNK):
        block = source[c : c + CHUNK, pl.ds(base, half_r + 8), :].reshape(CHUNK * (groups + 1), 8, cells_c)
        low = pltpu.roll(block[..., :half_c], turn_c, 2)
        high = pltpu.roll(block[..., half_c:], turn_c, 2)
        block = pltpu.roll(jnp.where(left_part, low, high), turn_r, 1).reshape(CHUNK, groups + 1, 8, half_c)
        for k in range(groups):
            out[c : c + CHUNK, k * 8 : k * 8 + 8, :] = jnp.where(upper_part, block[:, k], block[:, k + 1])


def add_at(total, piece, first, begin):
    comps, half_r, half_c = piece.shape
    groups = half_r // 8
    base, rest = near(first, half_r)
    row = lax.broadcasted_iota(jnp.int32, (8, half_c), 0)
    lane = lax.broadcasted_iota(jnp.int32, (8, half_c), 1)
    turn_c = lax.rem(begin, half_c)
    turn_r = lax.rem(rest, 8)
    lower_part = row >= rest
    right_part = lane >= begin
    for c in range(0, comps, CHUNK):
        block = piece[c : c + CHUNK].reshape(CHUNK * groups, 8, half_c)
        block = pltpu.roll(block, turn_r, 1).reshape(CHUNK, groups, 8, half_c)
        none = jnp.zeros((CHUNK, 8, half_c), jnp.float32)
        for k in range(groups + 1):
            here = block[:, k] if k < groups else none
            above = block[:, k - 1] if k else none
            turned = pltpu.roll(jnp.where(lower_part, here, above), turn_c, 2)
            rows = pl.ds(base + k * 8, 8)
            total[c : c + CHUNK, rows, :half_c] += jnp.where(right_part, turned, 0.0)
            total[c : c + CHUNK, rows, half_c:] += jnp.where(right_part, 0.0, turned)


def fold(state, sponge, rows, fine):
    comps, cells_r, cells_c = state.shape
    half_r, half_c = cells_r // 2, cells_c // 2
    weight = sponge[0]

    def one(c, carry):
        block = weight * state[c]
        for k in range(cells_c // LANES):
            part = slice(k * LANES, (k + 1) * LANES)
            fine[k] = block[:, part]
            rows[c, :, part] = fine[k, pl.ds(0, half_r, 2), :] + fine[k, pl.ds(1, half_r, 2), :]
        return carry

    lax.fori_loop(0, comps, one, 0, unroll=4)
    return jnp.dot(
        rows[...].reshape(comps * half_r, cells_c),
        narrow(cells_c, half_c),
        precision=lax.Precision.HIGHEST,
        preferred_element_type=jnp.float32,
    ).reshape(comps, half_r, half_c)


def pack_fold(out, comps, above, below, low, high, sponge, fine):
    weight = sponge[0]
    cells_r, cells_c = weight.shape
    half_r, half_c = cells_r // 2, cells_c // 2
    lines = jnp.concatenate([weight[:1] * above, weight[cells_r - 1 :] * below], axis=0)
    out[: 2 * comps, :] = jnp.dot(
        lines, narrow(cells_c, half_c), precision=lax.Precision.HIGHEST, preferred_element_type=jnp.float32
    )
    for k, line in enumerate((weight[:, :1] * low, weight[:, cells_c - 1 :] * high)):
        fine[k] = line
        out[2 * comps + k * half_r : 2 * comps + (k + 1) * half_r, :] = (
            fine[k, pl.ds(0, half_r, 2), :] + fine[k, pl.ds(1, half_r, 2), :]
        )


def patch(block, extra, outs):
    comps, half_r, half_c = block.shape
    row = lax.broadcasted_iota(jnp.int32, (half_r, half_c), 0)
    lane = lax.broadcasted_iota(jnp.int32, (half_r, half_c), 1)
    low = extra[2 * comps : 2 * comps + half_r, :]
    high = extra[2 * comps + half_r : 2 * comps + 2 * half_r, :]
    for c in range(comps):
        total = block[c]
        total = total + jnp.where(row == 0, extra[c : c + 1, :], 0.0)
        total = total + jnp.where(row == half_r - 1, extra[comps + c : comps + c + 1, :], 0.0)
        total = total + jnp.where(lane == 0, pltpu.roll(low, (half_c - c) % half_c, 1), 0.0)
        total = total + jnp.where(lane == half_c - 1, pltpu.roll(high, half_c - 1 - c, 1), 0.0)
        for out in outs:
            out[c] = total


def first_kernel(*refs):
    given, early, mask, late, refs = refs[:5], refs[5:7], refs[7], refs[8:13], refs[13:]
    rows, fine, *held, done = refs
    copies = [pltpu.make_async_copy(source, to, done.at[k]) for k, (source, to) in enumerate(zip(given, held))]
    for copy in copies:
        copy.start()
    for copy in copies:
        copy.wait()
    *tables, state, sponge = held
    state = state.at[0]
    grid, _, _ = place()

    @pl.when(grid == 0)
    def _():
        table = list(pieces_of(*tables))
        crop_all(state, table, EARLY, early)
        crop_all(state, table, LATE, late)
        mark_turned(mask, table)

    @pl.when(grid > 0)
    def _():
        mask[...] = jnp.zeros_like(mask)
        block = fold(state, sponge, rows, fine)
        for slot in range(SLOTS):

            @pl.when(grid == slot + 1)
            def _():
                for out in child_outs(slot, early, late):
                    out[...] = block


def stage_kernel(token, *refs):
    given, held, (rates, plan), scratch = refs[:10], list(refs[10:16]), refs[16:18], refs[18:]
    speeds, *tables, done = scratch
    copies = [
        pltpu.make_async_copy(source, to, done.at[k])
        for k, (source, to) in enumerate(zip(given, held + [speeds] + tables))
    ]
    for copy in copies:
        copy.start()
    for copy in copies:
        copy.wait()
    grid, i, j = place()
    for cls in range(NCLS):
        rates[cls] = jnp.full(rates.shape[1:], speeds[grid, cls], jnp.float32)
    for k, (_, _, serves, first, begin) in enumerate(pieces_of(*tables)):
        plan[3 * k] = serves.astype(jnp.int32)
        plan[3 * k + 1] = first
        plan[3 * k + 2] = begin
    plan[6 * SLOTS] = tables[0][jnp.maximum(grid - 1, 0), j, i]


def edge_sides(index):
    even = lax.rem(index, 2) == 0
    return even, jnp.logical_not(even)


def update_kernel(n_cols, plan, rates, state, sponge, agg, brk, mask, diff, *rest):
    got, rest = rest[: 2 * SLOTS + 1], rest[2 * SLOTS + 1 :]
    wets, flux, sides = rest[0], rest[1], rest[2 : 4 + n_cols]
    nested, wide, coarse, fine = rest[4 + n_cols :]
    comps, cells_r, cells_c = wets.shape
    half_r, half_c = cells_r // 2, cells_c // 2
    grid, i, j = place()
    row_id = lax.broadcasted_iota(jnp.int32, (cells_r, cells_c), 0)
    col_id = lax.broadcasted_iota(jnp.int32, (cells_r, cells_c), 1)

    @pl.when(grid == 0)
    def _():
        covered = jnp.zeros((cells_r, cells_c), jnp.float32)
        for _, _, serves, first, begin in pieces(plan):
            inside = (row_id >= first) & (row_id < first + half_r) & (col_id >= begin) & (col_id < begin + half_c)
            covered = covered + jnp.where(inside & serves, 1.0, 0.0)
        keep = 1.0 - relaxation * covered

        def own(step, carry):
            rows = pl.ds(step * CHUNK, CHUNK)
            nested[rows] = keep * state[rows]
            return carry

        lax.fori_loop(0, comps // CHUNK, own, 0)
        for slot, kind, serves, first, begin in pieces(plan):

            @pl.when(serves)
            def _():
                add_at(nested, got[-1 if (slot, kind) == (FORWARDED, 1) else GOT.index((slot, kind))], first, begin)

    @pl.when(grid > 0)
    def _():
        for slot in range(SLOTS):
            for kind in range(1 if slot == TURNED else 2):

                @pl.when((grid == slot + 1) & ((plan[6 * SLOTS] == kind) | (slot == TURNED)))
                def _():
                    coarse[...] = got[GOT.index((slot, kind))][...]

        wide[...] = jnp.dot(
            coarse[...].reshape(comps * half_r, half_c),
            widen(half_c, cells_c) * (relaxation / 4.0),
            precision=lax.Precision.HIGHEST,
            preferred_element_type=jnp.float32,
        ).reshape(comps, half_r, cells_c)
        keep = 1.0 - sponge[0]

        def own(c, carry):
            for k in range(cells_c // LANES):
                part = slice(k * LANES, (k + 1) * LANES)
                block = wide[c, :, part]
                fine[k, pl.ds(0, half_r, 2), :] = block
                fine[k, pl.ds(1, half_r, 2), :] = block
                nested[c, :, part] = keep[:, part] * state[c, :, part] + fine[k]
            return carry

        lax.fori_loop(0, comps, own, 0, unroll=4)

    a, b = agg[0], brk[0]
    wet = mask[0].astype(jnp.float32)
    spread = diff[0]
    row_far = edge_sides(i)[::-1]
    col_far = edge_sides(j)
    lane = lax.broadcasted_iota(jnp.int32, (cells_r, LANES), 1)

    def level(step, carry):
        below, columns = carry
        l = LEV - 1 - step
        u0, u1, u2 = nested[l], nested[LEV + l], nested[2 * LEV + l]
        flocced = ((1.0 - a) * u0 + a * u1, b * u0 + (1.0 - a - b) * u1 + a * u2, b * u1 + (1.0 - b) * u2)
        columns = list(columns)
        for cls in range(NCLS):
            c = cls * LEV + l
            rate = rates[cls]
            w = wet * ((1.0 - rate) * flocced[cls] + rate * below[cls])
            f = spread * w
            wets[c] = w
            flux[c] = f
            for phase in range(2):
                sides[phase][pl.ds(c, 1), :] = jnp.where(row_far[phase], f[cells_r - 1 :], f[:1])
            for phase in range(n_cols):
                far = col_far[phase]
                slab = jnp.where(far, f[:, cells_c - LANES :], f[:, :LANES])
                turn = lax.rem(c - jnp.where(far, LANES - 1, 0) + LANES, LANES)
                columns[phase] = jnp.where(lane == c, pltpu.roll(slab, turn, 1), columns[phase])
        return flocced, tuple(columns)

    nothing = jnp.zeros((cells_r, cells_c), jnp.float32)
    empty = jnp.zeros((cells_r, LANES), jnp.float32)
    _, columns = lax.fori_loop(0, LEV, level, ((nothing,) * NCLS, (empty,) * n_cols), unroll=True)
    for phase in range(n_cols):
        sides[2 + phase][...] = columns[phase]


def spread_kernel(last, wets, flux, *rest):
    bulk = rest[0].at[0] if last else rest[1]
    comps, cells_r, cells_c = bulk.shape
    grid, _, _ = place()
    row_id = lax.broadcasted_iota(jnp.int32, (cells_r, cells_c), 0)
    col_id = lax.broadcasted_iota(jnp.int32, (cells_r, cells_c), 1)

    def one(c, carry):
        f = flux[c]
        total = wets[c] - 4.0 * f
        total = total + jnp.where(row_id == 0, 0.0, pltpu.roll(f, 1, 0))
        total = total + jnp.where(row_id == cells_r - 1, 0.0, pltpu.roll(f, cells_r - 1, 0))
        total = total + jnp.where(col_id == 0, 0.0, pltpu.roll(f, 1, 1))
        total = total + jnp.where(col_id == cells_c - 1, 0.0, pltpu.roll(f, cells_c - 1, 1))
        bulk[c] = total
        return carry

    lax.fori_loop(0, comps, one, 0, unroll=2)
    if not last:
        sponge, _, folded, rows, fine = rest

        @pl.when(grid > 0)
        def _():
            folded[...] = fold(bulk, sponge, rows, fine)


def halo_kernel(n_cols, sizes, last, *rest):
    plan, rest = (None, rest) if last else (rest[0], rest[1:])
    bulk, rest = rest[0], rest[1:]
    given, rest = ((), rest) if last else (rest[:2], rest[2:])
    sides, state, rest = rest[: 2 + n_cols], rest[2 + n_cols], rest[3 + n_cols :]
    old, new = (bulk.at[0], state.at[0]) if last else (bulk, state)
    comps, cells_r, cells_c = new.shape
    grid, i, j = place()
    row = lax.broadcasted_iota(jnp.int32, (8, cells_c), 0)
    even, _ = edge_sides(i)
    second, first = sides[0][...], sides[1][...]
    above = jnp.where(i == 0, 0.0, jnp.where(even, second, first))
    below = jnp.where(i == sizes[0] - 1, 0.0, jnp.where(even, first, second))
    low = high = jnp.zeros((cells_r, LANES), jnp.float32)
    for phase, far in zip(range(n_cols), edge_sides(j)):
        column = sides[2 + phase][...]
        low = low + jnp.where(jnp.logical_not(far) & (j > 0), column, 0.0)
        high = high + jnp.where(far & (j < sizes[1] - 1), column, 0.0)
    for c in range(comps):
        new[c, :8, :] = old[c, :8, :] + jnp.where(row == 0, above[c : c + 1], 0.0)
        new[c, 8 : cells_r - 8, :] = old[c, 8 : cells_r - 8, :]
        new[c, cells_r - 8 :, :] = old[c, cells_r - 8 :, :] + jnp.where(row == 7, below[c : c + 1], 0.0)
    lane = lax.broadcasted_iota(jnp.int32, (cells_r, LANES), 1)

    @pl.when(j < sizes[1] - 1)
    def _():
        for c in range(comps):
            new[c, :, cells_c - LANES :] += jnp.where(lane == LANES - 1, pltpu.roll(high, LANES - 1 - c, 1), 0.0)

    @pl.when(j > 0)
    def _():
        for c in range(comps):
            new[c, :, :LANES] += jnp.where(lane == 0, pltpu.roll(low, (LANES - c) % LANES, 1), 0.0)

    if last:
        return
    sponge, folded = given
    early, mask, packed, fine = rest[:2], *rest[2:]

    @pl.when(grid == 0)
    def _():
        table = list(pieces(plan))
        crop_all(new, table, EARLY, early)
        mark_turned(mask, table)

    @pl.when(grid > 0)
    def _():
        mask[...] = jnp.zeros_like(mask)
        pack_fold(packed, comps, above, below, low, high, sponge, fine)

    @pl.when(grid == FORWARDED + 1)
    def _():
        patch(folded, packed, child_outs(FORWARDED, early, ()))


def crop_all(state, table, order, outs):
    for slot, kind, serves, first, begin in table:
        if (slot, kind) in order and ((slot, kind) != (TURNED, 1) or order is EARLY):

            @pl.when(serves)
            def _():
                crop(state, outs[order.index((slot, kind))], first, begin)


def mark_turned(mask, table):
    for slot, kind, serves, _, _ in table:
        if (slot, kind) == (TURNED, 0):
            mask[...] = jnp.full(mask.shape, jnp.where(serves, 0.0, 1.0), jnp.float32)


def child_outs(slot, early, late):
    if slot == FORWARDED:
        return [early[0]]
    return [late[LATE.index((slot, kind))] for kind in range(2)]


def late_kernel(plan, state, folded, packed, *outs):
    grid, _, _ = place()

    @pl.when(grid == 0)
    def _():
        crop_all(state, list(pieces(plan)), LATE, outs)

    for slot in range(SLOTS):
        if slot != FORWARDED:

            @pl.when(grid == slot + 1)
            def _():
                patch(folded, packed, child_outs(slot, (), outs))


def merge_kernel(mask, own, other, out):
    out[...] = jnp.where(mask[:1, :] > 0.5, other[...], own[...])


def between_parents(block):
    return lax.ppermute(block, ("grid", "gx"), [(i, i ^ 1) for i in range(lax.axis_size("gx"))])


def with_children(block, slot, kind, down=True, up=True):
    n_x = lax.axis_size("gx")
    pairs = []
    for i in range(n_x):
        parent, child = i, (slot + 1) * n_x + (i ^ kind)
        pairs += [(parent, child)] * down + [(child, parent)] * up
    return lax.ppermute(block, ("grid", "gx"), pairs)


def exchange(early, mask, late):
    blocks = dict(zip(LATE, late))
    blocks[EARLY[0]] = early[0]
    other = between_parents(early[1])
    own = blocks[TURNED, 0]
    blocks[TURNED, 0] = pl.pallas_call(
        merge_kernel,
        out_shape=jax.ShapeDtypeStruct(own.shape, own.dtype),
        in_specs=[VM] * 3,
        out_specs=VM,
        compiler_params=PARAMS,
        name="merge",
    )(mask, own, other)
    got = [
        with_children(blocks[slot, kind], slot, kind, up=(slot, kind) != (FORWARDED, 1), down=(slot, kind) != (TURNED, 1))
        for slot, kind in GOT
    ]
    forward, got[3] = lax.optimization_barrier((got[0], got[3]))
    return got + [between_parents(forward)]


def swap_pairs(size, phase):
    pairs = []
    for k in range(phase, size + phase, 2):
        first, second = k % size, (k + 1) % size
        pairs += [(first, second), (second, first)]
    return pairs


def local(adjoint, sea_mask, diffusivity, aggregation, breakup, sponge, settling, partner_flip, row_offset, col_offset):
    comps, cells_r, cells_c = adjoint.shape[1:]
    half_r, half_c = cells_r // 2, cells_c // 2
    n_x, n_y = lax.axis_size("gx"), lax.axis_size("gy")
    n_cols = 1 if n_y == 2 else 2
    f32 = jnp.float32
    tile = jax.ShapeDtypeStruct((comps, cells_r, cells_c), f32)
    block = jax.ShapeDtypeStruct((comps, half_r, half_c), f32)
    side = [jax.ShapeDtypeStruct((comps, cells_c), f32)] * 2 + [jax.ShapeDtypeStruct((cells_r, LANES), f32)] * n_cols
    fold_scratch = [pltpu.VMEM((comps, half_r, cells_c), f32), pltpu.VMEM((cells_c // LANES, cells_r, LANES), f32)]
    tables = [table.transpose(0, 2, 1) for table in (partner_flip, row_offset, col_offset)]

    flag = jax.ShapeDtypeStruct((8, half_c), f32)
    blocks = pl.pallas_call(
        first_kernel,
        out_shape=[block] * 2 + [flag] + [block] * 5,
        in_specs=[pl.BlockSpec(memory_space=pltpu.HBM)] * 5,
        out_specs=[VM] * 8,
        scratch_shapes=fold_scratch
        + [pltpu.SMEM(table.shape, table.dtype) for table in tables]
        + [pltpu.VMEM(adjoint.shape, f32), pltpu.VMEM(sponge.shape, f32), pltpu.SemaphoreType.DMA((5,))],
        compiler_params=pltpu.CompilerParams(vmem_limit_bytes=60 * 2**20),
        name="first_payload",
    )(*tables, adjoint, sponge)
    early, mask, late = blocks[:2], blocks[2], blocks[3:]
    fields = (adjoint, sponge, aggregation, breakup, sea_mask, diffusivity)
    state, sponge, *fields, rates, plan = pl.pallas_call(
        stage_kernel,
        out_shape=[jax.ShapeDtypeStruct(field.shape, field.dtype) for field in fields]
        + [jax.ShapeDtypeStruct((NCLS, 1, cells_c), f32), jax.ShapeDtypeStruct((6 * SLOTS + 1,), jnp.int32)],
        in_specs=[VM] + [pl.BlockSpec(memory_space=pltpu.HBM)] * 10,
        out_specs=[VM] * 7 + [SM],
        scratch_shapes=[pltpu.SMEM(settling.shape, f32)]
        + [pltpu.SMEM(table.shape, table.dtype) for table in tables]
        + [pltpu.SemaphoreType.DMA((10,))],
        compiler_params=PARAMS,
        name="stage_fields",
    )(mask, *fields, settling, *tables)
    state = state.reshape(tile.shape)
    fold_scratch = [pltpu.VMEM((comps, half_r, cells_c), f32), pltpu.VMEM((cells_c // LANES, cells_r, LANES), f32)]
    for step in range(STEPS):
        last = step == STEPS - 1
        new = jax.ShapeDtypeStruct(adjoint.shape, f32) if last else tile
        got = exchange(early, mask, late)
        wets, flux, *sides = pl.pallas_call(
            functools.partial(update_kernel, n_cols),
            out_shape=[tile] * 2 + side,
            in_specs=[SM] + [VM] * (8 + 2 * SLOTS),
            out_specs=[VM] * (2 + len(side)),
            scratch_shapes=[
                pltpu.VMEM(tile.shape, f32),
                pltpu.VMEM((comps, half_r, cells_c), f32),
                pltpu.VMEM(block.shape, f32),
                pltpu.VMEM((cells_c // LANES, cells_r, LANES), f32),
            ],
            compiler_params=PARAMS,
            name="update",
        )(plan, rates, state, sponge, *fields, *got)
        sides = [lax.ppermute(sides[k], "gx", swap_pairs(n_x, 1 - k)) for k in range(2)] + [
            lax.ppermute(sides[2 + k], "gy", swap_pairs(n_y, k)) for k in range(n_cols)
        ]
        bulk, *folded = pl.pallas_call(
            functools.partial(spread_kernel, last),
            out_shape=[new] + ([] if last else [block]),
            in_specs=[VM] * (2 if last else 3),
            out_specs=[VM] * (1 if last else 2),
            scratch_shapes=[] if last else fold_scratch,
            compiler_params=PARAMS,
            name="spread_last" if last else "spread",
        )(wets, flux, *([] if last else [sponge]))
        extra = jax.ShapeDtypeStruct((2 * comps + 2 * half_r, half_c), f32)
        extra = jax.ShapeDtypeStruct((2 * comps + 2 * half_r, half_c), f32)
        state, *out = pl.pallas_call(
            functools.partial(halo_kernel, n_cols, (n_x, n_y), last),
            out_shape=[new] + ([] if last else [block] * 2 + [flag, extra]),
            in_specs=[SM] * (0 if last else 1) + [VM] * (1 + len(side) + (0 if last else 2)),
            out_specs=[VM] * (1 if last else 5),
            scratch_shapes=[] if last else fold_scratch[1:],
            compiler_params=PARAMS,
            name="halo_last" if last else "halo",
        )(*([] if last else [plan]), bulk, *([] if last else [sponge, *folded]), *sides)
        if not last:
            early, mask, packed = out[:2], out[2], out[3]
            late = pl.pallas_call(
                late_kernel,
                out_shape=[block] * 5,
                in_specs=[SM] + [VM] * 3,
                out_specs=[VM] * 5,
                compiler_params=PARAMS,
                name="late_payload",
            )(plan, state, *folded, packed)
    return state


def solution(mesh):
    in_specs = (
        P("grid", None, "gx", "gy"),
        P("grid", "gx", "gy"),
        P("grid", "gx", "gy"),
        P("grid", "gx", "gy"),
        P("grid", "gx", "gy"),
        P("grid", "gx", "gy"),
        P(),
        P(),
        P(),
        P(),
    )
    out_specs = P("grid", None, "gx", "gy")
    return jax.shard_map(local, mesh=mesh, in_specs=in_specs, out_specs=out_specs, check_vma=False)
```

```python
import functools

import jax
import jax.numpy as jnp
from jax import lax
from jax.experimental import pallas as pl
from jax.experimental.pallas import tpu as pltpu
from jax.sharding import PartitionSpec as P

NCLS = 3
LEV = 8
STEPS = 2
SLOTS = 3
LANES = 128
CHUNK = 8

relaxation = 0.125

VM = pl.BlockSpec(memory_space=pltpu.VMEM)
SM = pl.BlockSpec(memory_space=pltpu.SMEM)
PARAMS = pltpu.CompilerParams(vmem_limit_bytes=16 * 2**20)


def place():
    return lax.axis_index("grid"), lax.axis_index("gx"), lax.axis_index("gy")


TURNED = 2
FORWARDED = 0
EARLY = ((FORWARDED, 0), (TURNED, 1))
LATE = ((1, 0), (2, 1), (0, 1), (1, 1), (2, 0))
GOT = (EARLY[0],) + LATE


def pieces_of(flip, top, left):
    _, i, j = place()
    for slot in range(SLOTS):
        for kind, row in ((0, i), (1, jnp.bitwise_xor(i, 1))):
            yield slot, kind, flip[slot, j, row] == kind, top[slot, j, row], left[slot, j, row]


def pieces(plan):
    for k in range(2 * SLOTS):
        yield k // 2, k % 2, plan[3 * k] == 1, plan[3 * k + 1], plan[3 * k + 2]


def widen(half, cells):
    row = lax.broadcasted_iota(jnp.int32, (half, cells), 0)
    col = lax.broadcasted_iota(jnp.int32, (half, cells), 1)
    return (lax.shift_right_logical(col, 1) == row).astype(jnp.float32)


def narrow(cells, half):
    row = lax.broadcasted_iota(jnp.int32, (cells, half), 0)
    col = lax.broadcasted_iota(jnp.int32, (cells, half), 1)
    return (lax.shift_right_logical(row, 1) == col).astype(jnp.float32)


def near(first, half_r):
    base = jnp.minimum(lax.shift_right_logical(first, 3) * 8, half_r - 8)
    return pl.multiple_of(base, 8), first - base


def crop(source, out, first, begin):
    comps, cells_r, cells_c = source.shape
    half_r, half_c = out.shape[1:]
    groups = half_r // 8
    base, rest = near(first, half_r)
    row = lax.broadcasted_iota(jnp.int32, (8, half_c), 0)
    lane = lax.broadcasted_iota(jnp.int32, (8, half_c), 1)
    turn_c = lax.rem(2 * half_c - begin, half_c)
    turn_r = lax.rem(8 - rest, 8)
    left_part = lane < half_c - begin
    upper_part = row < 8 - rest
    for c in range(0, comps, CHUNK):
        block = source[c : c + CHUNK, pl.ds(base, half_r + 8), :].reshape(CHUNK * (groups + 1), 8, cells_c)
        low = pltpu.roll(block[..., :half_c], turn_c, 2)
        high = pltpu.roll(block[..., half_c:], turn_c, 2)
        block = pltpu.roll(jnp.where(left_part, low, high), turn_r, 1).reshape(CHUNK, groups + 1, 8, half_c)
        for k in range(groups):
            out[c : c + CHUNK, k * 8 : k * 8 + 8, :] = jnp.where(upper_part, block[:, k], block[:, k + 1])


def add_at(total, piece, first, begin):
    comps, half_r, half_c = piece.shape
    groups = half_r // 8
    base, rest = near(first, half_r)
    row = lax.broadcasted_iota(jnp.int32, (8, half_c), 0)
    lane = lax.broadcasted_iota(jnp.int32, (8, half_c), 1)
    turn_c = lax.rem(begin, half_c)
    turn_r = lax.rem(rest, 8)
    lower_part = row >= rest
    right_part = lane >= begin
    for c in range(0, comps, CHUNK):
        block = piece[c : c + CHUNK].reshape(CHUNK * groups, 8, half_c)
        block = pltpu.roll(block, turn_r, 1).reshape(CHUNK, groups, 8, half_c)
        none = jnp.zeros((CHUNK, 8, half_c), jnp.float32)
        for k in range(groups + 1):
            here = block[:, k] if k < groups else none
            above = block[:, k - 1] if k else none
            turned = pltpu.roll(jnp.where(lower_part, here, above), turn_c, 2)
            rows = pl.ds(base + k * 8, 8)
            total[c : c + CHUNK, rows, :half_c] += jnp.where(right_part, turned, 0.0)
            total[c : c + CHUNK, rows, half_c:] += jnp.where(right_part, 0.0, turned)


def fold(state, sponge, rows, fine):
    comps, cells_r, cells_c = state.shape
    half_r, half_c = cells_r // 2, cells_c // 2
    weight = sponge[0]

    def one(c, carry):
        block = weight * state[c]
        for k in range(cells_c // LANES):
            part = slice(k * LANES, (k + 1) * LANES)
            fine[k] = block[:, part]
            rows[c, :, part] = fine[k, pl.ds(0, half_r, 2), :] + fine[k, pl.ds(1, half_r, 2), :]
        return carry

    lax.fori_loop(0, comps, one, 0, unroll=4)
    return jnp.dot(
        rows[...].reshape(comps * half_r, cells_c),
        narrow(cells_c, half_c),
        precision=lax.Precision.HIGHEST,
        preferred_element_type=jnp.float32,
    ).reshape(comps, half_r, half_c)


def pack_fold(out, comps, above, below, low, high, sponge, fine):
    weight = sponge[0]
    cells_r, cells_c = weight.shape
    half_r, half_c = cells_r // 2, cells_c // 2
    lines = jnp.concatenate([weight[:1] * above, weight[cells_r - 1 :] * below], axis=0)
    out[: 2 * comps, :] = jnp.dot(
        lines, narrow(cells_c, half_c), precision=lax.Precision.HIGHEST, preferred_element_type=jnp.float32
    )
    for k, line in enumerate((weight[:, :1] * low, weight[:, cells_c - 1 :] * high)):
        fine[k] = line
        out[2 * comps + k * half_r : 2 * comps + (k + 1) * half_r, :] = (
            fine[k, pl.ds(0, half_r, 2), :] + fine[k, pl.ds(1, half_r, 2), :]
        )


def patch(block, extra, outs):
    comps, half_r, half_c = block.shape
    row = lax.broadcasted_iota(jnp.int32, (half_r, half_c), 0)
    lane = lax.broadcasted_iota(jnp.int32, (half_r, half_c), 1)
    low = extra[2 * comps : 2 * comps + half_r, :]
    high = extra[2 * comps + half_r : 2 * comps + 2 * half_r, :]
    for c in range(comps):
        total = block[c]
        total = total + jnp.where(row == 0, extra[c : c + 1, :], 0.0)
        total = total + jnp.where(row == half_r - 1, extra[comps + c : comps + c + 1, :], 0.0)
        total = total + jnp.where(lane == 0, pltpu.roll(low, (half_c - c) % half_c, 1), 0.0)
        total = total + jnp.where(lane == half_c - 1, pltpu.roll(high, half_c - 1 - c, 1), 0.0)
        for out in outs:
            out[c] = total


def first_kernel(*refs):
    given, early, mask, late, refs = refs[:5], refs[5:7], refs[7], refs[8:13], refs[13:]
    rows, fine, *held, done = refs
    copies = [pltpu.make_async_copy(source, to, done.at[k]) for k, (source, to) in enumerate(zip(given, held))]
    for copy in copies:
        copy.start()
    for copy in copies:
        copy.wait()
    *tables, state, sponge = held
    state = state.at[0]
    grid, _, _ = place()

    @pl.when(grid == 0)
    def _():
        table = list(pieces_of(*tables))
        crop_all(state, table, EARLY, early)
        crop_all(state, table, LATE, late)
        mark_turned(mask, table)

    @pl.when(grid > 0)
    def _():
        mask[...] = jnp.zeros_like(mask)
        block = fold(state, sponge, rows, fine)
        for slot in range(SLOTS):

            @pl.when(grid == slot + 1)
            def _():
                for out in child_outs(slot, early, late):
                    out[...] = block


def stage_kernel(token, *refs):
    given, held, (rates, plan), scratch = refs[:10], list(refs[10:16]), refs[16:18], refs[18:]
    speeds, *tables, done = scratch
    copies = [
        pltpu.make_async_copy(source, to, done.at[k])
        for k, (source, to) in enumerate(zip(given, held + [speeds] + tables))
    ]
    for copy in copies:
        copy.start()
    for copy in copies:
        copy.wait()
    grid, i, j = place()
    for cls in range(NCLS):
        rates[cls] = jnp.full(rates.shape[1:], speeds[grid, cls], jnp.float32)
    for k, (_, _, serves, first, begin) in enumerate(pieces_of(*tables)):
        plan[3 * k] = serves.astype(jnp.int32)
        plan[3 * k + 1] = first
        plan[3 * k + 2] = begin
    plan[6 * SLOTS] = tables[0][jnp.maximum(grid - 1, 0), j, i]


def edge_sides(index):
    even = lax.rem(index, 2) == 0
    return even, jnp.logical_not(even)


def update_kernel(n_cols, plan, rates, state, sponge, agg, brk, mask, diff, *rest):
    got, rest = rest[: 2 * SLOTS + 1], rest[2 * SLOTS + 1 :]
    wets, flux, sides = rest[0], rest[1], rest[2 : 4 + n_cols]
    nested, wide, coarse, fine = rest[4 + n_cols :]
    comps, cells_r, cells_c = wets.shape
    half_r, half_c = cells_r // 2, cells_c // 2
    grid, i, j = place()
    row_id = lax.broadcasted_iota(jnp.int32, (cells_r, cells_c), 0)
    col_id = lax.broadcasted_iota(jnp.int32, (cells_r, cells_c), 1)

    @pl.when(grid == 0)
    def _():
        covered = jnp.zeros((cells_r, cells_c), jnp.float32)
        for _, _, serves, first, begin in pieces(plan):
            inside = (row_id >= first) & (row_id < first + half_r) & (col_id >= begin) & (col_id < begin + half_c)
            covered = covered + jnp.where(inside & serves, 1.0, 0.0)
        keep = 1.0 - relaxation * covered

        def own(step, carry):
            rows = pl.ds(step * CHUNK, CHUNK)
            nested[rows] = keep * state[rows]
            return carry

        lax.fori_loop(0, comps // CHUNK, own, 0)
        for slot, kind, serves, first, begin in pieces(plan):

            @pl.when(serves)
            def _():
                add_at(nested, got[-1 if (slot, kind) == (FORWARDED, 1) else GOT.index((slot, kind))], first, begin)

    @pl.when(grid > 0)
    def _():
        for slot in range(SLOTS):
            for kind in range(1 if slot == TURNED else 2):

                @pl.when((grid == slot + 1) & ((plan[6 * SLOTS] == kind) | (slot == TURNED)))
                def _():
                    coarse[...] = got[GOT.index((slot, kind))][...]

        wide[...] = jnp.dot(
            coarse[...].reshape(comps * half_r, half_c),
            widen(half_c, cells_c) * (relaxation / 4.0),
            precision=lax.Precision.HIGHEST,
            preferred_element_type=jnp.float32,
        ).reshape(comps, half_r, cells_c)
        keep = 1.0 - sponge[0]

        def own(c, carry):
            for k in range(cells_c // LANES):
                part = slice(k * LANES, (k + 1) * LANES)
                block = wide[c, :, part]
                fine[k, pl.ds(0, half_r, 2), :] = block
                fine[k, pl.ds(1, half_r, 2), :] = block
                nested[c, :, part] = keep[:, part] * state[c, :, part] + fine[k]
            return carry

        lax.fori_loop(0, comps, own, 0, unroll=4)

    a, b = agg[0], brk[0]
    wet = mask[0].astype(jnp.float32)
    spread = diff[0]
    row_far = edge_sides(i)[::-1]
    col_far = edge_sides(j)
    lane = lax.broadcasted_iota(jnp.int32, (cells_r, LANES), 1)

    def level(step, carry):
        below, columns = carry
        l = LEV - 1 - step
        u0, u1, u2 = nested[l], nested[LEV + l], nested[2 * LEV + l]
        flocced = ((1.0 - a) * u0 + a * u1, b * u0 + (1.0 - a - b) * u1 + a * u2, b * u1 + (1.0 - b) * u2)
        columns = list(columns)
        for cls in range(NCLS):
            c = cls * LEV + l
            rate = rates[cls]
            w = wet * ((1.0 - rate) * flocced[cls] + rate * below[cls])
            f = spread * w
            wets[c] = w
            flux[c] = f
            for phase in range(2):
                sides[phase][pl.ds(c, 1), :] = jnp.where(row_far[phase], f[cells_r - 1 :], f[:1])
            for phase in range(n_cols):
                far = col_far[phase]
                slab = jnp.where(far, f[:, cells_c - LANES :], f[:, :LANES])
                turn = lax.rem(c - jnp.where(far, LANES - 1, 0) + LANES, LANES)
                columns[phase] = jnp.where(lane == c, pltpu.roll(slab, turn, 1), columns[phase])
        return flocced, tuple(columns)

    nothing = jnp.zeros((cells_r, cells_c), jnp.float32)
    empty = jnp.zeros((cells_r, LANES), jnp.float32)
    _, columns = lax.fori_loop(0, LEV, level, ((nothing,) * NCLS, (empty,) * n_cols), unroll=True)
    for phase in range(n_cols):
        sides[2 + phase][...] = columns[phase]


def spread_kernel(last, wets, flux, *rest):
    bulk = rest[0].at[0] if last else rest[1]
    comps, cells_r, cells_c = bulk.shape
    grid, _, _ = place()
    row_id = lax.broadcasted_iota(jnp.int32, (cells_r, cells_c), 0)
    col_id = lax.broadcasted_iota(jnp.int32, (cells_r, cells_c), 1)

    def one(c, carry):
        f = flux[c]
        total = wets[c] - 4.0 * f
        total = total + jnp.where(row_id == 0, 0.0, pltpu.roll(f, 1, 0))
        total = total + jnp.where(row_id == cells_r - 1, 0.0, pltpu.roll(f, cells_r - 1, 0))
        total = total + jnp.where(col_id == 0, 0.0, pltpu.roll(f, 1, 1))
        total = total + jnp.where(col_id == cells_c - 1, 0.0, pltpu.roll(f, cells_c - 1, 1))
        bulk[c] = total
        return carry

    lax.fori_loop(0, comps, one, 0, unroll=2)
    if not last:
        sponge, _, folded, rows, fine = rest

        @pl.when(grid > 0)
        def _():
            folded[...] = fold(bulk, sponge, rows, fine)


def halo_kernel(n_cols, sizes, last, *rest):
    plan, rest = (None, rest) if last else (rest[0], rest[1:])
    bulk, rest = rest[0], rest[1:]
    given, rest = ((), rest) if last else (rest[:2], rest[2:])
    sides, state, rest = rest[: 2 + n_cols], rest[2 + n_cols], rest[3 + n_cols :]
    old, new = (bulk.at[0], state.at[0]) if last else (bulk, state)
    comps, cells_r, cells_c = new.shape
    grid, i, j = place()
    row = lax.broadcasted_iota(jnp.int32, (8, cells_c), 0)
    even, _ = edge_sides(i)
    second, first = sides[0][...], sides[1][...]
    above = jnp.where(i == 0, 0.0, jnp.where(even, second, first))
    below = jnp.where(i == sizes[0] - 1, 0.0, jnp.where(even, first, second))
    low = high = jnp.zeros((cells_r, LANES), jnp.float32)
    for phase, far in zip(range(n_cols), edge_sides(j)):
        column = sides[2 + phase][...]
        low = low + jnp.where(jnp.logical_not(far) & (j > 0), column, 0.0)
        high = high + jnp.where(far & (j < sizes[1] - 1), column, 0.0)
    for c in range(comps):
        new[c, :8, :] = old[c, :8, :] + jnp.where(row == 0, above[c : c + 1], 0.0)
        new[c, 8 : cells_r - 8, :] = old[c, 8 : cells_r - 8, :]
        new[c, cells_r - 8 :, :] = old[c, cells_r - 8 :, :] + jnp.where(row == 7, below[c : c + 1], 0.0)
    lane = lax.broadcasted_iota(jnp.int32, (cells_r, LANES), 1)

    @pl.when(j < sizes[1] - 1)
    def _():
        for c in range(comps):
            new[c, :, cells_c - LANES :] += jnp.where(lane == LANES - 1, pltpu.roll(high, LANES - 1 - c, 1), 0.0)

    @pl.when(j > 0)
    def _():
        for c in range(comps):
            new[c, :, :LANES] += jnp.where(lane == 0, pltpu.roll(low, (LANES - c) % LANES, 1), 0.0)

    if last:
        return
    sponge, folded = given
    early, mask, packed, fine = rest[:2], *rest[2:]

    @pl.when(grid == 0)
    def _():
        table = list(pieces(plan))
        crop_all(new, table, EARLY, early)
        mark_turned(mask, table)

    @pl.when(grid > 0)
    def _():
        mask[...] = jnp.zeros_like(mask)
        pack_fold(packed, comps, above, below, low, high, sponge, fine)

    @pl.when(grid == FORWARDED + 1)
    def _():
        patch(folded, packed, child_outs(FORWARDED, early, ()))


def crop_all(state, table, order, outs):
    for slot, kind, serves, first, begin in table:
        if (slot, kind) in order and ((slot, kind) != (TURNED, 1) or order is EARLY):

            @pl.when(serves)
            def _():
                crop(state, outs[order.index((slot, kind))], first, begin)


def mark_turned(mask, table):
    for slot, kind, serves, _, _ in table:
        if (slot, kind) == (TURNED, 0):
            mask[...] = jnp.full(mask.shape, jnp.where(serves, 0.0, 1.0), jnp.float32)


def child_outs(slot, early, late):
    if slot == FORWARDED:
        return [early[0]]
    return [late[LATE.index((slot, kind))] for kind in range(2)]


def late_kernel(plan, state, folded, packed, *outs):
    grid, _, _ = place()

    @pl.when(grid == 0)
    def _():
        crop_all(state, list(pieces(plan)), LATE, outs)

    for slot in range(SLOTS):
        if slot != FORWARDED:

            @pl.when(grid == slot + 1)
            def _():
                patch(folded, packed, child_outs(slot, (), outs))


def merge_kernel(mask, own, other, out):
    out[...] = jnp.where(mask[:1, :] > 0.5, other[...], own[...])


def between_parents(block):
    return lax.ppermute(block, ("grid", "gx"), [(i, i ^ 1) for i in range(lax.axis_size("gx"))])


def with_children(block, slot, kind, down=True, up=True):
    n_x = lax.axis_size("gx")
    pairs = []
    for i in range(n_x):
        parent, child = i, (slot + 1) * n_x + (i ^ kind)
        pairs += [(parent, child)] * down + [(child, parent)] * up
    return lax.ppermute(block, ("grid", "gx"), pairs)


def exchange(early, mask, late):
    blocks = dict(zip(LATE, late))
    blocks[EARLY[0]] = early[0]
    other = between_parents(early[1])
    own = blocks[TURNED, 0]
    blocks[TURNED, 0] = pl.pallas_call(
        merge_kernel,
        out_shape=jax.ShapeDtypeStruct(own.shape, own.dtype),
        in_specs=[VM] * 3,
        out_specs=VM,
        compiler_params=PARAMS,
        name="merge",
    )(mask, own, other)
    got = [
        with_children(blocks[slot, kind], slot, kind, up=(slot, kind) != (FORWARDED, 1), down=(slot, kind) != (TURNED, 1))
        for slot, kind in GOT
    ]
    forward, got[1] = lax.optimization_barrier((got[0], got[1]))
    return got + [between_parents(forward)]


def swap_pairs(size, phase):
    pairs = []
    for k in range(phase, size + phase, 2):
        first, second = k % size, (k + 1) % size
        pairs += [(first, second), (second, first)]
    return pairs


def local(adjoint, sea_mask, diffusivity, aggregation, breakup, sponge, settling, partner_flip, row_offset, col_offset):
    comps, cells_r, cells_c = adjoint.shape[1:]
    half_r, half_c = cells_r // 2, cells_c // 2
    n_x, n_y = lax.axis_size("gx"), lax.axis_size("gy")
    n_cols = 1 if n_y == 2 else 2
    f32 = jnp.float32
    tile = jax.ShapeDtypeStruct((comps, cells_r, cells_c), f32)
    block = jax.ShapeDtypeStruct((comps, half_r, half_c), f32)
    side = [jax.ShapeDtypeStruct((comps, cells_c), f32)] * 2 + [jax.ShapeDtypeStruct((cells_r, LANES), f32)] * n_cols
    fold_scratch = [pltpu.VMEM((comps, half_r, cells_c), f32), pltpu.VMEM((cells_c // LANES, cells_r, LANES), f32)]
    tables = [table.transpose(0, 2, 1) for table in (partner_flip, row_offset, col_offset)]

    flag = jax.ShapeDtypeStruct((8, half_c), f32)
    blocks = pl.pallas_call(
        first_kernel,
        out_shape=[block] * 2 + [flag] + [block] * 5,
        in_specs=[pl.BlockSpec(memory_space=pltpu.HBM)] * 5,
        out_specs=[VM] * 8,
        scratch_shapes=fold_scratch
        + [pltpu.SMEM(table.shape, table.dtype) for table in tables]
        + [pltpu.VMEM(adjoint.shape, f32), pltpu.VMEM(sponge.shape, f32), pltpu.SemaphoreType.DMA((5,))],
        compiler_params=pltpu.CompilerParams(vmem_limit_bytes=60 * 2**20),
        name="first_payload",
    )(*tables, adjoint, sponge)
    early, mask, late = blocks[:2], blocks[2], blocks[3:]
    fields = (adjoint, sponge, aggregation, breakup, sea_mask, diffusivity)
    state, sponge, *fields, rates, plan = pl.pallas_call(
        stage_kernel,
        out_shape=[jax.ShapeDtypeStruct(field.shape, field.dtype) for field in fields]
        + [jax.ShapeDtypeStruct((NCLS, 1, cells_c), f32), jax.ShapeDtypeStruct((6 * SLOTS + 1,), jnp.int32)],
        in_specs=[VM] + [pl.BlockSpec(memory_space=pltpu.HBM)] * 10,
        out_specs=[VM] * 7 + [SM],
        scratch_shapes=[pltpu.SMEM(settling.shape, f32)]
        + [pltpu.SMEM(table.shape, table.dtype) for table in tables]
        + [pltpu.SemaphoreType.DMA((10,))],
        compiler_params=PARAMS,
        name="stage_fields",
    )(mask, *fields, settling, *tables)
    state = state.reshape(tile.shape)
    fold_scratch = [pltpu.VMEM((comps, half_r, cells_c), f32), pltpu.VMEM((cells_c // LANES, cells_r, LANES), f32)]
    for step in range(STEPS):
        last = step == STEPS - 1
        new = jax.ShapeDtypeStruct(adjoint.shape, f32) if last else tile
        got = exchange(early, mask, late)
        wets, flux, *sides = pl.pallas_call(
            functools.partial(update_kernel, n_cols),
            out_shape=[tile] * 2 + side,
            in_specs=[SM] + [VM] * (8 + 2 * SLOTS),
            out_specs=[VM] * (2 + len(side)),
            scratch_shapes=[
                pltpu.VMEM(tile.shape, f32),
                pltpu.VMEM((comps, half_r, cells_c), f32),
                pltpu.VMEM(block.shape, f32),
                pltpu.VMEM((cells_c // LANES, cells_r, LANES), f32),
            ],
            compiler_params=PARAMS,
            name="update",
        )(plan, rates, state, sponge, *fields, *got)
        sides = [lax.ppermute(sides[k], "gx", swap_pairs(n_x, 1 - k)) for k in range(2)] + [
            lax.ppermute(sides[2 + k], "gy", swap_pairs(n_y, k)) for k in range(n_cols)
        ]
        bulk, *folded = pl.pallas_call(
            functools.partial(spread_kernel, last),
            out_shape=[new] + ([] if last else [block]),
            in_specs=[VM] * (2 if last else 3),
            out_specs=[VM] * (1 if last else 2),
            scratch_shapes=[] if last else fold_scratch,
            compiler_params=PARAMS,
            name="spread_last" if last else "spread",
        )(wets, flux, *([] if last else [sponge]))
        extra = jax.ShapeDtypeStruct((2 * comps + 2 * half_r, half_c), f32)
        extra = jax.ShapeDtypeStruct((2 * comps + 2 * half_r, half_c), f32)
        state, *out = pl.pallas_call(
            functools.partial(halo_kernel, n_cols, (n_x, n_y), last),
            out_shape=[new] + ([] if last else [block] * 2 + [flag, extra]),
            in_specs=[SM] * (0 if last else 1) + [VM] * (1 + len(side) + (0 if last else 2)),
            out_specs=[VM] * (1 if last else 5),
            scratch_shapes=[] if last else fold_scratch[1:],
            compiler_params=PARAMS,
            name="halo_last" if last else "halo",
        )(*([] if last else [plan]), bulk, *([] if last else [sponge, *folded]), *sides)
        if not last:
            early, mask, packed = out[:2], out[2], out[3]
            late = pl.pallas_call(
                late_kernel,
                out_shape=[block] * 5,
                in_specs=[SM] + [VM] * 3,
                out_specs=[VM] * 5,
                compiler_params=PARAMS,
                name="late_payload",
            )(plan, state, *folded, packed)
    return state


def solution(mesh):
    in_specs = (
        P("grid", None, "gx", "gy"),
        P("grid", "gx", "gy"),
        P("grid", "gx", "gy"),
        P("grid", "gx", "gy"),
        P("grid", "gx", "gy"),
        P("grid", "gx", "gy"),
        P(),
        P(),
        P(),
        P(),
    )
    out_specs = P("grid", None, "gx", "gy")
    return jax.shard_map(local, mesh=mesh, in_specs=in_specs, out_specs=out_specs, check_vma=False)
```

```python
import functools

import jax
import jax.numpy as jnp
from jax import lax
from jax.experimental import pallas as pl
from jax.experimental.pallas import tpu as pltpu
from jax.sharding import PartitionSpec as P

NCLS = 3
LEV = 8
STEPS = 2
SLOTS = 3
LANES = 128
CHUNK = 8

relaxation = 0.125

VM = pl.BlockSpec(memory_space=pltpu.VMEM)
SM = pl.BlockSpec(memory_space=pltpu.SMEM)
PARAMS = pltpu.CompilerParams(vmem_limit_bytes=16 * 2**20)


def place():
    return lax.axis_index("grid"), lax.axis_index("gx"), lax.axis_index("gy")


TURNED = 2
FORWARDED = 0
EARLY = ((FORWARDED, 0), (TURNED, 1))
MIXED = (FORWARDED, 1)
LATE = ((1, 0), MIXED, (1, 1), (2, 0))
GOT = (EARLY[0],) + LATE


def pieces_of(flip, top, left):
    _, i, j = place()
    for slot in range(SLOTS):
        for kind, row in ((0, i), (1, jnp.bitwise_xor(i, 1))):
            yield slot, kind, flip[slot, j, row] == kind, top[slot, j, row], left[slot, j, row]


def pieces(plan):
    for k in range(2 * SLOTS):
        yield k // 2, k % 2, plan[3 * k] == 1, plan[3 * k + 1], plan[3 * k + 2]


def widen(half, cells):
    row = lax.broadcasted_iota(jnp.int32, (half, cells), 0)
    col = lax.broadcasted_iota(jnp.int32, (half, cells), 1)
    return (lax.shift_right_logical(col, 1) == row).astype(jnp.float32)


def narrow(cells, half):
    row = lax.broadcasted_iota(jnp.int32, (cells, half), 0)
    col = lax.broadcasted_iota(jnp.int32, (cells, half), 1)
    return (lax.shift_right_logical(row, 1) == col).astype(jnp.float32)


def near(first, half_r):
    base = jnp.minimum(lax.shift_right_logical(first, 3) * 8, half_r - 8)
    return pl.multiple_of(base, 8), first - base


def crop(source, out, first, begin):
    comps, cells_r, cells_c = source.shape
    half_r, half_c = out.shape[1:]
    groups = half_r // 8
    base, rest = near(first, half_r)
    row = lax.broadcasted_iota(jnp.int32, (8, half_c), 0)
    lane = lax.broadcasted_iota(jnp.int32, (8, half_c), 1)
    turn_c = lax.rem(2 * half_c - begin, half_c)
    turn_r = lax.rem(8 - rest, 8)
    left_part = lane < half_c - begin
    upper_part = row < 8 - rest
    for c in range(0, comps, CHUNK):
        block = source[c : c + CHUNK, pl.ds(base, half_r + 8), :].reshape(CHUNK * (groups + 1), 8, cells_c)
        low = pltpu.roll(block[..., :half_c], turn_c, 2)
        high = pltpu.roll(block[..., half_c:], turn_c, 2)
        block = pltpu.roll(jnp.where(left_part, low, high), turn_r, 1).reshape(CHUNK, groups + 1, 8, half_c)
        for k in range(groups):
            out[c : c + CHUNK, k * 8 : k * 8 + 8, :] = jnp.where(upper_part, block[:, k], block[:, k + 1])


def add_at(total, piece, first, begin):
    comps, half_r, half_c = piece.shape
    groups = half_r // 8
    base, rest = near(first, half_r)
    row = lax.broadcasted_iota(jnp.int32, (8, half_c), 0)
    lane = lax.broadcasted_iota(jnp.int32, (8, half_c), 1)
    turn_c = lax.rem(begin, half_c)
    turn_r = lax.rem(rest, 8)
    lower_part = row >= rest
    right_part = lane >= begin
    for c in range(0, comps, CHUNK):
        block = piece[c : c + CHUNK].reshape(CHUNK * groups, 8, half_c)
        block = pltpu.roll(block, turn_r, 1).reshape(CHUNK, groups, 8, half_c)
        none = jnp.zeros((CHUNK, 8, half_c), jnp.float32)
        for k in range(groups + 1):
            here = block[:, k] if k < groups else none
            above = block[:, k - 1] if k else none
            turned = pltpu.roll(jnp.where(lower_part, here, above), turn_c, 2)
            rows = pl.ds(base + k * 8, 8)
            total[c : c + CHUNK, rows, :half_c] += jnp.where(right_part, turned, 0.0)
            total[c : c + CHUNK, rows, half_c:] += jnp.where(right_part, 0.0, turned)


def fold(state, sponge, rows, fine):
    comps, cells_r, cells_c = state.shape
    half_r, half_c = cells_r // 2, cells_c // 2
    weight = sponge[0]

    def one(c, carry):
        block = weight * state[c]
        for k in range(cells_c // LANES):
            part = slice(k * LANES, (k + 1) * LANES)
            fine[k] = block[:, part]
            rows[c, :, part] = fine[k, pl.ds(0, half_r, 2), :] + fine[k, pl.ds(1, half_r, 2), :]
        return carry

    lax.fori_loop(0, comps, one, 0, unroll=4)
    return jnp.dot(
        rows[...].reshape(comps * half_r, cells_c),
        narrow(cells_c, half_c),
        precision=lax.Precision.HIGHEST,
        preferred_element_type=jnp.float32,
    ).reshape(comps, half_r, half_c)


def pack_fold(out, comps, above, below, low, high, sponge, fine):
    weight = sponge[0]
    cells_r, cells_c = weight.shape
    half_r, half_c = cells_r // 2, cells_c // 2
    lines = jnp.concatenate([weight[:1] * above, weight[cells_r - 1 :] * below], axis=0)
    out[: 2 * comps, :] = jnp.dot(
        lines, narrow(cells_c, half_c), precision=lax.Precision.HIGHEST, preferred_element_type=jnp.float32
    )
    for k, line in enumerate((weight[:, :1] * low, weight[:, cells_c - 1 :] * high)):
        fine[k] = line
        out[2 * comps + k * half_r : 2 * comps + (k + 1) * half_r, :] = (
            fine[k, pl.ds(0, half_r, 2), :] + fine[k, pl.ds(1, half_r, 2), :]
        )


def patch(block, extra, outs):
    comps, half_r, half_c = block.shape
    row = lax.broadcasted_iota(jnp.int32, (half_r, half_c), 0)
    lane = lax.broadcasted_iota(jnp.int32, (half_r, half_c), 1)
    low = extra[2 * comps : 2 * comps + half_r, :]
    high = extra[2 * comps + half_r : 2 * comps + 2 * half_r, :]
    for c in range(comps):
        total = block[c]
        total = total + jnp.where(row == 0, extra[c : c + 1, :], 0.0)
        total = total + jnp.where(row == half_r - 1, extra[comps + c : comps + c + 1, :], 0.0)
        total = total + jnp.where(lane == 0, pltpu.roll(low, (half_c - c) % half_c, 1), 0.0)
        total = total + jnp.where(lane == half_c - 1, pltpu.roll(high, half_c - 1 - c, 1), 0.0)
        for out in outs:
            out[c] = total


def first_kernel(*refs):
    given, early, mask, late, refs = refs[:5], refs[5:7], refs[7], refs[8:12], refs[12:]
    rows, fine, *held, done = refs
    copies = [pltpu.make_async_copy(source, to, done.at[k]) for k, (source, to) in enumerate(zip(given, held))]
    for copy in copies:
        copy.start()
    for copy in copies:
        copy.wait()
    *tables, state, sponge = held
    state = state.at[0]
    grid, _, _ = place()

    @pl.when(grid == 0)
    def _():
        table = list(pieces_of(*tables))
        crop_all(state, table, EARLY, early)
        crop_all(state, table, LATE, late)
        mark_turned(mask, table)

    @pl.when(grid > 0)
    def _():
        mask[...] = jnp.zeros_like(mask)
        block = fold(state, sponge, rows, fine)
        for slot in range(SLOTS):

            @pl.when(grid == slot + 1)
            def _():
                for out in child_outs(slot, early, late):
                    out[...] = block


def stage_kernel(token, *refs):
    given, held, (rates, plan), scratch = refs[:10], list(refs[10:16]), refs[16:18], refs[18:]
    speeds, *tables, done = scratch
    copies = [
        pltpu.make_async_copy(source, to, done.at[k])
        for k, (source, to) in enumerate(zip(given, held + [speeds] + tables))
    ]
    for copy in copies:
        copy.start()
    for copy in copies:
        copy.wait()
    grid, i, j = place()
    for cls in range(NCLS):
        rates[cls] = jnp.full(rates.shape[1:], speeds[grid, cls], jnp.float32)
    for k, (_, _, serves, first, begin) in enumerate(pieces_of(*tables)):
        plan[3 * k] = serves.astype(jnp.int32)
        plan[3 * k + 1] = first
        plan[3 * k + 2] = begin
    plan[6 * SLOTS] = tables[0][jnp.maximum(grid - 1, 0), j, i]


def edge_sides(index):
    even = lax.rem(index, 2) == 0
    return even, jnp.logical_not(even)


def arrived(slot, kind):
    return -1 if (slot, kind) == MIXED else GOT.index(MIXED if (slot, kind) == (TURNED, 1) else (slot, kind))


def update_kernel(n_cols, plan, rates, state, sponge, agg, brk, mask, diff, *rest):
    got, rest = rest[: 2 * SLOTS], rest[2 * SLOTS :]
    wets, flux, sides = rest[0], rest[1], rest[2 : 4 + n_cols]
    nested, wide, coarse, fine = rest[4 + n_cols :]
    comps, cells_r, cells_c = wets.shape
    half_r, half_c = cells_r // 2, cells_c // 2
    grid, i, j = place()
    row_id = lax.broadcasted_iota(jnp.int32, (cells_r, cells_c), 0)
    col_id = lax.broadcasted_iota(jnp.int32, (cells_r, cells_c), 1)

    @pl.when(grid == 0)
    def _():
        covered = jnp.zeros((cells_r, cells_c), jnp.float32)
        for _, _, serves, first, begin in pieces(plan):
            inside = (row_id >= first) & (row_id < first + half_r) & (col_id >= begin) & (col_id < begin + half_c)
            covered = covered + jnp.where(inside & serves, 1.0, 0.0)
        keep = 1.0 - relaxation * covered

        def own(step, carry):
            rows = pl.ds(step * CHUNK, CHUNK)
            nested[rows] = keep * state[rows]
            return carry

        lax.fori_loop(0, comps // CHUNK, own, 0)
        for slot, kind, serves, first, begin in pieces(plan):

            @pl.when(serves)
            def _():
                add_at(nested, got[arrived(slot, kind)], first, begin)

    @pl.when(grid > 0)
    def _():
        for slot in range(SLOTS):
            for kind in range(1 if slot == TURNED else 2):

                @pl.when((grid == slot + 1) & ((plan[6 * SLOTS] == kind) | (slot == TURNED)))
                def _():
                    coarse[...] = got[GOT.index((slot, kind))][...]

        wide[...] = jnp.dot(
            coarse[...].reshape(comps * half_r, half_c),
            widen(half_c, cells_c) * (relaxation / 4.0),
            precision=lax.Precision.HIGHEST,
            preferred_element_type=jnp.float32,
        ).reshape(comps, half_r, cells_c)
        keep = 1.0 - sponge[0]

        def own(c, carry):
            for k in range(cells_c // LANES):
                part = slice(k * LANES, (k + 1) * LANES)
                block = wide[c, :, part]
                fine[k, pl.ds(0, half_r, 2), :] = block
                fine[k, pl.ds(1, half_r, 2), :] = block
                nested[c, :, part] = keep[:, part] * state[c, :, part] + fine[k]
            return carry

        lax.fori_loop(0, comps, own, 0, unroll=4)

    a, b = agg[0], brk[0]
    wet = mask[0].astype(jnp.float32)
    spread = diff[0]
    row_far = edge_sides(i)[::-1]
    col_far = edge_sides(j)
    lane = lax.broadcasted_iota(jnp.int32, (cells_r, LANES), 1)

    def level(step, carry):
        below, columns = carry
        l = LEV - 1 - step
        u0, u1, u2 = nested[l], nested[LEV + l], nested[2 * LEV + l]
        flocced = ((1.0 - a) * u0 + a * u1, b * u0 + (1.0 - a - b) * u1 + a * u2, b * u1 + (1.0 - b) * u2)
        columns = list(columns)
        for cls in range(NCLS):
            c = cls * LEV + l
            rate = rates[cls]
            w = wet * ((1.0 - rate) * flocced[cls] + rate * below[cls])
            f = spread * w
            wets[c] = w
            flux[c] = f
            for phase in range(2):
                sides[phase][pl.ds(c, 1), :] = jnp.where(row_far[phase], f[cells_r - 1 :], f[:1])
            for phase in range(n_cols):
                far = col_far[phase]
                slab = jnp.where(far, f[:, cells_c - LANES :], f[:, :LANES])
                turn = lax.rem(c - jnp.where(far, LANES - 1, 0) + LANES, LANES)
                columns[phase] = jnp.where(lane == c, pltpu.roll(slab, turn, 1), columns[phase])
        return flocced, tuple(columns)

    nothing = jnp.zeros((cells_r, cells_c), jnp.float32)
    empty = jnp.zeros((cells_r, LANES), jnp.float32)
    _, columns = lax.fori_loop(0, LEV, level, ((nothing,) * NCLS, (empty,) * n_cols), unroll=True)
    for phase in range(n_cols):
        sides[2 + phase][...] = columns[phase]


def spread_kernel(last, wets, flux, *rest):
    bulk = rest[0].at[0] if last else rest[1]
    comps, cells_r, cells_c = bulk.shape
    grid, _, _ = place()
    row_id = lax.broadcasted_iota(jnp.int32, (cells_r, cells_c), 0)
    col_id = lax.broadcasted_iota(jnp.int32, (cells_r, cells_c), 1)

    def one(c, carry):
        f = flux[c]
        total = wets[c] - 4.0 * f
        total = total + jnp.where(row_id == 0, 0.0, pltpu.roll(f, 1, 0))
        total = total + jnp.where(row_id == cells_r - 1, 0.0, pltpu.roll(f, cells_r - 1, 0))
        total = total + jnp.where(col_id == 0, 0.0, pltpu.roll(f, 1, 1))
        total = total + jnp.where(col_id == cells_c - 1, 0.0, pltpu.roll(f, cells_c - 1, 1))
        bulk[c] = total
        return carry

    lax.fori_loop(0, comps, one, 0, unroll=2)
    if not last:
        sponge, _, folded, rows, fine = rest

        @pl.when(grid > 0)
        def _():
            folded[...] = fold(bulk, sponge, rows, fine)


def halo_kernel(n_cols, sizes, last, *rest):
    plan, rest = (None, rest) if last else (rest[0], rest[1:])
    bulk, rest = rest[0], rest[1:]
    given, rest = ((), rest) if last else (rest[:2], rest[2:])
    sides, state, rest = rest[: 2 + n_cols], rest[2 + n_cols], rest[3 + n_cols :]
    old, new = (bulk.at[0], state.at[0]) if last else (bulk, state)
    comps, cells_r, cells_c = new.shape
    grid, i, j = place()
    row = lax.broadcasted_iota(jnp.int32, (8, cells_c), 0)
    even, _ = edge_sides(i)
    second, first = sides[0][...], sides[1][...]
    above = jnp.where(i == 0, 0.0, jnp.where(even, second, first))
    below = jnp.where(i == sizes[0] - 1, 0.0, jnp.where(even, first, second))
    low = high = jnp.zeros((cells_r, LANES), jnp.float32)
    for phase, far in zip(range(n_cols), edge_sides(j)):
        column = sides[2 + phase][...]
        low = low + jnp.where(jnp.logical_not(far) & (j > 0), column, 0.0)
        high = high + jnp.where(far & (j < sizes[1] - 1), column, 0.0)
    for c in range(comps):
        new[c, :8, :] = old[c, :8, :] + jnp.where(row == 0, above[c : c + 1], 0.0)
        new[c, 8 : cells_r - 8, :] = old[c, 8 : cells_r - 8, :]
        new[c, cells_r - 8 :, :] = old[c, cells_r - 8 :, :] + jnp.where(row == 7, below[c : c + 1], 0.0)
    lane = lax.broadcasted_iota(jnp.int32, (cells_r, LANES), 1)

    @pl.when(j < sizes[1] - 1)
    def _():
        for c in range(comps):
            new[c, :, cells_c - LANES :] += jnp.where(lane == LANES - 1, pltpu.roll(high, LANES - 1 - c, 1), 0.0)

    @pl.when(j > 0)
    def _():
        for c in range(comps):
            new[c, :, :LANES] += jnp.where(lane == 0, pltpu.roll(low, (LANES - c) % LANES, 1), 0.0)

    if last:
        return
    sponge, folded = given
    early, mask, packed, fine = rest[:2], *rest[2:]

    @pl.when(grid == 0)
    def _():
        table = list(pieces(plan))
        crop_all(new, table, EARLY, early)
        mark_turned(mask, table)

    @pl.when(grid > 0)
    def _():
        mask[...] = jnp.zeros_like(mask)
        pack_fold(packed, comps, above, below, low, high, sponge, fine)

    @pl.when(grid == FORWARDED + 1)
    def _():
        patch(folded, packed, child_outs(FORWARDED, early, ()))


def crop_all(state, table, order, outs):
    for slot, kind, serves, first, begin in table:
        if (slot, kind) in order and ((slot, kind) != (TURNED, 1) or order is EARLY):

            @pl.when(serves)
            def _():
                crop(state, outs[order.index((slot, kind))], first, begin)


def mark_turned(mask, table):
    for slot, kind, serves, _, _ in table:
        if (slot, kind) == (TURNED, 0):
            mask[...] = jnp.full(mask.shape, jnp.where(serves, 0.0, 1.0), jnp.float32)


def child_outs(slot, early, late):
    if slot == FORWARDED:
        return [early[0]]
    return [late[LATE.index(MIXED if (slot, kind) == (TURNED, 1) else (slot, kind))] for kind in range(2)]


def late_kernel(plan, state, folded, packed, *outs):
    grid, _, _ = place()

    @pl.when(grid == 0)
    def _():
        crop_all(state, list(pieces(plan)), LATE, outs)

    for slot in range(SLOTS):
        if slot != FORWARDED:

            @pl.when(grid == slot + 1)
            def _():
                patch(folded, packed, child_outs(slot, (), outs))


def merge_kernel(mask, own, other, out):
    out[...] = jnp.where(mask[:1, :] > 0.5, other[...], own[...])


def between_parents(block):
    return lax.ppermute(block, ("grid", "gx"), [(i, i ^ 1) for i in range(lax.axis_size("gx"))])


def with_children(block, slot, kind):
    n_x = lax.axis_size("gx")
    pairs = []
    for i in range(n_x):
        parent, child = i, (slot + 1) * n_x + (i ^ kind)
        source = (TURNED + 1) * n_x + (i ^ kind) if (slot, kind) == MIXED else child
        pairs += [(parent, child), (source, parent)]
    return lax.ppermute(block, ("grid", "gx"), pairs)


def exchange(early, mask, late):
    blocks = dict(zip(LATE, late))
    blocks[EARLY[0]] = early[0]
    other = between_parents(early[1])
    own = blocks[TURNED, 0]
    blocks[TURNED, 0] = pl.pallas_call(
        merge_kernel,
        out_shape=jax.ShapeDtypeStruct(own.shape, own.dtype),
        in_specs=[VM] * 3,
        out_specs=VM,
        compiler_params=PARAMS,
        name="merge",
    )(mask, own, other)
    got = [
        with_children(blocks[slot, kind], slot, kind)
        for slot, kind in GOT
    ]
    forward, got[1] = lax.optimization_barrier((got[0], got[1]))
    return got + [between_parents(forward)]


def swap_pairs(size, phase):
    pairs = []
    for k in range(phase, size + phase, 2):
        first, second = k % size, (k + 1) % size
        pairs += [(first, second), (second, first)]
    return pairs


def local(adjoint, sea_mask, diffusivity, aggregation, breakup, sponge, settling, partner_flip, row_offset, col_offset):
    comps, cells_r, cells_c = adjoint.shape[1:]
    half_r, half_c = cells_r // 2, cells_c // 2
    n_x, n_y = lax.axis_size("gx"), lax.axis_size("gy")
    n_cols = 1 if n_y == 2 else 2
    f32 = jnp.float32
    tile = jax.ShapeDtypeStruct((comps, cells_r, cells_c), f32)
    block = jax.ShapeDtypeStruct((comps, half_r, half_c), f32)
    side = [jax.ShapeDtypeStruct((comps, cells_c), f32)] * 2 + [jax.ShapeDtypeStruct((cells_r, LANES), f32)] * n_cols
    fold_scratch = [pltpu.VMEM((comps, half_r, cells_c), f32), pltpu.VMEM((cells_c // LANES, cells_r, LANES), f32)]
    tables = [table.transpose(0, 2, 1) for table in (partner_flip, row_offset, col_offset)]

    flag = jax.ShapeDtypeStruct((8, half_c), f32)
    blocks = pl.pallas_call(
        first_kernel,
        out_shape=[block] * 2 + [flag] + [block] * 4,
        in_specs=[pl.BlockSpec(memory_space=pltpu.HBM)] * 5,
        out_specs=[VM] * 7,
        scratch_shapes=fold_scratch
        + [pltpu.SMEM(table.shape, table.dtype) for table in tables]
        + [pltpu.VMEM(adjoint.shape, f32), pltpu.VMEM(sponge.shape, f32), pltpu.SemaphoreType.DMA((5,))],
        compiler_params=pltpu.CompilerParams(vmem_limit_bytes=60 * 2**20),
        name="first_payload",
    )(*tables, adjoint, sponge)
    early, mask, late = blocks[:2], blocks[2], blocks[3:]
    fields = (adjoint, sponge, aggregation, breakup, sea_mask, diffusivity)
    state, sponge, *fields, rates, plan = pl.pallas_call(
        stage_kernel,
        out_shape=[jax.ShapeDtypeStruct(field.shape, field.dtype) for field in fields]
        + [jax.ShapeDtypeStruct((NCLS, 1, cells_c), f32), jax.ShapeDtypeStruct((6 * SLOTS + 1,), jnp.int32)],
        in_specs=[VM] + [pl.BlockSpec(memory_space=pltpu.HBM)] * 10,
        out_specs=[VM] * 7 + [SM],
        scratch_shapes=[pltpu.SMEM(settling.shape, f32)]
        + [pltpu.SMEM(table.shape, table.dtype) for table in tables]
        + [pltpu.SemaphoreType.DMA((10,))],
        compiler_params=PARAMS,
        name="stage_fields",
    )(mask, *fields, settling, *tables)
    state = state.reshape(tile.shape)
    fold_scratch = [pltpu.VMEM((comps, half_r, cells_c), f32), pltpu.VMEM((cells_c // LANES, cells_r, LANES), f32)]
    for step in range(STEPS):
        last = step == STEPS - 1
        new = jax.ShapeDtypeStruct(adjoint.shape, f32) if last else tile
        got = exchange(early, mask, late)
        wets, flux, *sides = pl.pallas_call(
            functools.partial(update_kernel, n_cols),
            out_shape=[tile] * 2 + side,
            in_specs=[SM] + [VM] * (7 + 2 * SLOTS),
            out_specs=[VM] * (2 + len(side)),
            scratch_shapes=[
                pltpu.VMEM(tile.shape, f32),
                pltpu.VMEM((comps, half_r, cells_c), f32),
                pltpu.VMEM(block.shape, f32),
                pltpu.VMEM((cells_c // LANES, cells_r, LANES), f32),
            ],
            compiler_params=PARAMS,
            name="update",
        )(plan, rates, state, sponge, *fields, *got)
        sides = [lax.ppermute(sides[k], "gx", swap_pairs(n_x, 1 - k)) for k in range(2)] + [
            lax.ppermute(sides[2 + k], "gy", swap_pairs(n_y, k)) for k in range(n_cols)
        ]
        bulk, *folded = pl.pallas_call(
            functools.partial(spread_kernel, last),
            out_shape=[new] + ([] if last else [block]),
            in_specs=[VM] * (2 if last else 3),
            out_specs=[VM] * (1 if last else 2),
            scratch_shapes=[] if last else fold_scratch,
            compiler_params=PARAMS,
            name="spread_last" if last else "spread",
        )(wets, flux, *([] if last else [sponge]))
        extra = jax.ShapeDtypeStruct((2 * comps + 2 * half_r, half_c), f32)
        extra = jax.ShapeDtypeStruct((2 * comps + 2 * half_r, half_c), f32)
        state, *out = pl.pallas_call(
            functools.partial(halo_kernel, n_cols, (n_x, n_y), last),
            out_shape=[new] + ([] if last else [block] * 2 + [flag, extra]),
            in_specs=[SM] * (0 if last else 1) + [VM] * (1 + len(side) + (0 if last else 2)),
            out_specs=[VM] * (1 if last else 5),
            scratch_shapes=[] if last else fold_scratch[1:],
            compiler_params=PARAMS,
            name="halo_last" if last else "halo",
        )(*([] if last else [plan]), bulk, *([] if last else [sponge, *folded]), *sides)
        if not last:
            early, mask, packed = out[:2], out[2], out[3]
            late = pl.pallas_call(
                late_kernel,
                out_shape=[block] * 4,
                in_specs=[SM] + [VM] * 3,
                out_specs=[VM] * 4,
                compiler_params=PARAMS,
                name="late_payload",
            )(plan, state, *folded, packed)
    return state


def solution(mesh):
    in_specs = (
        P("grid", None, "gx", "gy"),
        P("grid", "gx", "gy"),
        P("grid", "gx", "gy"),
        P("grid", "gx", "gy"),
        P("grid", "gx", "gy"),
        P("grid", "gx", "gy"),
        P(),
        P(),
        P(),
        P(),
    )
    out_specs = P("grid", None, "gx", "gy")
    return jax.shard_map(local, mesh=mesh, in_specs=in_specs, out_specs=out_specs, check_vma=False)
```

```python
import functools

import jax
import jax.numpy as jnp
from jax import lax
from jax.experimental import pallas as pl
from jax.experimental.pallas import tpu as pltpu
from jax.sharding import PartitionSpec as P

NCLS = 3
LEV = 8
STEPS = 2
SLOTS = 3
LANES = 128
CHUNK = 8

relaxation = 0.125

VM = pl.BlockSpec(memory_space=pltpu.VMEM)
SM = pl.BlockSpec(memory_space=pltpu.SMEM)
PARAMS = pltpu.CompilerParams(vmem_limit_bytes=16 * 2**20)


def place():
    return lax.axis_index("grid"), lax.axis_index("gx"), lax.axis_index("gy")


TURNED = 2
FORWARDED = 0
EARLY = ((FORWARDED, 0), (TURNED, 1))
MIXED = (FORWARDED, 1)
LATE = ((1, 0), MIXED, (1, 1), (2, 0))
GOT = (EARLY[0],) + LATE


def pieces_of(flip, top, left):
    _, i, j = place()
    for slot in range(SLOTS):
        for kind, row in ((0, i), (1, jnp.bitwise_xor(i, 1))):
            yield slot, kind, flip[slot, j, row] == kind, top[slot, j, row], left[slot, j, row]


def pieces(plan):
    for k in range(2 * SLOTS):
        yield k // 2, k % 2, plan[3 * k] == 1, plan[3 * k + 1], plan[3 * k + 2]


def widen(half, cells):
    row = lax.broadcasted_iota(jnp.int32, (half, cells), 0)
    col = lax.broadcasted_iota(jnp.int32, (half, cells), 1)
    return (lax.shift_right_logical(col, 1) == row).astype(jnp.float32)


def narrow(cells, half):
    row = lax.broadcasted_iota(jnp.int32, (cells, half), 0)
    col = lax.broadcasted_iota(jnp.int32, (cells, half), 1)
    return (lax.shift_right_logical(row, 1) == col).astype(jnp.float32)


def near(first, half_r):
    base = jnp.minimum(lax.shift_right_logical(first, 3) * 8, half_r - 8)
    return pl.multiple_of(base, 8), first - base


def crop(source, out, first, begin):
    comps, cells_r, cells_c = source.shape
    half_r, half_c = out.shape[1:]
    groups = half_r // 8
    base, rest = near(first, half_r)
    row = lax.broadcasted_iota(jnp.int32, (8, half_c), 0)
    lane = lax.broadcasted_iota(jnp.int32, (8, half_c), 1)
    turn_c = lax.rem(2 * half_c - begin, half_c)
    turn_r = lax.rem(8 - rest, 8)
    left_part = lane < half_c - begin
    upper_part = row < 8 - rest
    for c in range(0, comps, CHUNK):
        block = source[c : c + CHUNK, pl.ds(base, half_r + 8), :].reshape(CHUNK * (groups + 1), 8, cells_c)
        low = pltpu.roll(block[..., :half_c], turn_c, 2)
        high = pltpu.roll(block[..., half_c:], turn_c, 2)
        block = pltpu.roll(jnp.where(left_part, low, high), turn_r, 1).reshape(CHUNK, groups + 1, 8, half_c)
        for k in range(groups):
            out[c : c + CHUNK, k * 8 : k * 8 + 8, :] = jnp.where(upper_part, block[:, k], block[:, k + 1])


def add_at(total, piece, first, begin):
    comps, half_r, half_c = piece.shape
    groups = half_r // 8
    base, rest = near(first, half_r)
    row = lax.broadcasted_iota(jnp.int32, (8, half_c), 0)
    lane = lax.broadcasted_iota(jnp.int32, (8, half_c), 1)
    turn_c = lax.rem(begin, half_c)
    turn_r = lax.rem(rest, 8)
    lower_part = row >= rest
    right_part = lane >= begin
    for c in range(0, comps, CHUNK):
        block = piece[c : c + CHUNK].reshape(CHUNK * groups, 8, half_c)
        block = pltpu.roll(block, turn_r, 1).reshape(CHUNK, groups, 8, half_c)
        none = jnp.zeros((CHUNK, 8, half_c), jnp.float32)
        for k in range(groups + 1):
            here = block[:, k] if k < groups else none
            above = block[:, k - 1] if k else none
            turned = pltpu.roll(jnp.where(lower_part, here, above), turn_c, 2)
            rows = pl.ds(base + k * 8, 8)
            total[c : c + CHUNK, rows, :half_c] += jnp.where(right_part, turned, 0.0)
            total[c : c + CHUNK, rows, half_c:] += jnp.where(right_part, 0.0, turned)


def fold(state, sponge, rows, fine):
    comps, cells_r, cells_c = state.shape
    half_r, half_c = cells_r // 2, cells_c // 2
    weight = sponge[0]

    def one(c, carry):
        block = weight * state[c]
        for k in range(cells_c // LANES):
            part = slice(k * LANES, (k + 1) * LANES)
            fine[k] = block[:, part]
            rows[c, :, part] = fine[k, pl.ds(0, half_r, 2), :] + fine[k, pl.ds(1, half_r, 2), :]
        return carry

    lax.fori_loop(0, comps, one, 0, unroll=4)
    return jnp.dot(
        rows[...].reshape(comps * half_r, cells_c),
        narrow(cells_c, half_c),
        precision=lax.Precision.HIGHEST,
        preferred_element_type=jnp.float32,
    ).reshape(comps, half_r, half_c)


def pack_fold(out, comps, above, below, low, high, sponge, fine):
    weight = sponge[0]
    cells_r, cells_c = weight.shape
    half_r, half_c = cells_r // 2, cells_c // 2
    lines = jnp.concatenate([weight[:1] * above, weight[cells_r - 1 :] * below], axis=0)
    out[: 2 * comps, :] = jnp.dot(
        lines, narrow(cells_c, half_c), precision=lax.Precision.HIGHEST, preferred_element_type=jnp.float32
    )
    for k, line in enumerate((weight[:, :1] * low, weight[:, cells_c - 1 :] * high)):
        fine[k] = line
        out[2 * comps + k * half_r : 2 * comps + (k + 1) * half_r, :] = (
            fine[k, pl.ds(0, half_r, 2), :] + fine[k, pl.ds(1, half_r, 2), :]
        )


def patch(block, extra, outs):
    comps, half_r, half_c = block.shape
    row = lax.broadcasted_iota(jnp.int32, (half_r, half_c), 0)
    lane = lax.broadcasted_iota(jnp.int32, (half_r, half_c), 1)
    low = extra[2 * comps : 2 * comps + half_r, :]
    high = extra[2 * comps + half_r : 2 * comps + 2 * half_r, :]
    for c in range(comps):
        total = block[c]
        total = total + jnp.where(row == 0, extra[c : c + 1, :], 0.0)
        total = total + jnp.where(row == half_r - 1, extra[comps + c : comps + c + 1, :], 0.0)
        total = total + jnp.where(lane == 0, pltpu.roll(low, (half_c - c) % half_c, 1), 0.0)
        total = total + jnp.where(lane == half_c - 1, pltpu.roll(high, half_c - 1 - c, 1), 0.0)
        for out in outs:
            out[c] = total


def first_kernel(*refs):
    given, early, mask, late, refs = refs[:5], refs[5:7], refs[7], refs[8:12], refs[12:]
    rows, fine, *held, done = refs
    copies = [pltpu.make_async_copy(source, to, done.at[k]) for k, (source, to) in enumerate(zip(given, held))]
    for copy in copies:
        copy.start()
    for copy in copies:
        copy.wait()
    *tables, state, sponge = held
    state = state.at[0]
    grid, _, _ = place()

    @pl.when(grid == 0)
    def _():
        table = list(pieces_of(*tables))
        crop_all(state, table, EARLY, early)
        crop_all(state, table, LATE, late)
        mark_turned(mask, table)

    @pl.when(grid > 0)
    def _():
        mask[...] = jnp.zeros_like(mask)
        block = fold(state, sponge, rows, fine)
        for slot in range(SLOTS):

            @pl.when(grid == slot + 1)
            def _():
                for out in child_outs(slot, early, late):
                    out[...] = block


def stage_kernel(token, *refs):
    given, held, (rates, plan), scratch = refs[:10], list(refs[10:16]), refs[16:18], refs[18:]
    speeds, *tables, done = scratch
    copies = [
        pltpu.make_async_copy(source, to, done.at[k])
        for k, (source, to) in enumerate(zip(given, held + [speeds] + tables))
    ]
    for copy in copies:
        copy.start()
    for copy in copies:
        copy.wait()
    grid, i, j = place()
    for cls in range(NCLS):
        rates[cls] = jnp.full(rates.shape[1:], speeds[grid, cls], jnp.float32)
    for k, (_, _, serves, first, begin) in enumerate(pieces_of(*tables)):
        plan[3 * k] = serves.astype(jnp.int32)
        plan[3 * k + 1] = first
        plan[3 * k + 2] = begin
    plan[6 * SLOTS] = tables[0][jnp.maximum(grid - 1, 0), j, i]


def edge_sides(index):
    even = lax.rem(index, 2) == 0
    return even, jnp.logical_not(even)


def arrived(slot, kind):
    return -1 if (slot, kind) == MIXED else GOT.index(MIXED if (slot, kind) == (TURNED, 1) else (slot, kind))


def update_kernel(n_cols, plan, rates, state, sponge, agg, brk, mask, diff, *rest):
    got, rest = rest[: 2 * SLOTS], rest[2 * SLOTS :]
    wets, flux, sides = rest[0], rest[1], rest[2 : 4 + n_cols]
    nested, wide, coarse, fine = rest[4 + n_cols :]
    comps, cells_r, cells_c = wets.shape
    half_r, half_c = cells_r // 2, cells_c // 2
    grid, i, j = place()
    row_id = lax.broadcasted_iota(jnp.int32, (cells_r, cells_c), 0)
    col_id = lax.broadcasted_iota(jnp.int32, (cells_r, cells_c), 1)

    @pl.when(grid == 0)
    def _():
        covered = jnp.zeros((cells_r, cells_c), jnp.float32)
        for _, _, serves, first, begin in pieces(plan):
            inside = (row_id >= first) & (row_id < first + half_r) & (col_id >= begin) & (col_id < begin + half_c)
            covered = covered + jnp.where(inside & serves, 1.0, 0.0)
        keep = 1.0 - relaxation * covered

        def own(step, carry):
            rows = pl.ds(step * CHUNK, CHUNK)
            nested[rows] = keep * state[rows]
            return carry

        lax.fori_loop(0, comps // CHUNK, own, 0)
        for slot, kind, serves, first, begin in pieces(plan):

            @pl.when(serves)
            def _():
                add_at(nested, got[arrived(slot, kind)], first, begin)

    @pl.when(grid > 0)
    def _():
        for slot in range(SLOTS):
            for kind in range(1 if slot == TURNED else 2):

                @pl.when((grid == slot + 1) & ((plan[6 * SLOTS] == kind) | (slot == TURNED)))
                def _():
                    coarse[...] = got[GOT.index((slot, kind))][...]

        wide[...] = jnp.dot(
            coarse[...].reshape(comps * half_r, half_c),
            widen(half_c, cells_c) * (relaxation / 4.0),
            precision=lax.Precision.HIGHEST,
            preferred_element_type=jnp.float32,
        ).reshape(comps, half_r, cells_c)
        keep = 1.0 - sponge[0]

        def own(c, carry):
            for k in range(cells_c // LANES):
                part = slice(k * LANES, (k + 1) * LANES)
                block = wide[c, :, part]
                fine[k, pl.ds(0, half_r, 2), :] = block
                fine[k, pl.ds(1, half_r, 2), :] = block
                nested[c, :, part] = keep[:, part] * state[c, :, part] + fine[k]
            return carry

        lax.fori_loop(0, comps, own, 0, unroll=4)

    a, b = agg[0], brk[0]
    wet = mask[0].astype(jnp.float32)
    spread = diff[0]
    row_far = edge_sides(i)[::-1]
    col_far = edge_sides(j)
    lane = lax.broadcasted_iota(jnp.int32, (cells_r, LANES), 1)

    def level(step, carry):
        below, columns = carry
        l = LEV - 1 - step
        u0, u1, u2 = nested[l], nested[LEV + l], nested[2 * LEV + l]
        flocced = ((1.0 - a) * u0 + a * u1, b * u0 + (1.0 - a - b) * u1 + a * u2, b * u1 + (1.0 - b) * u2)
        columns = list(columns)
        for cls in range(NCLS):
            c = cls * LEV + l
            rate = rates[cls]
            w = wet * ((1.0 - rate) * flocced[cls] + rate * below[cls])
            f = spread * w
            wets[c] = w
            flux[c] = f
            for phase in range(2):
                sides[phase][pl.ds(c, 1), :] = jnp.where(row_far[phase], f[cells_r - 1 :], f[:1])
            for phase in range(n_cols):
                far = col_far[phase]
                slab = jnp.where(far, f[:, cells_c - LANES :], f[:, :LANES])
                turn = lax.rem(c - jnp.where(far, LANES - 1, 0) + LANES, LANES)
                columns[phase] = jnp.where(lane == c, pltpu.roll(slab, turn, 1), columns[phase])
        return flocced, tuple(columns)

    nothing = jnp.zeros((cells_r, cells_c), jnp.float32)
    empty = jnp.zeros((cells_r, LANES), jnp.float32)
    _, columns = lax.fori_loop(0, LEV, level, ((nothing,) * NCLS, (empty,) * n_cols), unroll=True)
    for phase in range(n_cols):
        sides[2 + phase][...] = columns[phase]


def spread_kernel(last, wets, flux, *rest):
    bulk = rest[0].at[0] if last else rest[1]
    comps, cells_r, cells_c = bulk.shape
    grid, _, _ = place()
    row_id = lax.broadcasted_iota(jnp.int32, (cells_r, cells_c), 0)
    col_id = lax.broadcasted_iota(jnp.int32, (cells_r, cells_c), 1)

    def one(c, carry):
        f = flux[c]
        total = wets[c] - 4.0 * f
        total = total + jnp.where(row_id == 0, 0.0, pltpu.roll(f, 1, 0))
        total = total + jnp.where(row_id == cells_r - 1, 0.0, pltpu.roll(f, cells_r - 1, 0))
        total = total + jnp.where(col_id == 0, 0.0, pltpu.roll(f, 1, 1))
        total = total + jnp.where(col_id == cells_c - 1, 0.0, pltpu.roll(f, cells_c - 1, 1))
        bulk[c] = total
        return carry

    lax.fori_loop(0, comps, one, 0, unroll=6)
    if not last:
        sponge, _, folded, rows, fine = rest

        @pl.when(grid > 0)
        def _():
            folded[...] = fold(bulk, sponge, rows, fine)


def halo_kernel(n_cols, sizes, last, *rest):
    plan, rest = (None, rest) if last else (rest[0], rest[1:])
    bulk, rest = rest[0], rest[1:]
    given, rest = ((), rest) if last else (rest[:2], rest[2:])
    sides, state, rest = rest[: 2 + n_cols], rest[2 + n_cols], rest[3 + n_cols :]
    old, new = (bulk.at[0], state.at[0]) if last else (bulk, state)
    comps, cells_r, cells_c = new.shape
    grid, i, j = place()
    row = lax.broadcasted_iota(jnp.int32, (8, cells_c), 0)
    even, _ = edge_sides(i)
    second, first = sides[0][...], sides[1][...]
    above = jnp.where(i == 0, 0.0, jnp.where(even, second, first))
    below = jnp.where(i == sizes[0] - 1, 0.0, jnp.where(even, first, second))
    low = high = jnp.zeros((cells_r, LANES), jnp.float32)
    for phase, far in zip(range(n_cols), edge_sides(j)):
        column = sides[2 + phase][...]
        low = low + jnp.where(jnp.logical_not(far) & (j > 0), column, 0.0)
        high = high + jnp.where(far & (j < sizes[1] - 1), column, 0.0)
    for c in range(comps):
        new[c, :8, :] = old[c, :8, :] + jnp.where(row == 0, above[c : c + 1], 0.0)
        new[c, 8 : cells_r - 8, :] = old[c, 8 : cells_r - 8, :]
        new[c, cells_r - 8 :, :] = old[c, cells_r - 8 :, :] + jnp.where(row == 7, below[c : c + 1], 0.0)
    lane = lax.broadcasted_iota(jnp.int32, (cells_r, LANES), 1)

    @pl.when(j < sizes[1] - 1)
    def _():
        for c in range(comps):
            new[c, :, cells_c - LANES :] += jnp.where(lane == LANES - 1, pltpu.roll(high, LANES - 1 - c, 1), 0.0)

    @pl.when(j > 0)
    def _():
        for c in range(comps):
            new[c, :, :LANES] += jnp.where(lane == 0, pltpu.roll(low, (LANES - c) % LANES, 1), 0.0)

    if last:
        return
    sponge, folded = given
    early, mask, packed, fine = rest[:2], *rest[2:]

    @pl.when(grid == 0)
    def _():
        table = list(pieces(plan))
        crop_all(new, table, EARLY, early)
        mark_turned(mask, table)

    @pl.when(grid > 0)
    def _():
        mask[...] = jnp.zeros_like(mask)
        pack_fold(packed, comps, above, below, low, high, sponge, fine)

    @pl.when(grid == FORWARDED + 1)
    def _():
        patch(folded, packed, child_outs(FORWARDED, early, ()))


def crop_all(state, table, order, outs):
    for slot, kind, serves, first, begin in table:
        if (slot, kind) in order and ((slot, kind) != (TURNED, 1) or order is EARLY):

            @pl.when(serves)
            def _():
                crop(state, outs[order.index((slot, kind))], first, begin)


def mark_turned(mask, table):
    for slot, kind, serves, _, _ in table:
        if (slot, kind) == (TURNED, 0):
            mask[...] = jnp.full(mask.shape, jnp.where(serves, 0.0, 1.0), jnp.float32)


def child_outs(slot, early, late):
    if slot == FORWARDED:
        return [early[0]]
    return [late[LATE.index(MIXED if (slot, kind) == (TURNED, 1) else (slot, kind))] for kind in range(2)]


def late_kernel(plan, state, folded, packed, *outs):
    grid, _, _ = place()

    @pl.when(grid == 0)
    def _():
        crop_all(state, list(pieces(plan)), LATE, outs)

    for slot in range(SLOTS):
        if slot != FORWARDED:

            @pl.when(grid == slot + 1)
            def _():
                patch(folded, packed, child_outs(slot, (), outs))


def merge_kernel(mask, own, other, out):
    out[...] = jnp.where(mask[:1, :] > 0.5, other[...], own[...])


def between_parents(block):
    return lax.ppermute(block, ("grid", "gx"), [(i, i ^ 1) for i in range(lax.axis_size("gx"))])


def with_children(block, slot, kind):
    n_x = lax.axis_size("gx")
    pairs = []
    for i in range(n_x):
        parent, child = i, (slot + 1) * n_x + (i ^ kind)
        source = (TURNED + 1) * n_x + (i ^ kind) if (slot, kind) == MIXED else child
        pairs += [(parent, child), (source, parent)]
    return lax.ppermute(block, ("grid", "gx"), pairs)


def exchange(early, mask, late):
    blocks = dict(zip(LATE, late))
    blocks[EARLY[0]] = early[0]
    other = between_parents(early[1])
    own = blocks[TURNED, 0]
    blocks[TURNED, 0] = pl.pallas_call(
        merge_kernel,
        out_shape=jax.ShapeDtypeStruct(own.shape, own.dtype),
        in_specs=[VM] * 3,
        out_specs=VM,
        compiler_params=PARAMS,
        name="merge",
    )(mask, own, other)
    got = [
        with_children(blocks[slot, kind], slot, kind)
        for slot, kind in GOT
    ]
    forward, got[1] = lax.optimization_barrier((got[0], got[1]))
    return got + [between_parents(forward)]


def swap_pairs(size, phase):
    pairs = []
    for k in range(phase, size + phase, 2):
        first, second = k % size, (k + 1) % size
        pairs += [(first, second), (second, first)]
    return pairs


def local(adjoint, sea_mask, diffusivity, aggregation, breakup, sponge, settling, partner_flip, row_offset, col_offset):
    comps, cells_r, cells_c = adjoint.shape[1:]
    half_r, half_c = cells_r // 2, cells_c // 2
    n_x, n_y = lax.axis_size("gx"), lax.axis_size("gy")
    n_cols = 1 if n_y == 2 else 2
    f32 = jnp.float32
    tile = jax.ShapeDtypeStruct((comps, cells_r, cells_c), f32)
    block = jax.ShapeDtypeStruct((comps, half_r, half_c), f32)
    side = [jax.ShapeDtypeStruct((comps, cells_c), f32)] * 2 + [jax.ShapeDtypeStruct((cells_r, LANES), f32)] * n_cols
    fold_scratch = [pltpu.VMEM((comps, half_r, cells_c), f32), pltpu.VMEM((cells_c // LANES, cells_r, LANES), f32)]
    tables = [table.transpose(0, 2, 1) for table in (partner_flip, row_offset, col_offset)]

    flag = jax.ShapeDtypeStruct((8, half_c), f32)
    blocks = pl.pallas_call(
        first_kernel,
        out_shape=[block] * 2 + [flag] + [block] * 4,
        in_specs=[pl.BlockSpec(memory_space=pltpu.HBM)] * 5,
        out_specs=[VM] * 7,
        scratch_shapes=fold_scratch
        + [pltpu.SMEM(table.shape, table.dtype) for table in tables]
        + [pltpu.VMEM(adjoint.shape, f32), pltpu.VMEM(sponge.shape, f32), pltpu.SemaphoreType.DMA((5,))],
        compiler_params=pltpu.CompilerParams(vmem_limit_bytes=60 * 2**20),
        name="first_payload",
    )(*tables, adjoint, sponge)
    early, mask, late = blocks[:2], blocks[2], blocks[3:]
    fields = (adjoint, sponge, aggregation, breakup, sea_mask, diffusivity)
    state, sponge, *fields, rates, plan = pl.pallas_call(
        stage_kernel,
        out_shape=[jax.ShapeDtypeStruct(field.shape, field.dtype) for field in fields]
        + [jax.ShapeDtypeStruct((NCLS, 1, cells_c), f32), jax.ShapeDtypeStruct((6 * SLOTS + 1,), jnp.int32)],
        in_specs=[VM] + [pl.BlockSpec(memory_space=pltpu.HBM)] * 10,
        out_specs=[VM] * 7 + [SM],
        scratch_shapes=[pltpu.SMEM(settling.shape, f32)]
        + [pltpu.SMEM(table.shape, table.dtype) for table in tables]
        + [pltpu.SemaphoreType.DMA((10,))],
        compiler_params=PARAMS,
        name="stage_fields",
    )(mask, *fields, settling, *tables)
    state = state.reshape(tile.shape)
    fold_scratch = [pltpu.VMEM((comps, half_r, cells_c), f32), pltpu.VMEM((cells_c // LANES, cells_r, LANES), f32)]
    for step in range(STEPS):
        last = step == STEPS - 1
        new = jax.ShapeDtypeStruct(adjoint.shape, f32) if last else tile
        got = exchange(early, mask, late)
        wets, flux, *sides = pl.pallas_call(
            functools.partial(update_kernel, n_cols),
            out_shape=[tile] * 2 + side,
            in_specs=[SM] + [VM] * (7 + 2 * SLOTS),
            out_specs=[VM] * (2 + len(side)),
            scratch_shapes=[
                pltpu.VMEM(tile.shape, f32),
                pltpu.VMEM((comps, half_r, cells_c), f32),
                pltpu.VMEM(block.shape, f32),
                pltpu.VMEM((cells_c // LANES, cells_r, LANES), f32),
            ],
            compiler_params=PARAMS,
            name="update",
        )(plan, rates, state, sponge, *fields, *got)
        sides = [lax.ppermute(sides[k], "gx", swap_pairs(n_x, 1 - k)) for k in range(2)] + [
            lax.ppermute(sides[2 + k], "gy", swap_pairs(n_y, k)) for k in range(n_cols)
        ]
        bulk, *folded = pl.pallas_call(
            functools.partial(spread_kernel, last),
            out_shape=[new] + ([] if last else [block]),
            in_specs=[VM] * (2 if last else 3),
            out_specs=[VM] * (1 if last else 2),
            scratch_shapes=[] if last else fold_scratch,
            compiler_params=PARAMS,
            name="spread_last" if last else "spread",
        )(wets, flux, *([] if last else [sponge]))
        extra = jax.ShapeDtypeStruct((2 * comps + 2 * half_r, half_c), f32)
        extra = jax.ShapeDtypeStruct((2 * comps + 2 * half_r, half_c), f32)
        state, *out = pl.pallas_call(
            functools.partial(halo_kernel, n_cols, (n_x, n_y), last),
            out_shape=[new] + ([] if last else [block] * 2 + [flag, extra]),
            in_specs=[SM] * (0 if last else 1) + [VM] * (1 + len(side) + (0 if last else 2)),
            out_specs=[VM] * (1 if last else 5),
            scratch_shapes=[] if last else fold_scratch[1:],
            compiler_params=PARAMS,
            name="halo_last" if last else "halo",
        )(*([] if last else [plan]), bulk, *([] if last else [sponge, *folded]), *sides)
        if not last:
            early, mask, packed = out[:2], out[2], out[3]
            late = pl.pallas_call(
                late_kernel,
                out_shape=[block] * 4,
                in_specs=[SM] + [VM] * 3,
                out_specs=[VM] * 4,
                compiler_params=PARAMS,
                name="late_payload",
            )(plan, state, *folded, packed)
    return state


def solution(mesh):
    in_specs = (
        P("grid", None, "gx", "gy"),
        P("grid", "gx", "gy"),
        P("grid", "gx", "gy"),
        P("grid", "gx", "gy"),
        P("grid", "gx", "gy"),
        P("grid", "gx", "gy"),
        P(),
        P(),
        P(),
        P(),
    )
    out_specs = P("grid", None, "gx", "gy")
    return jax.shard_map(local, mesh=mesh, in_specs=in_specs, out_specs=out_specs, check_vma=False)
```
